32 devices in a mesh: dp: 2 (over x), seq: 16 (over z, y, core).
Axes of the slice: x: 2, y: 2, z: 4, core: 2. Of those that a mesh axis runs over, the one named last changes fastest.
Arguments:
- mixed: bfloat16 [2, 2048, 4096], P('dp', 'seq'), may hold values from -6 to 6
- conv_weight: bfloat16 [4, 4096], replicated, may hold values from -3 to 3
- log_decay: float32 [2, 16, 2048], P('dp', None, 'seq'), may hold values from -0.75 to 0, as said below
- beta: float32 [2, 16, 2048], P('dp', None, 'seq'), may hold values from 0.01 to 0.5
- doc_ids: int32 [2, 2048], P('dp', 'seq'), may hold values from 0 to 7, never falling along the last dimension, each value on 1 to 1024 neighbouring positions
- out_grad: bfloat16 [2, 2048, 2048], P('dp', 'seq'), may hold values from -6 to 6
Outputs:
- output: bfloat16 [2, 2048, 2048], P('dp', 'seq')
- d_mixed: bfloat16 [2, 2048, 4096], P('dp', 'seq')
- d_conv_weight: float32 [4, 4096], replicated
- d_log_decay: float32 [2, 16, 2048], P('dp', None, 'seq')
- d_beta: float32 [2, 16, 2048], P('dp', None, 'seq')
The draws below stay inside these ranges and needn't reach their ends.
Inputs may be any that keep to these rules, and one draw needn't show every extreme that they name: `doc_ids`: document numbers never fall along a slab; each of the 8 documents holds 1 to 1024 tokens, and one holds exactly 1024. `log_decay`: every entry is negative.
All inputs are finite; a program needn't handle non-finite values.
Results may differ from the reference program's by a relative error of at most 0.00115.
Values may be sent and summed in bfloat16 or wider, within the bound.
No kernel may reach another device: no remote copies, remote signals or barrier semaphores. Data moves between devices by JAX's collectives and lax.ppermute only.
A program may use at most 128 MiB of HBM per device.

```python
import math
import jax
import jax.numpy as jnp
import numpy as np
from jax import lax

DK = 128
KH = 8
VH = 16
CH = 64
DOCS = 8
C = 4096
SLABS = 2
PIECE_LENGTH = 2048
DOC_MOST = 1024


def draw_log_decay(key, part):
    document_streams = jax.random.split(key, 4)
    lowest = math.log(0.25 / PIECE_LENGTH)
    upper = math.log(1.0 / 30.0)
    tensor_extent = (SLABS, VH, PIECE_LENGTH)
    gating_numbers = jnp.exp(jax.random.uniform(document_streams[0], (SLABS, VH, 1), jnp.float32, lowest, upper))
    approximate_guess = jax.random.uniform(document_streams[1], tensor_extent, jnp.float32, 0.5, 1.5)
    packet_clusters = (jax.random.uniform(document_streams[2], tensor_extent, jnp.float32) < 3.0 / PIECE_LENGTH).astype(jnp.float32)
    nesting_level = jax.random.uniform(document_streams[3], tensor_extent, jnp.float32, 0.22, 0.69)
    return -(gating_numbers * approximate_guess) - packet_clusters * nesting_level


def level_of(own_key, dims, cuts, smallest, top_value):
    factor_of, own = 1.0, jax.random.fold_in(own_key, 6)
    for dim, parts in cuts:
        steps = jnp.exp(jax.random.uniform(jax.random.fold_in(own, dim), (parts,), jnp.float32, smallest / len(cuts), top_value / len(cuts)))
        factor_of = factor_of * jnp.repeat(steps, dims[dim] // parts).reshape([-1 if axis == dim else 1 for axis in range(len(dims))])
    return factor_of


def profile(count, total, most, slope):
    loads = [(1 << 20) // math.isqrt(rank ** slope) + 1 for rank in range(2, count + 1)]
    surplus, holding = total - most - (count - 1), [1] * (count - 1)
    while surplus > 0:
        movable = [i for i in range(count - 1) if holding[i] < most]
        pool, remaining = sum([loads[i] for i in movable]), surplus
        for i in movable:
            more = min(most - holding[i], max(1, remaining * loads[i] // pool), surplus)
            holding[i] = holding[i] + more
            surplus = surplus - more
    return np.array([most] + holding)


def ragged(key, count, total, most, lean):
    if count == 2:
        one = jax.random.randint(key, (), max(1, total - most), min(most, total - 1) + 1)
        return jnp.stack([one, total - one])
    tallies = jnp.asarray(profile(count, total, most, lean), jnp.int32)
    twos = (count - 1) // 2
    giver, sink = tallies[1:1 + 2 * twos:2], tallies[2:2 + 2 * twos:2]
    slack = jnp.minimum(giver - 1, most - sink)
    shifted = jax.random.randint(jax.random.fold_in(key, 1), (twos,), 0, 1 << 20) % (slack + 1)
    tallies = tallies.at[1:1 + 2 * twos:2].set(giver - shifted).at[2:2 + 2 * twos:2].set(sink + shifted)
    return tallies[jax.random.permutation(jax.random.fold_in(key, 2), count)]


def gaussian(stream_key, shape, width, most, cuts=(), held_as=jnp.bfloat16):
    gain = level_of(stream_key, shape, cuts, -0.22, 0.18) if cuts else 1.0
    result = jax.random.normal(stream_key, shape, jnp.float32) * width * gain
    return jnp.minimum(jnp.maximum(result, -most), most).astype(held_as)


def setup_inputs(seed: int = 0) -> dict:
    streams_of = jax.random.split(jax.random.key(seed), 7)
    mixed = gaussian(streams_of[0], (SLABS, PIECE_LENGTH, C), 1.0, 6.0, ((0, 2), (1, 16)))
    conv_weight = gaussian(streams_of[1], (4, C), 4 ** -0.5, 3.0)
    log_decay = draw_log_decay(jax.random.fold_in(streams_of[6], 71), 0)
    beta = jnp.clip(jnp.exp(math.log(0.5) - 3.912023 * jax.random.uniform(streams_of[3], (SLABS, VH, PIECE_LENGTH), jnp.float32) ** level_of(streams_of[3], (SLABS, VH, PIECE_LENGTH), ((0, 2), (2, 16)), -0.2, 0.2)), 0.01, 0.5)
    doc_ids = jax.vmap(lambda own: jnp.searchsorted(jnp.cumsum(ragged(own, DOCS, PIECE_LENGTH, DOC_MOST, 2)), jnp.arange(PIECE_LENGTH), side="right"))(jax.random.split(streams_of[4], SLABS)).reshape((SLABS, PIECE_LENGTH)).astype(jnp.int32)
    out_grad = gaussian(streams_of[5], (SLABS, PIECE_LENGTH, VH * DK), 1.0, 6.0, ((0, 2), (1, 16)))
    return dict(mixed=mixed, conv_weight=conv_weight, log_decay=log_decay, beta=beta, doc_ids=doc_ids, out_grad=out_grad)


highest_precision = lax.Precision.HIGHEST
epsilon = 1e-06

def unit_norm(values):
    return values * lax.rsqrt(lax.optimization_barrier(jnp.sum(values * values, -1, keepdims=True)) + epsilon)

def conv_active(rows, weight, documents):
    summed = weight[3] * rows
    for offset in (1, 2, 3):
        moved = jnp.concatenate([jnp.zeros((offset, rows.shape[1]), jnp.float32), rows[:-offset]], 0)
        moved_docs = jnp.concatenate([jnp.full((offset,), -1, jnp.int32), documents[:-offset]], 0)
        summed = summed + weight[3 - offset] * jnp.where((moved_docs == documents)[:, None], moved, 0.0)
    return jax.nn.silu(summed)

def token_step(memory_state, item):
    query_matrix, key_rows, values, fading, rate, starting = item
    memory_state = jnp.where(starting, 0.0, memory_state)
    project_input = jnp.einsum('es,esz->ez', key_rows, memory_state, precision=highest_precision)
    memory_state = fading[:, None, None] * (memory_state - rate[:, None, None] * key_rows[:, :, None] * project_input[:, None, :])
    memory_state = memory_state + rate[:, None, None] * key_rows[:, :, None] * values[:, None, :]
    emitted_output = jnp.einsum('es,esz->ez', query_matrix, memory_state, precision=highest_precision)
    return (memory_state, emitted_output)

@jax.checkpoint
def block_step(memory_state, item):
    return lax.scan(token_step, memory_state, item)

def forward(rows, weight, decay, rate, documents):
    length = rows.shape[0]
    active = conv_active(rows, weight, documents)
    query_matrix = active[:, :KH * DK].reshape(length, KH, DK)
    key_rows = active[:, KH * DK:2 * KH * DK].reshape(length, KH, DK)
    values = active[:, 2 * KH * DK:].reshape(length, VH, DK)
    query_matrix = jnp.repeat(unit_norm(query_matrix) * DK ** (-0.5), VH // KH, axis=1)
    key_rows = jnp.repeat(unit_norm(key_rows), VH // KH, axis=1)
    fading = jnp.exp(decay.T)
    starting = documents != jnp.concatenate([jnp.full((1,), -1, jnp.int32), documents[:-1]], 0)
    blocks = length // CH
    items = (query_matrix.reshape(blocks, CH, VH, DK), key_rows.reshape(blocks, CH, VH, DK), values.reshape(blocks, CH, VH, DK), fading.reshape(blocks, CH, VH), rate.T.reshape(blocks, CH, VH), starting.reshape(blocks, CH))
    initial = jnp.zeros((VH, DK, DK), jnp.float32)
    final_state, emitted_output = lax.scan(block_step, initial, items)
    return emitted_output.reshape(length, VH * DK)

def reference(mixed, conv_weight, log_decay, beta, doc_ids, out_grad):
    weight = conv_weight.astype(jnp.float32)

    def one_slab(item):
        rows, decay, rate, documents, cotangent = item

        def local_forward(rows_in, weight_in, decay_in, rate_in):
            return forward(rows_in, weight_in, decay_in, rate_in, documents)
        read, pullback = jax.vjp(local_forward, rows.astype(jnp.float32), weight, decay, rate)
        grad_rows, grad_weight, grad_decay, grad_rate = pullback(cotangent.astype(jnp.float32))
        return (read.astype(jnp.bfloat16), grad_rows.astype(jnp.bfloat16), grad_weight, grad_decay, grad_rate)
    results = lax.map(one_slab, (mixed, log_decay, beta, doc_ids, out_grad))
    return (results[0], results[1], lax.optimization_barrier(jnp.sum(results[2], 0)), results[3], results[4])
```

```python
import functools

import jax
import jax.numpy as jnp
from jax import lax
from jax.experimental import pallas as pl
from jax.experimental.pallas import tpu as pltpu
from jax.sharding import PartitionSpec as P

DK = 128
DOC_MOST = 1024
EPS = 1e-6
RIM = 16
f32 = jnp.float32
bf16 = jnp.bfloat16


def dg(a, b, ca, cb):
    return lax.dot_general(a, b, (((ca,), (cb,)), ((), ())), preferred_element_type=f32)


def split(x):
    hi = x.astype(bf16)
    return (hi, (x - hi.astype(f32)).astype(bf16))


def cat(parts, axis):
    return tuple(jnp.concatenate(leaves, axis) for leaves in zip(*parts))


def mm(a, b, ca, cb):
    out = dg(a[0], b[0], ca, cb)
    if len(b) > 1:
        out = out + dg(a[0], b[1], ca, cb)
    if len(a) > 1:
        out = out + dg(a[1], b[0], ca, cb)
    return out


def iota2(shape, dim):
    return lax.broadcasted_iota(jnp.int32, shape, dim)


def conv_inputs(x_ref, n, shift_ref, docs):
    length = docs.shape[0]
    shift_ref[5:8, :] = x_ref[n, length : length + 3, :].astype(f32)
    rows = x_ref[n, :length, :].astype(f32)
    shift_ref[8 : 8 + length, :] = rows
    at = iota2((length, DK), 0)
    first = docs[0:1, :]
    taps = [rows]
    for off in (1, 2, 3):
        earlier = jnp.where(at >= off, pltpu.roll(docs, off, 0), first)
        ok = earlier == docs
        moved = shift_ref[8 - off : 8 - off + length, :]
        width = moved.shape[1] // DK
        taps.append(jnp.where(jnp.concatenate([ok] * width, 1), moved, 0.0))
    return taps


def conv_out(taps, w):
    return sum(w[3 - off : 4 - off, :] * taps[off] for off in range(4))


def heads_of(z):
    sig = 1.0 / (1.0 + jnp.exp(-z))
    act = z * sig
    q, k, v = act[:, :DK], act[:, DK : 2 * DK], act[:, 2 * DK :]
    rq = lax.rsqrt(jnp.sum(q * q, -1, keepdims=True) + EPS)
    rk = lax.rsqrt(jnp.sum(k * k, -1, keepdims=True) + EPS)
    return sig, q * rq, k * rk, v, rq, rk


class Meta:
    def __init__(self, numbers, per_key):
        length = numbers.shape[1]
        rows = numbers.astype(f32)
        row_at = iota2((RIM, DK), 0)
        i, j = iota2((length, length), 0), iota2((length, length), 1)
        self.lower, self.strict = i >= j, i > j

        def column(first, count):
            pick = ((row_at >= first) & (row_at < first + count)).astype(f32).astype(bf16)
            return dg(numbers, pick, 0, 0)

        self.docs = column(3, 1)
        doc_row = rows[3:4]
        self.same = (self.docs == doc_row) & self.lower
        carry = (self.docs > 0) & (self.docs == doc_row[:, 0:1])
        ending = self.docs == doc_row[:, length - 1 : length]
        until = (i <= j).astype(f32).astype(bf16)
        row_sums = dg(numbers, until, 1, 0)
        ones = jnp.ones((length, DK), bf16)
        self.c_row, self.c_col, self.beta, self.beta_row = [], [], [], []
        self.entry, self.tail, self.keep = [], [], []
        for h in range(per_key):
            at = 4 + 3 * h
            self.c_row.append(row_sums[at : at + 1] + row_sums[at + 1 : at + 2] + row_sums[at + 2 : at + 3])
            c_col = 0.0
            for part in (2, 1, 0):
                c_col = c_col + dg(jnp.where(self.lower, rows[at + part : at + part + 1], 0.0).astype(bf16), ones, 1, 0)
            self.c_col.append(c_col)
            at = 4 + 3 * per_key + 3 * h
            self.beta.append(column(at, 3))
            self.beta_row.append(rows[at : at + 1] + rows[at + 1 : at + 2] + rows[at + 2 : at + 3])
            self.entry.append(jnp.where(carry, jnp.exp(c_col), 0.0))
            last = self.c_row[h][:, length - 1 : length]
            self.tail.append(jnp.where(ending, jnp.exp(jnp.minimum(last - c_col, 0.0)), 0.0))
            self.keep.append(self.entry[h][length - 1 : length, :])

    def fading(self, h):
        gap = jnp.minimum(self.c_col[h] - self.c_row[h], 0.0)
        return jnp.where(self.same, jnp.exp(gap), 0.0)


def inverse(mats):
    length = mats[0].shape[0]
    i, j = iota2((length, length), 0), iota2((length, length), 1)
    eye = (i == j).astype(f32)
    inner = [jnp.where((i // 8) == (j // 8), n, 0.0) for n in mats]
    s1 = [split(n) for n in inner]
    s2 = [split(mm(a, a, 1, 0)) for a in s1]
    low = [eye - n + (a[0].astype(f32) + a[1].astype(f32)) - mm(b, a, 1, 0) for n, a, b in zip(inner, s2, s1)]
    s4 = [split(mm(a, a, 1, 0)) for a in s2]
    inv = [t + mm(split(t), a, 1, 0) for t, a in zip(low, s4)]
    width = 8
    while width < length:
        cross = ((i // (2 * width)) == (j // (2 * width))) & ((i // width) > (j // width))
        st = [split(t) for t in inv]
        half = [mm(split(jnp.where(cross, n, 0.0)), t, 1, 0) for n, t in zip(mats, st)]
        inv = [t - mm(s, split(x), 1, 0) for t, s, x in zip(inv, st, half)]
        width *= 2
    return inv


def rows_from(x):
    ones = jnp.ones((8, x.shape[1]), bf16)
    return mm((ones,), split(x), 1, 1)[0:1]


def first_kernel(per_key, count, x_ref, og_ref, w_ref, q_ref, k_ref, f_ref, n_ref, p_ref, t_ref, w_out, u_ref,
                 y_ref, pu_ref, r_ref, a_ref, b_ref, g_ref, fwd_ref, bwd_ref, shift_ref, a_all, g_all):
    step = pl.program_id(0)
    steps = pl.num_programs(0)
    length = og_ref.shape[1]
    eye = (iota2((DK, DK), 0) == iota2((DK, DK), 1)).astype(f32)

    @pl.when(step == 0)
    def _():
        fwd_ref[...] = jnp.zeros_like(fwd_ref)

    w = w_ref[...]
    pairs = [(n, h) for n in range(count) for h in range(per_key)]
    metas, qs, ks, vs = [], [], [], []
    for n in range(count):
        meta = Meta(x_ref[n, length:, DK : 2 * DK], per_key)
        taps = conv_inputs(x_ref, n, shift_ref.at[n], meta.docs)
        _, q, k, v, _, _ = heads_of(conv_out(taps, w))
        q = q * DK**-0.5
        q_ref[n], k_ref[n] = q, k
        metas.append(meta)
        qs.append(q)
        ks.append(k)
        vs.append(v)
    sk = [split(k) for k in ks]
    both = [mm(cat([s, split(q)], 0), s, 1, 1) for s, q in zip(sk, qs)]
    fs = [metas[n].fading(h) for n, h in pairs]
    ns = [jnp.where(metas[n].strict, metas[n].beta[h] * both[n][:length] * f, 0.0) for (n, h), f in zip(pairs, fs)]
    ps = [both[n][length:] * f for (n, h), f in zip(pairs, fs)]
    for (n, h), f, nn, p in zip(pairs, fs, ns, ps):
        f_ref[n, h], n_ref[n, h], p_ref[n, h] = f, nn, p
    ts = inverse(ns)
    rhs = [
        jnp.concatenate([metas[n].beta[h] * metas[n].entry[h] * ks[n], metas[n].beta[h] * vs[n][:, h * DK : (h + 1) * DK]], 1)
        for n, h in pairs
    ]
    wu = [mm(split(t), split(r), 1, 0) for t, r in zip(ts, rhs)]
    swu = [split(x) for x in wu]
    sp = [split(p) for p in ps]
    kwu = [mm(split(metas[n].tail[h] * ks[n]), s, 0, 0) for (n, h), s in zip(pairs, swu)]
    pwu = [mm(p, s, 1, 0) for p, s in zip(sp, swu)]
    ys = [metas[n].entry[h] * qs[n] - x[:, :DK] for (n, h), x in zip(pairs, pwu)]
    dos = [(og_ref[n, :, h * DK : (h + 1) * DK],) for n, h in pairs]
    gs = [mm(split(y), d, 0, 0) for y, d in zip(ys, dos)]
    rs = [mm(p, d, 0, 0) for p, d in zip(sp, dos)]
    for m, (n, h) in enumerate(pairs):
        a = metas[n].keep[h] * eye - kwu[m][:, :DK]
        t_ref[n, h], w_out[n, h], u_ref[n, h] = ts[m], wu[m][:, :DK], wu[m][:, DK:]
        y_ref[n, h], pu_ref[n, h], r_ref[n, h] = ys[m], pwu[m][:, DK:], rs[m]
        a_ref[n, h], b_ref[n, h], g_ref[n, h] = a, kwu[m][:, DK:], gs[m]
        a_all[step * count + n, h], g_all[step * count + n, h] = a, gs[m]
        fwd_ref[h] = mm(split(a), split(fwd_ref[h]), 1, 0) + kwu[m][:, DK:]

    @pl.when(step == steps - 1)
    def _():
        blocks = a_all.shape[0]

        def back(s, states):
            n = blocks - 1 - s
            return tuple(
                mm(split(a_all[n, h]), split(states[h]), 0, 0) + g_all[n, h] for h in range(per_key)
            )

        states = lax.fori_loop(0, blocks, back, tuple(jnp.zeros((DK, DK), f32) for h in range(per_key)))
        for h in range(per_key):
            bwd_ref[h] = states[h]


def second_kernel(per_key, count, in_ref, w_ref, u_ref, y_ref, pu_ref, a_ref, b_ref, o_ref, d_ref, s_ref, state):
    @pl.when(pl.program_id(0) == 0)
    def _():
        state[...] = in_ref[...]

    length = w_ref.shape[2]
    for n in range(count):
        for h in range(per_key):
            now = state[h]
            s_ref[n, h] = now
            sn = split(now)
            both = mm(cat([split(w_ref[n, h]), split(y_ref[n, h]), split(a_ref[n, h])], 0), sn, 1, 0)
            d_ref[n, h] = u_ref[n, h] - both[:length]
            o_ref[n, :, h * DK : (h + 1) * DK] = (both[length : 2 * length] + pu_ref[n, h]).astype(bf16)
            state[h] = both[2 * length :] + b_ref[n, h]


def third_kernel(per_key, count, in_ref, x_ref, og_ref, w_ref, q_ref, k_ref, f_ref, n_ref, p_ref, t_ref, r_ref, a_ref,
                 g_ref, d_ref, s_ref, dx_ref, gates_ref, rim_ref, dw_ref, state, shift_ref, dz_ref, doc_next):
    step = pl.program_id(0)

    @pl.when(step == 0)
    def _():
        state[...] = in_ref[...]
        dw_ref[...] = jnp.zeros_like(dw_ref)
        dz_ref[...] = jnp.zeros_like(dz_ref)
        doc_next[...] = jnp.zeros_like(doc_next)

    w = w_ref[...]
    length = og_ref.shape[1]
    i, j = iota2((length, length), 0), iota2((length, length), 1)
    from_here = (i >= j).astype(f32).astype(bf16)
    for n in reversed(range(count)):
        meta = Meta(x_ref[n, length:, DK : 2 * DK], per_key)
        taps = conv_inputs(x_ref, n, shift_ref, meta.docs)
        z = conv_out(taps, w)
        sig, q_hat, k_hat, v, rq, rk = heads_of(z)
        q, k = q_ref[n], k_ref[n]
        sq, sk = split(q), split(k)
        dq, dk = jnp.zeros_like(q), jnp.zeros_like(k)
        dvs = []
        for h in range(per_key):
            beta, entry, tail = meta.beta[h], meta.entry[h], meta.tail[h]
            later = state[h]
            s_later, s_state, s_d = split(later), split(s_ref[n, h]), split(d_ref[n, h])
            do = (og_ref[n, :, h * DK : (h + 1) * DK],)
            v_h = v[:, h * DK : (h + 1) * DK]
            f = f_ref[n, h]
            x1 = mm(split(tail * k), s_later, 1, 0)
            e = mm(split(t_ref[n, h]), split(r_ref[n, h] + x1), 0, 0)
            se = split(e)
            dp = mm(do, s_d, 1, 1)
            dn = -mm(se, s_d, 1, 1)
            dos = mm(do, s_state, 1, 1)
            es = mm(se, s_state, 1, 1)
            dds = mm(s_d, s_later, 1, 1)
            dpf = dp * f
            dkk = jnp.where(meta.strict, dn * beta * f, 0.0)
            s_dpf, s_dkk = split(dpf), split(dkk)
            dqk = mm(cat([s_dpf, s_dkk], 0), sk, 1, 0)
            ends = tail * dds
            enter = entry * dos
            bes = beta * entry * es
            dq = dq + enter + dqk[:length]
            dk = dk + dqk[length:] + mm(cat([s_dpf, s_dkk], 0), cat([sq, sk], 0), 0, 0) - bes + ends
            dvs.append(beta * e)
            nn = dn * n_ref[n, h]
            gaps = dp * p_ref[n, h] + nn
            ek = ends * k
            dc = rows_from(gaps + enter * q - bes * k - ek) - jnp.sum(gaps, 0, keepdims=True)
            at_end = jnp.sum(jnp.sum(ek, 0, keepdims=True), 1, keepdims=True) + jnp.sum(
                jnp.sum(later * s_ref[n, h] * meta.keep[h], 0, keepdims=True), 1, keepdims=True
            )
            dc = jnp.broadcast_to(dc, (8, length))
            d_decay = mm(split(dc), (from_here,), 1, 0)[0:1] + at_end
            d_beta = rows_from(e * v_h - entry * es * k) + rows_from(nn) / meta.beta_row[h]
            gates_ref[n, h : h + 1, :] = d_decay
            gates_ref[n, per_key + h : per_key + h + 1, :] = d_beta
            state[h] = mm(split(a_ref[n, h]), s_later, 0, 0) + g_ref[n, h]
        dq_act = (DK**-0.5) * rq * (dq - q_hat * jnp.sum(dq * q_hat, -1, keepdims=True))
        dk_act = rk * (dk - k_hat * jnp.sum(dk * k_hat, -1, keepdims=True))
        d_act = jnp.concatenate([dq_act, dk_act] + dvs, 1)
        dz = d_act * (sig + z * sig * (1.0 - sig))
        dz_ref[8 + length :, :] = dz_ref[8 : 16, :]
        dz_ref[8 : 8 + length, :] = dz
        docs_after = doc_next[...]
        at = iota2((length, DK), 0)
        dx = w[3:4, :] * dz
        width = dz.shape[1] // DK
        for off in (1, 2, 3):
            ahead = pltpu.roll(meta.docs, length - off, 0)
            for r in range(off):
                ahead = jnp.where(at == length - off + r, docs_after[r : r + 1, :], ahead)
            ok = jnp.abs(ahead) == jnp.abs(meta.docs)
            dx = dx + w[3 - off : 4 - off, :] * jnp.where(
                jnp.concatenate([ok] * width, 1), dz_ref[8 + off : 8 + off + length, :], 0.0
            )
        doc_next[...] = meta.docs[0:8, :]
        dx_ref[n] = dx.astype(bf16)
        for off in range(4):
            dw_ref[3 - off : 4 - off, :] += jnp.sum(dz * taps[off], 0, keepdims=True)
        head = jnp.where(
            jnp.concatenate([meta.docs[0:8, :] == meta.docs[0:1, :]] * width, 1), dz[0:8, :], 0.0
        )
        rims = []
        for r in range(3):
            total = 0.0
            for off in range(3 - r, 4):
                total = total + w[3 - off : 4 - off, :] * head[r + off - 3 : r + off - 2, :]
            rims.append(total)
        rim_ref[...] = jnp.concatenate(rims + [jnp.zeros((5, dz.shape[1]), f32)], 0)


def three(x):
    hi = lax.reduce_precision(x, 8, 7)
    mid = lax.reduce_precision(x - hi, 8, 7)
    return jnp.stack([hi, mid, x - hi - mid], -2).astype(bf16)


def local(mixed, conv_weight, log_decay, beta, doc_ids, out_grad):
    n_seq, n_dp = lax.axis_size("seq"), lax.axis_size("dp")
    rows, docs, og = mixed[0], doc_ids[0], out_grad[0]
    length, channels = rows.shape
    heads = log_decay.shape[1]
    key_heads = (channels - heads * DK) // (2 * DK)
    per_key = heads // key_heads
    G = key_heads
    assert n_seq % G == 0 and G * length >= DOC_MOST
    member = lax.axis_index("seq") % G
    team = [list(range(s, s + G)) for s in range(0, n_seq, G)]
    own = 2 * DK + per_key * DK

    def shifted(x, by):
        return lax.ppermute(x, "seq", [(s, s + by) for s in range(n_seq) if 0 <= s + by < n_seq])

    def by_member(x):
        lead = x.shape[:-1]
        parts = (x[..., : G * DK], x[..., G * DK : 2 * G * DK], x[..., 2 * G * DK :])
        return jnp.concatenate([jnp.moveaxis(y.reshape(lead + (G, -1)), -2, 0) for y in parts], -1)

    def to_channels(x):
        parts = (x[..., :DK], x[..., DK : 2 * DK], x[..., 2 * DK :])
        return jnp.concatenate(
            [jnp.moveaxis(y, 0, -2).reshape(x.shape[1:-1] + (-1,)) for y in parts], -1
        )

    def swap(x):
        return lax.all_to_all(x, "seq", 0, 0, axis_index_groups=team)

    rim_rows, rim_docs = shifted((rows[-3:], docs[-3:]), 1)
    doc_after = shifted(docs[:1], -1)
    rim_rows = jnp.where((rim_docs == docs[0])[:, None], rim_rows, 0)
    signed = jnp.where(rim_docs[-1] == docs[0], docs + 1, -docs - 1).astype(bf16)
    numbers = jnp.concatenate(
        [
            jnp.broadcast_to(signed, (G, 1, length)),
            three(log_decay[0].reshape(G, per_key, length)).reshape(G, -1, length),
            three(beta[0].reshape(G, per_key, length)).reshape(G, -1, length),
        ],
        1,
    )
    numbers = jnp.pad(numbers, ((0, 0), (0, 0), (DK, per_key * DK)))
    packed = jnp.concatenate([by_member(rows), by_member(rim_rows), numbers], 1)
    x = swap(packed)
    og_in = swap(jnp.moveaxis(og.reshape(length, G, per_key * DK), 1, 0))
    weight = lax.dynamic_index_in_dim(by_member(conv_weight.astype(f32)), member, 0, keepdims=False)

    count = 2
    steps = G // count
    pair = (per_key, DK, DK)

    def spec(shape, back=False):
        if back:
            return pl.BlockSpec((count,) + shape, lambda s: (steps - 1 - s,) + (0,) * len(shape))
        return pl.BlockSpec((count,) + shape, lambda s: (s,) + (0,) * len(shape))

    def full(shape):
        return pl.BlockSpec(shape, lambda s: (0,) * len(shape))

    def out(shape):
        return jax.ShapeDtypeStruct((G,) + shape, f32)

    params = pltpu.CompilerParams(vmem_limit_bytes=48 << 20)
    first = pl.pallas_call(
        functools.partial(first_kernel, per_key, count),
        grid=(steps,),
        in_specs=[spec((length + RIM, own)), spec((length, per_key * DK)), full((4, own))],
        out_specs=[spec((length, DK))] * 2 + [spec(pair)] * 12 + [full(pair)] * 2,
        out_shape=[out((length, DK))] * 2 + [out(pair)] * 12 + [jax.ShapeDtypeStruct(pair, f32)] * 2,
        scratch_shapes=[
            pltpu.VMEM((count, 8 + length, own), f32),
            pltpu.VMEM((G,) + pair, f32),
            pltpu.VMEM((G,) + pair, f32),
        ],
        compiler_params=params,
        name="blocks",
    )
    q, k, f, n, p, t, w_out, u, y, pu, r, a, b, g, fwd, bwd = first(x, og_in, weight)
    state_in = shifted(fwd, G)
    back_in = shifted(bwd, -G)
    o, d, s = pl.pallas_call(
        functools.partial(second_kernel, per_key, count),
        grid=(steps,),
        in_specs=[full(pair)] + [spec(pair)] * 6,
        out_specs=[spec((length, per_key * DK)), spec(pair), spec(pair)],
        out_shape=[jax.ShapeDtypeStruct((G, length, per_key * DK), bf16), out(pair), out(pair)],
        scratch_shapes=[pltpu.VMEM(pair, f32)],
        compiler_params=params,
        name="read",
    )(state_in, w_out, u, y, pu, a, b)
    dx, gates, rim, dw = pl.pallas_call(
        functools.partial(third_kernel, per_key, count),
        grid=(steps,),
        in_specs=[full(pair), spec((length + RIM, own), True), spec((length, per_key * DK), True), full((4, own))]
        + [spec((length, DK), True)] * 2
        + [spec(pair, True)] * 9,
        out_specs=[spec((length, own), True), spec((2 * per_key, length), True), full((8, own)), full((4, own))],
        out_shape=[
            jax.ShapeDtypeStruct((G, length, own), bf16),
            out((2 * per_key, length)),
            jax.ShapeDtypeStruct((8, own), f32),
            jax.ShapeDtypeStruct((4, own), f32),
        ],
        scratch_shapes=[
            pltpu.VMEM(pair, f32),
            pltpu.VMEM((8 + length, own), f32),
            pltpu.VMEM((16 + length, own), f32),
            pltpu.VMEM((8, DK), f32),
        ],
        compiler_params=params,
        name="gradients",
    )(back_in, x, og_in, weight, q, k, f, n, p, t, r, a, g, d, s)

    output = jnp.moveaxis(swap(o), 0, 1).reshape(length, -1)
    d_rows = to_channels(swap(dx))
    gates = swap(gates)
    rim = rim[:3].astype(bf16)
    pieces = [
        lax.ppermute(rim, "seq", [(s + m, s - 1) for s in range(G, n_seq, G)]) for m in range(G)
    ]
    incoming = to_channels(jnp.stack(pieces))
    incoming = jnp.where((docs[-3:] == doc_after)[:, None], incoming, 0).astype(f32)
    d_tail = (d_rows[-3:].astype(f32) + incoming).astype(bf16)
    d_rows = jnp.concatenate([d_rows[:-3], d_tail], 0)
    step = 1
    while step < n_dp:
        dw = dw + lax.ppermute(dw, "dp", [(s, s ^ step) for s in range(n_dp)])
        step *= 2
    step = G
    while step < n_seq:
        dw = dw + lax.ppermute(dw, "seq", [(s, s ^ step) for s in range(n_seq)])
        step *= 2
    gathered = jnp.zeros((G,) + dw.shape, f32)
    for m in range(G):
        piece = lax.ppermute(dw, "seq", [(s, s ^ m) for s in range(n_seq)]) if m else dw
        gathered = lax.dynamic_update_index_in_dim(gathered, piece, member ^ m, 0)
    d_weight = to_channels(gathered)
    d_decay = gates[:, :per_key].reshape(heads, length)
    d_beta = gates[:, per_key:].reshape(heads, length)
    return (output[None], d_rows[None], d_weight, d_decay[None], d_beta[None])


def solution(mesh):
    in_specs = (
        P("dp", "seq", None),
        P(),
        P("dp", None, "seq"),
        P("dp", None, "seq"),
        P("dp", "seq"),
        P("dp", "seq", None),
    )
    out_specs = (
        P("dp", "seq", None),
        P("dp", "seq", None),
        P(),
        P("dp", None, "seq"),
        P("dp", None, "seq"),
    )
    return jax.shard_map(
        local, mesh=mesh, in_specs=in_specs, out_specs=out_specs, check_vma=False
    )
```

```python
import functools

import jax
import jax.numpy as jnp
from jax import lax
from jax.experimental import pallas as pl
from jax.experimental.pallas import tpu as pltpu
from jax.sharding import PartitionSpec as P

DK = 128
DOC_MOST = 1024
EPS = 1e-6
CODE = 16
COUNTS = (2, 2, 2, 2)
VMEM = 56 << 20
RIM = 16
f32 = jnp.float32
bf16 = jnp.bfloat16


def dg(a, b, ca, cb):
    return lax.dot_general(a, b, (((ca,), (cb,)), ((), ())), preferred_element_type=f32)


def split(x):
    hi = x.astype(bf16)
    return (hi, (x - hi.astype(f32)).astype(bf16))


def cat(parts, axis):
    return tuple(jnp.concatenate(leaves, axis) for leaves in zip(*parts))


def mm(a, b, ca, cb):
    out = dg(a[0], b[0], ca, cb)
    if len(b) > 1:
        out = out + dg(a[0], b[1], ca, cb)
    if len(a) > 1:
        out = out + dg(a[1], b[0], ca, cb)
    return out


def iota2(shape, dim):
    return lax.broadcasted_iota(jnp.int32, shape, dim)


def conv_inputs(x_ref, n, width, shift_ref, docs):
    length = docs.shape[0]
    shift_ref[5:8, :width] = x_ref[n, length : length + 3, :width].astype(f32)
    rows = x_ref[n, :length, :width].astype(f32)
    shift_ref[8 : 8 + length, :width] = rows
    at = iota2((length, DK), 0)
    first = docs[0:1, :]
    taps = [rows]
    for off in (1, 2, 3):
        earlier = jnp.where(at >= off, pltpu.roll(docs, off, 0), first)
        ok = earlier == docs
        moved = shift_ref[8 - off : 8 - off + length, :width]
        taps.append(jnp.where(wide(ok, width), moved, 0.0))
    return taps


def wide(x, width):
    return jnp.concatenate([x] * (width // DK), 1)


def conv_out(taps, w):
    return sum(w[3 - off : 4 - off, :] * taps[off] for off in range(4))


def conv_back(dz, taps, w, code, plain, dz_ref, doc_next, dw_ref, rim_ref):
    length, width = dz.shape
    dz_ref[8 + length :, :] = dz_ref[8:16, :]
    dz_ref[8 : 8 + length, :] = dz
    docs_after = doc_next[...]
    at = iota2((length, DK), 0)
    dx = w[3:4, :] * dz
    for off in (1, 2, 3):
        ahead = pltpu.roll(plain, length - off, 0)
        for r in range(off):
            ahead = jnp.where(at == length - off + r, docs_after[r : r + 1, :], ahead)
        moved = dz_ref[8 + off : 8 + off + length, :]
        dx = dx + w[3 - off : 4 - off, :] * jnp.where(wide(ahead == plain, width), moved, 0.0)
    doc_next[...] = plain[0:8, :]
    for off in range(4):
        dw_ref[3 - off : 4 - off, :] += jnp.sum(dz * taps[off], 0, keepdims=True)
    head = jnp.where(wide(code[0:8, :] == code[0:1, :], width), dz[0:8, :], 0.0)
    held = wide(code[0:1, :], width)
    for r in range(3):
        total = 0.0
        for off in range(3 - r, 4):
            total = total + w[3 - off : 4 - off, :] * head[r + off - 3 : r + off - 2, :]
        rim_ref[r : r + 1, :] = jnp.where(held >= CODE * (3 - r), total, 0.0)
    return dx


def unit(x):
    inv = lax.rsqrt(jnp.sum(x * x, -1, keepdims=True) + EPS)
    return x * inv, inv


def unit_back(grad, hat, inv):
    return inv * (grad - hat * jnp.sum(grad * hat, -1, keepdims=True))


def sigmoid(z):
    return 1.0 / (1.0 + jnp.exp(-z))


class Meta:
    def __init__(self, numbers, per_key):
        length = numbers.shape[1]
        rows = numbers.astype(f32)
        row_at = iota2((RIM, DK), 0)
        i, j = iota2((length, length), 0), iota2((length, length), 1)
        self.lower, self.strict = i >= j, i > j

        def column(first, count):
            pick = ((row_at >= first) & (row_at < first + count)).astype(f32).astype(bf16)
            return dg(numbers, pick, 0, 0)

        self.code = column(3, 1)
        self.plain = self.code - CODE * jnp.floor(self.code * (1.0 / CODE))
        code_row = rows[3:4]
        self.same = (self.code == code_row) & self.lower
        carry = (self.code >= CODE) & (self.code == code_row[:, 0:1])
        ending = self.code == code_row[:, length - 1 : length]
        until = (i <= j).astype(f32).astype(bf16)
        row_sums = dg(numbers, until, 1, 0)
        ones = jnp.ones((length, DK), bf16)
        self.c_row, self.c_col, self.beta, self.beta_row = [], [], [], []
        self.entry, self.tail, self.keep = [], [], []
        for h in range(per_key):
            at = 4 + 3 * h
            self.c_row.append(row_sums[at : at + 1] + row_sums[at + 1 : at + 2] + row_sums[at + 2 : at + 3])
            c_col = 0.0
            for part in (2, 1, 0):
                c_col = c_col + dg(jnp.where(self.lower, rows[at + part : at + part + 1], 0.0).astype(bf16), ones, 1, 0)
            self.c_col.append(c_col)
            at = 4 + 3 * per_key + 3 * h
            self.beta.append(column(at, 3))
            self.beta_row.append(rows[at : at + 1] + rows[at + 1 : at + 2] + rows[at + 2 : at + 3])
            self.entry.append(jnp.where(carry, jnp.exp(c_col), 0.0))
            last = self.c_row[h][:, length - 1 : length]
            self.tail.append(jnp.where(ending, jnp.exp(jnp.minimum(last - c_col, 0.0)), 0.0))
            self.keep.append(self.entry[h][length - 1 : length, :])

    def fading(self, h):
        gap = jnp.minimum(self.c_col[h] - self.c_row[h], 0.0)
        return jnp.where(self.same, jnp.exp(gap), 0.0)


def inverse(mats):
    length = mats[0].shape[0]
    i, j = iota2((length, length), 0), iota2((length, length), 1)
    eye = (i == j).astype(f32)
    inner = [jnp.where((i // 8) == (j // 8), n, 0.0) for n in mats]
    s1 = [split(n) for n in inner]
    s2 = [split(mm(a, a, 1, 0)) for a in s1]
    low = [eye - n + (a[0].astype(f32) + a[1].astype(f32)) - mm(b, a, 1, 0) for n, a, b in zip(inner, s2, s1)]
    s4 = [split(mm(a, a, 1, 0)) for a in s2]
    inv = [t + mm(split(t), a, 1, 0) for t, a in zip(low, s4)]
    width = 8
    while width < length:
        cross = ((i // (2 * width)) == (j // (2 * width))) & ((i // width) > (j // width))
        st = [split(t) for t in inv]
        half = [mm(split(jnp.where(cross, n, 0.0)), t, 1, 0) for n, t in zip(mats, st)]
        inv = [t - mm(s, split(x), 1, 0) for t, s, x in zip(inv, st, half)]
        width *= 2
    return inv


def rows_from(x):
    ones = jnp.ones((8, x.shape[1]), bf16)
    return mm((ones,), split(x), 1, 1)[0:1]


def three_rows(x):
    hi = x.astype(bf16).astype(f32)
    mid = (x - hi).astype(bf16).astype(f32)
    return jnp.concatenate([hi, mid, x - hi - mid], 0)


def key_kernel(per_key, count, x_ref, w_ref, k_ref, f_ref, n_ref, t_ref, w_out, u_ref, a_ref, m_ref, s_ref, end_ref,
               chain, shift_ref):
    step = pl.program_id(0)
    length = k_ref.shape[1]
    own = w_ref.shape[1]
    eye = (iota2((DK, DK), 0) == iota2((DK, DK), 1)).astype(f32)

    @pl.when(step == 0)
    def _():
        for h in range(per_key):
            chain[h] = jnp.concatenate([eye, jnp.zeros((DK, DK), f32)], 1)

    w = w_ref[...]
    pairs = [(n, h) for n in range(count) for h in range(per_key)]
    metas, ks, vs = [], [], []
    for n in range(count):
        meta = Meta(x_ref[n, length:, :DK], per_key)
        z = conv_out(conv_inputs(x_ref, n, own, shift_ref.at[n], meta.code), w)
        act = z * sigmoid(z)
        k, _ = unit(act[:, :DK])
        k_ref[n] = k
        metas.append(meta)
        ks.append(k)
        vs.append(act[:, DK:])
    sk = [split(k) for k in ks]
    kk = [mm(s, s, 1, 1) for s in sk]
    fs = [metas[n].fading(h) for n, h in pairs]
    ns = [jnp.where(metas[n].strict, metas[n].beta[h] * kk[n] * f, 0.0) for (n, h), f in zip(pairs, fs)]
    ts = inverse(ns)
    rhs = [
        jnp.concatenate([metas[n].beta[h] * metas[n].entry[h] * ks[n], metas[n].beta[h] * vs[n][:, h * DK : (h + 1) * DK]], 1)
        for n, h in pairs
    ]
    wu = [mm(split(t), split(r), 1, 0) for t, r in zip(ts, rhs)]
    kwu = [mm(split(metas[n].tail[h] * ks[n]), split(x), 0, 0) for (n, h), x in zip(pairs, wu)]
    for m, (n, h) in enumerate(pairs):
        f_ref[n, h], n_ref[n, h], t_ref[n, h] = fs[m], ns[m], ts[m]
        w_out[n, h], u_ref[n, h] = wu[m][:, :DK], wu[m][:, DK:]
        a = metas[n].keep[h] * eye - kwu[m][:, :DK]
        a_ref[n, h] = a
        now = chain[h]
        m_ref[n, h], s_ref[n, h] = now[:, :DK], now[:, DK:]
        later = mm(split(a), split(now), 1, 0)
        chain[h] = jnp.concatenate([later[:, :DK], later[:, DK:] + kwu[m][:, DK:]], 1)
    for h in range(per_key):
        end_ref[h] = chain[h, :, DK:]


def query_kernel(per_key, count, x_ref, y_ref, w_ref, k_ref, f_ref, w_in, u_ref, a_ref, p_ref, y_out, pu_ref, r_ref,
                 m_ref, g_ref, start_ref, chain, shift_ref):
    step = pl.program_id(0)
    length = k_ref.shape[1]
    eye = (iota2((DK, DK), 0) == iota2((DK, DK), 1)).astype(f32)

    @pl.when(step == 0)
    def _():
        for h in range(per_key):
            chain[h] = jnp.concatenate([eye, jnp.zeros((DK, DK), f32)], 1)

    w = w_ref[...]
    pairs = [(n, h) for n in reversed(range(count)) for h in range(per_key)]
    metas, qs, qk = {}, {}, {}
    for n in range(count):
        metas[n] = Meta(x_ref[n, length:, :DK], per_key)
        z = conv_out(conv_inputs(y_ref, n, DK, shift_ref.at[n], metas[n].code), w)
        q, _ = unit(z * sigmoid(z))
        qs[n] = q * DK**-0.5
        qk[n] = mm(split(qs[n]), split(k_ref[n]), 1, 1)
    ps = [qk[n] * f_ref[n, h] for n, h in pairs]
    sp = [split(p) for p in ps]
    swu = [cat([split(w_in[n, h]), split(u_ref[n, h])], 1) for n, h in pairs]
    pwu = [mm(p, s, 1, 0) for p, s in zip(sp, swu)]
    ys = [metas[n].entry[h] * qs[n] - x[:, :DK] for (n, h), x in zip(pairs, pwu)]
    dos = [(y_ref[n, :length, (h + 1) * DK : (h + 2) * DK],) for n, h in pairs]
    gs = [mm(split(y), d, 0, 0) for y, d in zip(ys, dos)]
    rs = [mm(p, d, 0, 0) for p, d in zip(sp, dos)]
    for m, (n, h) in enumerate(pairs):
        p_ref[n, h], y_out[n, h], pu_ref[n, h], r_ref[n, h] = ps[m], ys[m], pwu[m][:, DK:], rs[m]
        now = chain[h]
        m_ref[n, h], g_ref[n, h] = now[:, :DK], now[:, DK:]
        later = mm(split(a_ref[n, h]), split(now), 0, 0)
        chain[h] = jnp.concatenate([later[:, :DK], later[:, DK:] + gs[m]], 1)
    for h in range(per_key):
        start_ref[h] = chain[h, :, DK:]


def read_kernel(per_key, count, in_ref, x_ref, y_ref, w_ref, k_ref, f_ref, p_ref, w_in, u_ref, y_in, pu_ref, m_ref,
                sl_ref, out_ref, d_ref, s_ref, dk_ref, dc_ref, rim_ref, dw_ref, shift_ref, dz_ref, doc_next):
    length = k_ref.shape[1]

    @pl.when(pl.program_id(0) == 0)
    def _():
        dw_ref[...] = jnp.zeros_like(dw_ref)
        dz_ref[...] = jnp.zeros_like(dz_ref)
        doc_next[...] = jnp.zeros_like(doc_next)

    w = w_ref[...]
    s_in = [split(in_ref[h]) for h in range(per_key)]
    pairs = [(n, h) for n in reversed(range(count)) for h in range(per_key)]
    metas, taps, sig, zs, hats, inv, qs, sq, sk = {}, {}, {}, {}, {}, {}, {}, {}, {}
    for n in range(count):
        metas[n] = Meta(x_ref[n, length:, :DK], per_key)
        taps[n] = conv_inputs(y_ref, n, DK, shift_ref.at[n], metas[n].code)
        zs[n] = conv_out(taps[n], w)
        sig[n] = sigmoid(zs[n])
        hats[n], inv[n] = unit(zs[n] * sig[n])
        qs[n] = hats[n] * DK**-0.5
        sq[n], sk[n] = split(qs[n]), split(k_ref[n])
    states = [sl_ref[n, h] + mm(split(m_ref[n, h]), s_in[h], 1, 0) for n, h in pairs]
    ss = [split(s) for s in states]
    both = [mm(cat([split(w_in[n, h]), split(y_in[n, h])], 0), s, 1, 0) for (n, h), s in zip(pairs, ss)]
    ds = [u_ref[n, h] - x[:length] for (n, h), x in zip(pairs, both)]
    dos = [(y_ref[n, :length, (h + 1) * DK : (h + 2) * DK],) for n, h in pairs]
    dps = [mm(do, split(d), 1, 1) for do, d in zip(dos, ds)]
    enters = [metas[n].entry[h] * mm(do, s, 1, 1) for (n, h), do, s in zip(pairs, dos, ss)]
    dpf = [split(dp * f_ref[n, h]) for (n, h), dp in zip(pairs, dps)]
    dqs = [e + mm(x, sk[n], 1, 0) for (n, h), e, x in zip(pairs, enters, dpf)]
    dks = [mm(x, sq[n], 0, 0) for (n, h), x in zip(pairs, dpf)]
    dq, dk = {}, {}
    for m, (n, h) in enumerate(pairs):
        s_ref[n, h], d_ref[n, h] = states[m], ds[m]
        out_ref[n, :, (h + 1) * DK : (h + 2) * DK] = (both[m][length:] + pu_ref[n, h]).astype(bf16)
        gaps = dps[m] * p_ref[n, h]
        dc_ref[n, h : h + 1, :] = rows_from(gaps + enters[m] * qs[n]) - jnp.sum(gaps, 0, keepdims=True)
        dq[n] = dq[n] + dqs[m] if h else dqs[m]
        dk[n] = dk[n] + dks[m] if h else dks[m]
    for n in reversed(range(count)):
        dk_ref[n] = dk[n]
        grad = unit_back(DK**-0.5 * dq[n], hats[n], inv[n])
        dz = grad * (sig[n] + zs[n] * sig[n] * (1.0 - sig[n]))
        dx = conv_back(dz, taps[n], w, metas[n].code, metas[n].plain, dz_ref, doc_next, dw_ref, rim_ref)
        out_ref[n, :, :DK] = dx.astype(bf16)


def write_kernel(per_key, count, in_ref, x_ref, w_ref, k_ref, f_ref, n_ref, t_ref, r_ref, m_ref, gl_ref, d_ref, s_ref,
                 dk_ref, dc_ref, dx_ref, rim_ref, dw_ref, shift_ref, dz_ref, doc_next):
    length = k_ref.shape[1]
    own = w_ref.shape[1]

    @pl.when(pl.program_id(0) == 0)
    def _():
        dw_ref[...] = jnp.zeros_like(dw_ref)
        dz_ref[...] = jnp.zeros_like(dz_ref)
        doc_next[...] = jnp.zeros_like(doc_next)

    w = w_ref[...]
    i, j = iota2((length, length), 0), iota2((length, length), 1)
    from_here = (i >= j).astype(f32).astype(bf16)
    g_in = [split(in_ref[h]) for h in range(per_key)]
    pairs = [(n, h) for n in reversed(range(count)) for h in range(per_key)]
    metas, taps, sig, zs, hats, inv, vs, sk = {}, {}, {}, {}, {}, {}, {}, {}
    for n in range(count):
        metas[n] = Meta(x_ref[n, length:, :DK], per_key)
        taps[n] = conv_inputs(x_ref, n, own, shift_ref.at[n], metas[n].code)
        zs[n] = conv_out(taps[n], w)
        sig[n] = sigmoid(zs[n])
        act = zs[n] * sig[n]
        hats[n], inv[n] = unit(act[:, :DK])
        vs[n] = act[:, DK:]
        sk[n] = split(k_ref[n])
    later = [gl_ref[n, h] + mm(split(m_ref[n, h]), g_in[h], 1, 0) for n, h in pairs]
    s_later = [split(x) for x in later]
    s_d = [split(d_ref[n, h]) for n, h in pairs]
    s_s = [split(s_ref[n, h]) for n, h in pairs]
    x1 = [mm(split(metas[n].tail[h] * k_ref[n]), s, 1, 0) for (n, h), s in zip(pairs, s_later)]
    es = [mm(split(t_ref[n, h]), split(r_ref[n, h] + x), 0, 0) for (n, h), x in zip(pairs, x1)]
    se = [split(e) for e in es]
    ends = [metas[n].tail[h] * mm(d, s, 1, 1) for (n, h), d, s in zip(pairs, s_d, s_later)]
    dns = [-mm(e, d, 1, 1) for e, d in zip(se, s_d)]
    ess = [mm(e, s, 1, 1) for e, s in zip(se, s_s)]
    dkk = [
        split(jnp.where(metas[n].strict, dn * metas[n].beta[h] * f_ref[n, h], 0.0)) for (n, h), dn in zip(pairs, dns)
    ]
    dks = [mm(x, sk[n], 1, 0) + mm(x, sk[n], 0, 0) for (n, h), x in zip(pairs, dkk)]
    dk, dv, rows = {n: dk_ref[n] for n in range(count)}, {}, {}
    for m, (n, h) in enumerate(pairs):
        meta, k = metas[n], k_ref[n]
        bes = meta.beta[h] * meta.entry[h] * ess[m]
        dk[n] = dk[n] + dks[m] - bes + ends[m]
        dv[n, h] = meta.beta[h] * es[m]
        nn = dns[m] * n_ref[n, h]
        ek = ends[m] * k
        dc = dc_ref[n, h : h + 1, :] + rows_from(nn - bes * k - ek) - jnp.sum(nn, 0, keepdims=True)
        last = jnp.sum(ek + later[m] * s_ref[n, h] * meta.keep[h], 0, keepdims=True)
        at_end = jnp.sum(last, 1, keepdims=True)
        rows[n, h] = mm(split(jnp.broadcast_to(dc, (8, length))), (from_here,), 1, 0)[0:1] + at_end
        own_v = vs[n][:, h * DK : (h + 1) * DK]
        rows[n, per_key + h] = (
            rows_from(es[m] * own_v - meta.entry[h] * ess[m] * k) + rows_from(nn) / meta.beta_row[h]
        )
    for n in reversed(range(count)):
        dk_act = unit_back(dk[n], hats[n], inv[n])
        d_act = jnp.concatenate([dk_act] + [dv[n, h] for h in range(per_key)], 1)
        dz = d_act * (sig[n] + zs[n] * sig[n] * (1.0 - sig[n]))
        dx = conv_back(dz, taps[n], w, metas[n].code, metas[n].plain, dz_ref, doc_next, dw_ref, rim_ref)
        dx_ref[n, :length, :] = dx.astype(bf16)
        gates = three_rows(jnp.concatenate([rows[n, m] for m in range(2 * per_key)], 0))
        gates = jnp.concatenate([gates, jnp.zeros((RIM - gates.shape[0], length), f32)], 0)
        dx_ref[n, length:, :] = jnp.concatenate([gates, jnp.zeros((RIM, own - DK), f32)], 1).astype(bf16)


def three(x):
    hi = lax.reduce_precision(x, 8, 7)
    mid = lax.reduce_precision(x - hi, 8, 7)
    return jnp.stack([hi, mid, x - hi - mid], -2).astype(bf16)


def local(mixed, conv_weight, log_decay, beta, doc_ids, out_grad):
    n_seq, n_dp = lax.axis_size("seq"), lax.axis_size("dp")
    rows, docs, og = mixed[0], doc_ids[0], out_grad[0]
    length, channels = rows.shape
    heads = log_decay.shape[1]
    key_heads = (channels - heads * DK) // (2 * DK)
    per_key = heads // key_heads
    G = key_heads
    assert n_seq % G == 0 and G * length >= DOC_MOST
    member = lax.axis_index("seq") % G
    team = [list(range(s, s + G)) for s in range(0, n_seq, G)]
    own = DK + per_key * DK

    def shifted(x, by):
        return lax.ppermute(x, "seq", [(s, s + by) for s in range(n_seq) if 0 <= s + by < n_seq])

    def by_member(x):
        return jnp.moveaxis(x.reshape(x.shape[:-1] + (G, -1)), -2, 0)

    def of_members(x):
        return jnp.moveaxis(x, 0, -2).reshape(x.shape[1:-1] + (-1,))

    def keys_values(x):
        return jnp.concatenate([by_member(x[..., G * DK : 2 * G * DK]), by_member(x[..., 2 * G * DK :])], -1)

    def swap(x):
        return lax.all_to_all(x, "seq", 0, 0, axis_index_groups=team)

    doc_row = jnp.pad((docs[-3:] + 1).astype(bf16), (0, channels - 3))
    rim = shifted(jnp.concatenate([rows[-3:], doc_row[None]], 0), 1)
    held = rim[3, :3] == (docs[0] + 1).astype(bf16)
    rim_rows = jnp.where(held[:, None], rim[:3], 0)
    code = (docs + 1 + CODE * jnp.sum(held.astype(jnp.int32))).astype(bf16)
    numbers = jnp.concatenate(
        [
            jnp.broadcast_to(code, (G, 1, length)),
            three(log_decay[0].reshape(G, per_key, length)).reshape(G, -1, length),
            three(beta[0].reshape(G, per_key, length)).reshape(G, -1, length),
        ],
        1,
    )
    numbers = jnp.pad(numbers, ((0, 0), (0, 0), (0, own - DK)))
    x = swap(jnp.concatenate([keys_values(rows), keys_values(rim_rows), numbers], 1))
    queries = jnp.concatenate([by_member(rows[:, : G * DK]), by_member(rim_rows[:, : G * DK])], 1)
    queries = jnp.pad(queries, ((0, 0), (0, RIM - 3), (0, 0)))
    asked = jnp.pad(by_member(og), ((0, 0), (0, RIM), (0, 0)))
    later_part = jnp.concatenate([queries, asked], 2)
    later_part, x = lax.optimization_barrier((later_part, x))
    y = swap(later_part)
    taps = conv_weight.astype(f32)
    w_kv = lax.dynamic_index_in_dim(keys_values(taps), member, 0, keepdims=False)
    w_q = lax.dynamic_index_in_dim(by_member(taps[:, : G * DK]), member, 0, keepdims=False)

    pair = (per_key, DK, DK)
    block = (length, DK)

    def call(kernel, count, name, back, fulls, ins, out_shapes, out_fulls, scratch, flops):
        steps = G // count
        order = (lambda s: steps - 1 - s) if back else (lambda s: s)

        def spec(shape):
            return pl.BlockSpec((count,) + shape, lambda s: (order(s),) + (0,) * len(shape))

        def full(shape):
            return pl.BlockSpec(shape, lambda s: (0,) * len(shape))

        in_specs = [full(a.shape) if m in fulls else spec(a.shape[1:]) for m, a in enumerate(ins)]
        return pl.pallas_call(
            functools.partial(kernel, per_key, count),
            grid=(steps,),
            in_specs=in_specs,
            out_specs=[spec(s) for s, _ in out_shapes] + [full(s) for s in out_fulls],
            out_shape=[jax.ShapeDtypeStruct((G,) + s, t) for s, t in out_shapes]
            + [jax.ShapeDtypeStruct(s, f32) for s in out_fulls],
            scratch_shapes=scratch(count),
            compiler_params=pltpu.CompilerParams(vmem_limit_bytes=VMEM),
            cost_estimate=pl.CostEstimate(flops=flops, bytes_accessed=8 << 20, transcendentals=0),
            name=name,
        )(*ins)

    def conv_scratch(width):
        return lambda count: [
            pltpu.VMEM((count, 8 + length, width), f32),
            pltpu.VMEM((16 + length, width), f32),
            pltpu.VMEM((8, DK), f32),
        ]

    def chain_scratch(width):
        return lambda count: [pltpu.VMEM((per_key, DK, 2 * DK), f32), pltpu.VMEM((count, 8 + length, width), f32)]

    k, f, n, t, w_out, u, a, m_fwd, s_local, end = call(
        key_kernel, COUNTS[0], "keys", False, (1,), (x, w_kv), [(block, f32)] + [(pair, f32)] * 8, [pair],
        chain_scratch(own), 15 * 10**9,
    )
    state_in = shifted(end, G)
    p, y_read, pu, r, m_bwd, g_local, start = call(
        query_kernel, COUNTS[1], "queries", True, (2,), (x, y, w_q, k, f, w_out, u, a), [(pair, f32)] * 6, [pair],
        chain_scratch(DK), 8 * 10**9,
    )
    back_in = shifted(start, -G)
    o, d, s, dk, dc, rim_q, dw_q = call(
        read_kernel, COUNTS[2], "reads", True, (0, 3), (state_in, x, y, w_q, k, f, p, w_out, u, y_read, pu, m_fwd, s_local),
        [((length, own), bf16), (pair, f32), (pair, f32), (block, f32), ((per_key, length), f32)],
        [(3, DK), (4, DK)], conv_scratch(DK), 8 * 10**9,
    )
    o = swap(o)
    dx, rim_kv, dw_kv = call(
        write_kernel, COUNTS[3], "writes", True, (0, 2), (back_in, x, w_kv, k, f, n, t, r, m_bwd, g_local, d, s, dk, dc),
        [((length + RIM, own), bf16)], [(3, own), (4, own)], conv_scratch(own), 15 * 10**9,
    )
    dx = swap(dx)

    small = jnp.concatenate([jnp.concatenate([dw_q, dw_kv], 1), jnp.concatenate([rim_q, rim_kv], 1)], 0)
    gathered = small[None]
    step = 1
    while step < G:
        other = lax.ppermute(gathered, "seq", [(s, s ^ step) for s in range(n_seq)])
        upper = (member & step) > 0
        gathered = jnp.where(upper, jnp.concatenate([other, gathered], 0), jnp.concatenate([gathered, other], 0))
        step *= 2
    total = of_members(gathered[:, :, :DK]), of_members(gathered[:, :, DK : 2 * DK]), of_members(gathered[:, :, 2 * DK :])
    total = jnp.concatenate(total, -1)
    d_weight, rim_grad = total[:4], total[4:]
    step = G
    while step < n_seq:
        d_weight = d_weight + lax.ppermute(d_weight, "seq", [(s, s ^ step) for s in range(n_seq)])
        step *= 2
    step = 1
    while step < n_dp:
        d_weight = d_weight + lax.ppermute(d_weight, "dp", [(s, s ^ step) for s in range(n_dp)])
        step *= 2
    incoming = lax.ppermute(rim_grad.astype(bf16), "seq", [(s, s - 1) for s in range(G, n_seq, G)])

    output = of_members(o[:, :, DK:])
    d_rows = jnp.concatenate(
        [of_members(o[:, :, :DK]), of_members(dx[:, :length, :DK]), of_members(dx[:, :length, DK:])], -1
    )
    d_tail = (d_rows[-3:].astype(f32) + incoming.astype(f32)).astype(bf16)
    d_rows = jnp.concatenate([d_rows[:-3], d_tail], 0)
    gates = dx[:, length : length + 6 * per_key, :DK].astype(f32).reshape(G, 3, 2, per_key, length)
    gates = gates[:, 0] + (gates[:, 1] + gates[:, 2])
    d_decay, d_beta = gates[:, 0].reshape(heads, length), gates[:, 1].reshape(heads, length)
    return (output[None], d_rows[None], d_weight, d_decay[None], d_beta[None])


def solution(mesh):
    in_specs = (
        P("dp", "seq", None),
        P(),
        P("dp", None, "seq"),
        P("dp", None, "seq"),
        P("dp", "seq"),
        P("dp", "seq", None),
    )
    out_specs = (
        P("dp", "seq", None),
        P("dp", "seq", None),
        P(),
        P("dp", None, "seq"),
        P("dp", None, "seq"),
    )
    return jax.shard_map(
        local, mesh=mesh, in_specs=in_specs, out_specs=out_specs, check_vma=False
    )
```

```python
import functools

import jax
import jax.numpy as jnp
from jax import lax
from jax.experimental import pallas as pl
from jax.experimental.pallas import tpu as pltpu
from jax.sharding import PartitionSpec as P

DK = 128
DOC_MOST = 1024
EPS = 1e-6
CODE = 16
COUNTS = (4, 4, 2, 4)
VMEM = 56 << 20
RIM = 16
f32 = jnp.float32
bf16 = jnp.bfloat16


def dg(a, b, ca, cb):
    return lax.dot_general(a, b, (((ca,), (cb,)), ((), ())), preferred_element_type=f32)


def split(x):
    hi = x.astype(bf16)
    return (hi, (x - hi.astype(f32)).astype(bf16))


def cat(parts, axis):
    return tuple(jnp.concatenate(leaves, axis) for leaves in zip(*parts))


def mm(a, b, ca, cb):
    out = dg(a[0], b[0], ca, cb)
    if len(b) > 1:
        out = out + dg(a[0], b[1], ca, cb)
    if len(a) > 1:
        out = out + dg(a[1], b[0], ca, cb)
    return out


def iota2(shape, dim):
    return lax.broadcasted_iota(jnp.int32, shape, dim)


def conv_inputs(x_ref, n, width, shift_ref, docs, lane=0):
    length = docs.shape[0]
    to = slice(0, width)
    shift_ref[5:8, to] = x_ref[n, length : length + 3, lane : lane + width].astype(f32)
    rows = x_ref[n, :length, lane : lane + width].astype(f32)
    shift_ref[8 : 8 + length, to] = rows
    at = iota2((length, DK), 0)
    first = docs[0:1, :]
    taps = [rows]
    for off in (1, 2, 3):
        earlier = jnp.where(at >= off, pltpu.roll(docs, off, 0), first)
        ok = earlier == docs
        moved = shift_ref[8 - off : 8 - off + length, to]
        taps.append(jnp.where(wide(ok, width), moved, 0.0))
    return taps


def wide(x, width):
    return jnp.concatenate([x] * (width // DK), 1)


def conv_out(taps, w):
    return sum(w[3 - off : 4 - off, :] * taps[off] for off in range(4))


def conv_back(dz, taps, w, code, plain, dz_ref, doc_next, dw_ref, rim_ref):
    length, width = dz.shape
    dz_ref[8 + length :, :] = dz_ref[8:16, :]
    dz_ref[8 : 8 + length, :] = dz
    docs_after = doc_next[...]
    at = iota2((length, DK), 0)
    dx = w[3:4, :] * dz
    for off in (1, 2, 3):
        ahead = pltpu.roll(plain, length - off, 0)
        for r in range(off):
            ahead = jnp.where(at == length - off + r, docs_after[r : r + 1, :], ahead)
        moved = dz_ref[8 + off : 8 + off + length, :]
        dx = dx + w[3 - off : 4 - off, :] * jnp.where(wide(ahead == plain, width), moved, 0.0)
    doc_next[...] = plain[0:8, :]
    for off in range(4):
        dw_ref[3 - off : 4 - off, :] += jnp.sum(dz * taps[off], 0, keepdims=True)
    head = jnp.where(wide(code[0:8, :] == code[0:1, :], width), dz[0:8, :], 0.0)
    held = wide(code[0:1, :], width)
    for r in range(3):
        total = 0.0
        for off in range(3 - r, 4):
            total = total + w[3 - off : 4 - off, :] * head[r + off - 3 : r + off - 2, :]
        rim_ref[r : r + 1, :] = jnp.where(held >= CODE * (3 - r), total, 0.0)
    return dx


def unit(x):
    inv = lax.rsqrt(jnp.sum(x * x, -1, keepdims=True) + EPS)
    return x * inv, inv


def unit_back(grad, hat, inv):
    return inv * (grad - hat * jnp.sum(grad * hat, -1, keepdims=True))


def sigmoid(z):
    return 1.0 / (1.0 + jnp.exp(-z))


class Meta:
    def __init__(self, numbers, per_key):
        length = numbers.shape[1]
        rows = numbers.astype(f32)
        row_at = iota2((RIM, DK), 0)
        i, j = iota2((length, length), 0), iota2((length, length), 1)
        self.lower, self.strict = i >= j, i > j

        def column(first, count):
            pick = ((row_at >= first) & (row_at < first + count)).astype(f32).astype(bf16)
            return dg(numbers, pick, 0, 0)

        self.code = column(3, 1)
        self.plain = self.code - CODE * jnp.floor(self.code * (1.0 / CODE))
        code_row = rows[3:4]
        self.same = (self.code == code_row) & self.lower
        carry = (self.code >= CODE) & (self.code == code_row[:, 0:1])
        ending = self.code == code_row[:, length - 1 : length]
        until = (i <= j).astype(f32).astype(bf16)
        row_sums = dg(numbers, until, 1, 0)
        ones = jnp.ones((length, DK), bf16)
        self.c_row, self.c_col, self.beta, self.beta_row = [], [], [], []
        self.entry, self.tail, self.keep, self.both = [], [], [], []
        for h in range(per_key):
            at = 4 + 3 * h
            self.c_row.append(row_sums[at : at + 1] + row_sums[at + 1 : at + 2] + row_sums[at + 2 : at + 3])
            c_col = 0.0
            for part in (2, 1, 0):
                c_col = c_col + dg(jnp.where(self.lower, rows[at + part : at + part + 1], 0.0).astype(bf16), ones, 1, 0)
            self.c_col.append(c_col)
            at = 4 + 3 * per_key + 3 * h
            self.beta.append(column(at, 3))
            self.beta_row.append(rows[at : at + 1] + rows[at + 1 : at + 2] + rows[at + 2 : at + 3])
            self.entry.append(jnp.where(carry, jnp.exp(c_col), 0.0))
            last = self.c_row[h][:, length - 1 : length]
            self.tail.append(jnp.where(ending, jnp.exp(jnp.minimum(last - c_col, 0.0)), 0.0))
            self.keep.append(self.entry[h][length - 1 : length, :])
            self.both.append(self.beta[h] * self.entry[h])

    def fading(self, h):
        gap = jnp.minimum(self.c_col[h] - self.c_row[h], 0.0)
        return jnp.where(self.same, jnp.exp(gap), 0.0)


def inverse(mats):
    length = mats[0].shape[0]
    i, j = iota2((length, length), 0), iota2((length, length), 1)
    eye = (i == j).astype(f32)
    inner = [jnp.where((i // 8) == (j // 8), n, 0.0) for n in mats]
    s1 = [split(n) for n in inner]
    s2 = [split(mm(a, a, 1, 0)) for a in s1]
    low = [eye - n + (a[0].astype(f32) + a[1].astype(f32)) - mm(b, a, 1, 0) for n, a, b in zip(inner, s2, s1)]
    s4 = [split(mm(a, a, 1, 0)) for a in s2]
    inv = [t + mm(split(t), a, 1, 0) for t, a in zip(low, s4)]
    width = 8
    while width < length:
        cross = ((i // (2 * width)) == (j // (2 * width))) & ((i // width) > (j // width))
        st = [split(t) for t in inv]
        half = [mm(split(jnp.where(cross, n, 0.0)), t, 1, 0) for n, t in zip(mats, st)]
        inv = [t - mm(s, split(x), 1, 0) for t, s, x in zip(inv, st, half)]
        width *= 2
    return inv


def rows_from(xs):
    wide_x = split(jnp.concatenate(xs, 1))
    shape = (len(xs) * DK, DK)
    pick = ((iota2(shape, 0) // DK) == iota2(shape, 1)).astype(f32).astype(bf16)
    return mm(wide_x, (pick,), 1, 0).T


def key_kernel(per_key, count, x_ref, w_ref, k_ref, t_ref, w_out, u_ref, a_ref, m_ref, s_ref, end_ref, chain, shift_ref):
    step = pl.program_id(0)
    length = k_ref.shape[1]
    own = w_ref.shape[1]
    eye = (iota2((DK, DK), 0) == iota2((DK, DK), 1)).astype(f32)

    @pl.when(step == 0)
    def _():
        for h in range(per_key):
            chain[h] = jnp.concatenate([eye, jnp.zeros((DK, DK), f32)], 1)

    w = w_ref[...]
    pairs = [(n, h) for n in range(count) for h in range(per_key)]
    metas, ks, vs = [], [], []
    for n in range(count):
        meta = Meta(x_ref[n, length:, :DK], per_key)
        z = conv_out(conv_inputs(x_ref, n, own, shift_ref.at[n], meta.code), w)
        act = z * sigmoid(z)
        k, _ = unit(act[:, :DK])
        k_ref[n] = k
        metas.append(meta)
        ks.append(k)
        vs.append(act[:, DK:])
    sk = [split(k) for k in ks]
    kk = [mm(s, s, 1, 1) for s in sk]
    ns = [
        jnp.where(metas[n].strict, metas[n].beta[h] * kk[n] * metas[n].fading(h), 0.0) for n, h in pairs
    ]
    ts = inverse(ns)
    rhs = [
        jnp.concatenate([metas[n].both[h] * ks[n], metas[n].beta[h] * vs[n][:, h * DK : (h + 1) * DK]], 1)
        for n, h in pairs
    ]
    wu = [mm(split(t), split(r), 1, 0) for t, r in zip(ts, rhs)]
    kwu = [mm(split(metas[n].tail[h] * ks[n]), split(x), 0, 0) for (n, h), x in zip(pairs, wu)]
    for m, (n, h) in enumerate(pairs):
        t_ref[n, h], w_out[n, h], u_ref[n, h] = ts[m], wu[m][:, :DK], wu[m][:, DK:]
        a = metas[n].keep[h] * eye - kwu[m][:, :DK]
        a_ref[n, h] = a
        now = chain[h]
        m_ref[n, h], s_ref[n, h] = now[:, :DK], now[:, DK:]
        later = mm(split(a), split(now), 1, 0)
        chain[h] = jnp.concatenate([later[:, :DK], later[:, DK:] + kwu[m][:, DK:]], 1)
    for h in range(per_key):
        end_ref[h] = chain[h, :, DK:]


def query_kernel(per_key, count, x_ref, y_ref, w_ref, k_ref, t_ref, a_ref, e_ref, m_ref, g_ref, start_ref, chain, shift_ref):
    step = pl.program_id(0)
    length = k_ref.shape[1]
    eye = (iota2((DK, DK), 0) == iota2((DK, DK), 1)).astype(f32)

    @pl.when(step == 0)
    def _():
        for h in range(per_key):
            chain[h] = jnp.concatenate([eye, jnp.zeros((DK, DK), f32)], 1)

    w = w_ref[...]
    pairs = [(n, h) for n in reversed(range(count)) for h in range(per_key)]
    metas, sq, sk, qk = {}, {}, {}, {}
    for n in range(count):
        metas[n] = Meta(x_ref[n, length:, :DK], per_key)
        z = conv_out(conv_inputs(y_ref, n, DK, shift_ref.at[n], metas[n].code), w)
        q, _ = unit(z * sigmoid(z))
        sq[n], sk[n] = split(q * DK**-0.5), split(k_ref[n])
        qk[n] = mm(sq[n], sk[n], 1, 1)
    dos = [(y_ref[n, :length, (h + 1) * DK : (h + 2) * DK],) for n, h in pairs]
    rs = [mm(split(qk[n] * metas[n].fading(h)), d, 0, 0) for (n, h), d in zip(pairs, dos)]
    es = [mm(split(t_ref[n, h]), split(r), 0, 0) for (n, h), r in zip(pairs, rs)]
    gs = []
    for at in range(0, len(pairs), per_key):
        n = pairs[at][0]
        asked = jnp.concatenate([metas[n].entry[h] * dos[at + h][0].astype(f32) for h in range(per_key)], 1)
        undone = jnp.concatenate([-metas[n].both[h] * es[at + h] for h in range(per_key)], 1)
        b = mm(cat([sq[n], sk[n]], 0), cat([split(asked), split(undone)], 0), 0, 0)
        gs += [b[:, h * DK : (h + 1) * DK] for h in range(per_key)]
    for m, (n, h) in enumerate(pairs):
        e_ref[n, h] = es[m]
        now = chain[h]
        m_ref[n, h], g_ref[n, h] = now[:, :DK], now[:, DK:]
        later = mm(split(a_ref[n, h]), split(now), 0, 0)
        chain[h] = jnp.concatenate([later[:, :DK], later[:, DK:] + gs[m]], 1)
    for h in range(per_key):
        start_ref[h] = chain[h, :, DK:]


def read_kernel(per_key, count, in_ref, x_ref, y_ref, w_ref, k_ref, w_in, u_ref, m_ref, sl_ref, out_ref, d_ref, s_ref,
                dk_ref, dc_ref, rim_ref, dw_ref, shift_ref, dz_ref, doc_next):
    length = k_ref.shape[1]

    @pl.when(pl.program_id(0) == 0)
    def _():
        dw_ref[...] = jnp.zeros_like(dw_ref)
        dz_ref[...] = jnp.zeros_like(dz_ref)
        doc_next[...] = jnp.zeros_like(doc_next)

    w = w_ref[...]
    s_in = [split(in_ref[h]) for h in range(per_key)]
    pairs = [(n, h) for n in reversed(range(count)) for h in range(per_key)]
    metas, taps, sig, zs, hats, inv, qs, sq, sk, qk = {}, {}, {}, {}, {}, {}, {}, {}, {}, {}
    for n in range(count):
        metas[n] = Meta(x_ref[n, length:, :DK], per_key)
        taps[n] = conv_inputs(y_ref, n, DK, shift_ref.at[n], metas[n].code)
        zs[n] = conv_out(taps[n], w)
        sig[n] = sigmoid(zs[n])
        hats[n], inv[n] = unit(zs[n] * sig[n])
        qs[n] = hats[n] * DK**-0.5
        sq[n], sk[n] = split(qs[n]), split(k_ref[n])
        qk[n] = mm(sq[n], sk[n], 1, 1)
    states = [sl_ref[n, h] + mm(split(m_ref[n, h]), s_in[h], 1, 0) for n, h in pairs]
    ss = [split(s) for s in states]
    fs = [metas[n].fading(h) for n, h in pairs]
    ds = [u_ref[n, h] - mm(split(w_in[n, h]), s, 1, 0) for (n, h), s in zip(pairs, ss)]
    sd = [split(d) for d in ds]
    qss = {n: mm(sq[n], cat([ss[m] for m in range(len(pairs)) if pairs[m][0] == n], 1), 1, 0) for n in range(count)}
    outs = [
        metas[n].entry[h] * qss[n][:, h * DK : (h + 1) * DK] + mm(split(qk[n] * f), d, 1, 0)
        for (n, h), f, d in zip(pairs, fs, sd)
    ]
    dos = [(y_ref[n, :length, (h + 1) * DK : (h + 2) * DK],) for n, h in pairs]
    back = [mm(do, cat([d, s], 0), 1, 1) for do, d, s in zip(dos, sd, ss)]
    dps = [x[:, :length] * f for x, f in zip(back, fs)]
    enters = [metas[n].entry[h] * x[:, length:] for (n, h), x in zip(pairs, back)]
    dq, dk = {}, {}
    for n in range(count):
        mine = [m for m in range(len(pairs)) if pairs[m][0] == n]
        s_dp = split(sum(dps[m] for m in mine))
        dq[n] = mm(s_dp, sk[n], 1, 0) + sum(enters[m] for m in mine)
        dk[n] = mm(s_dp, sq[n], 0, 0)
        gaps = [dps[m] * qk[n] for m in mine]
        sums = rows_from([g + enters[m] * qs[n] for g, m in zip(gaps, mine)])
        for h, m in enumerate(mine):
            s_ref[n, h], d_ref[n, h] = states[m], ds[m]
            out_ref[n, :, (h + 1) * DK : (h + 2) * DK] = outs[m].astype(bf16)
            dc_ref[n, h : h + 1, :] = sums[h : h + 1] - jnp.sum(gaps[h], 0, keepdims=True)
    for n in reversed(range(count)):
        dk_ref[n] = dk[n]
        grad = unit_back(DK**-0.5 * dq[n], hats[n], inv[n])
        dz = grad * (sig[n] + zs[n] * sig[n] * (1.0 - sig[n]))
        dx = conv_back(dz, taps[n], w, metas[n].code, metas[n].plain, dz_ref, doc_next, dw_ref, rim_ref)
        out_ref[n, :, :DK] = dx.astype(bf16)


def write_kernel(per_key, count, in_ref, x_ref, w_ref, k_ref, t_ref, e_ref, m_ref, gl_ref, d_ref, s_ref, dk_ref, dc_ref,
                 dwq_ref, rimq_ref, dx_ref, gates_ref, small_ref, shift_ref, dz_ref, doc_next, dw_ref, rim_ref):
    step, steps = pl.program_id(0), pl.num_programs(0)
    length = k_ref.shape[1]
    own = w_ref.shape[1]

    @pl.when(step == 0)
    def _():
        dw_ref[...] = jnp.zeros_like(dw_ref)
        dz_ref[...] = jnp.zeros_like(dz_ref)
        doc_next[...] = jnp.zeros_like(doc_next)

    w = w_ref[...]
    i, j = iota2((length, length), 0), iota2((length, length), 1)
    from_here = (i >= j).astype(f32).astype(bf16)
    g_in = [split(in_ref[h]) for h in range(per_key)]
    pairs = [(n, h) for n in reversed(range(count)) for h in range(per_key)]
    metas, taps, sig, zs, hats, inv, vs, sk, kk = {}, {}, {}, {}, {}, {}, {}, {}, {}
    for n in range(count):
        metas[n] = Meta(x_ref[n, length:, :DK], per_key)
        taps[n] = conv_inputs(x_ref, n, own, shift_ref.at[n], metas[n].code)
        zs[n] = conv_out(taps[n], w)
        sig[n] = sigmoid(zs[n])
        act = zs[n] * sig[n]
        hats[n], inv[n] = unit(act[:, :DK])
        vs[n] = act[:, DK:]
        sk[n] = split(k_ref[n])
        kk[n] = mm(sk[n], sk[n], 1, 1)
    later = [gl_ref[n, h] + mm(split(m_ref[n, h]), g_in[h], 1, 0) for n, h in pairs]
    s_later = [split(x) for x in later]
    s_d = [split(d_ref[n, h]) for n, h in pairs]
    s_s = [split(s_ref[n, h]) for n, h in pairs]
    kg = {n: mm(sk[n], cat([s_later[m] for m in range(len(pairs)) if pairs[m][0] == n], 1), 1, 0) for n in range(count)}
    x1 = [metas[n].tail[h] * kg[n][:, h * DK : (h + 1) * DK] for n, h in pairs]
    es = [e_ref[n, h] + mm(split(t_ref[n, h]), split(x), 0, 0) for (n, h), x in zip(pairs, x1)]
    se = [split(e) for e in es]
    ends = [metas[n].tail[h] * mm(d, s, 1, 1) for (n, h), d, s in zip(pairs, s_d, s_later)]
    back = [mm(e, cat([d, s], 0), 1, 1) for e, d, s in zip(se, s_d, s_s)]
    ess = [x[:, length:] for x in back]
    dkk = [
        jnp.where(metas[n].strict, x[:, :length] * (-metas[n].beta[h] * metas[n].fading(h)), 0.0)
        for (n, h), x in zip(pairs, back)
    ]
    dk, dv, rows = {}, {}, {}
    for n in range(count):
        mine = [m for m in range(len(pairs)) if pairs[m][0] == n]
        meta, k = metas[n], k_ref[n]
        s_dkk = split(sum(dkk[m] for m in mine))
        bes = [meta.both[h] * ess[m] for h, m in enumerate(mine)]
        dk[n] = dk_ref[n] + mm(s_dkk, sk[n], 1, 0) + mm(s_dkk, sk[n], 0, 0) + sum(ends[m] - b for b, m in zip(bes, mine))
        nn = [dkk[m] * kk[n] for m in mine]
        ek = [ends[m] * k for m in mine]
        mats = [x - b * k - y for x, b, y in zip(nn, bes, ek)] + nn
        mats += [
            es[m] * vs[n][:, h * DK : (h + 1) * DK] - meta.entry[h] * ess[m] * k for h, m in enumerate(mine)
        ]
        sums = rows_from(mats)
        dc = [
            dc_ref[n, h : h + 1, :] + sums[h : h + 1] - jnp.sum(nn[h], 0, keepdims=True) for h in range(per_key)
        ]
        dc = jnp.concatenate(dc + [jnp.zeros((8 - per_key, length), f32)], 0)
        decays = mm(split(dc), (from_here,), 1, 0)
        for h, m in enumerate(mine):
            dv[n, h] = meta.beta[h] * es[m]
            last = jnp.sum(ek[h] + later[m] * s_ref[n, h] * meta.keep[h], 0, keepdims=True)
            rows[n, h] = decays[h : h + 1] + jnp.sum(last, 1, keepdims=True)
            rows[n, per_key + h] = (
                sums[2 * per_key + h : 2 * per_key + h + 1] + sums[per_key + h : per_key + h + 1] / meta.beta_row[h]
            )
    for n in reversed(range(count)):
        dk_act = unit_back(dk[n], hats[n], inv[n])
        d_act = jnp.concatenate([dk_act] + [dv[n, h] for h in range(per_key)], 1)
        dz = d_act * (sig[n] + zs[n] * sig[n] * (1.0 - sig[n]))
        dx = conv_back(dz, taps[n], w, metas[n].code, metas[n].plain, dz_ref, doc_next, dw_ref, rim_ref)
        dx_ref[n] = dx.astype(bf16)
        gates_ref[n] = jnp.concatenate([rows[n, m] for m in range(2 * per_key)], 0)

    @pl.when(step == steps - 1)
    def _():
        small_ref[0:4, :DK], small_ref[0:4, DK:] = dwq_ref[...], dw_ref[...]
        small_ref[4:7, :DK], small_ref[4:7, DK:] = rimq_ref[...], rim_ref[...]
        small_ref[7:8, :] = jnp.zeros((1, small_ref.shape[1]), f32)


def places(G, per_key):
    starts = [lambda m: m * DK, lambda m: (G + m) * DK]
    starts += [lambda m, h=h: (2 * G + m * per_key + h) * DK for h in range(per_key)]
    return starts


def tail_kernel(groups, next_ref, gates_ref, dx_ref, *refs):
    refs, out_ref = refs[:-1], refs[-1]
    taps = [ref[0:4, :] for ref in refs]
    while len(taps) > 1:
        taps = [i + j for i, j in zip(taps[::2], taps[1::2])]
    rims = sum(next_ref[q] * refs[q][4:7, :] for q in range(groups))
    parts = range(refs[0].shape[1] // DK)
    shared = [taps[0][:, m * DK : (m + 1) * DK] for m in parts] + [rims[:, m * DK : (m + 1) * DK] for m in parts]
    for m in range(out_ref.shape[0]):
        x = jnp.concatenate([gates_ref[m]] + shared, 0)
        hi = x.astype(bf16)
        mid = (x - hi.astype(f32)).astype(bf16)
        low = (x - hi.astype(f32) - mid.astype(f32)).astype(bf16)
        out_ref[m] = jnp.concatenate([hi, mid, low], 1)


def reads_kernel(G, width, o_ref, out_ref):
    for m in range(G):
        out_ref[:, m * width : (m + 1) * width] = o_ref[m, :, DK:]


def unpack_kernel(G, per_key, last_ref, o_ref, dx_ref, rows_ref, dw_ref, decay_ref, beta_ref):
    length = rows_ref.shape[0]
    early = length - RIM
    gates, taps = 2 * per_key, 4 * (2 + per_key)
    for m in range(G):
        x = dx_ref[m, length:, :].astype(f32)
        x = x[:, :DK] + (x[:, DK : 2 * DK] + x[:, 2 * DK : 3 * DK])
        decay_ref[m * per_key : (m + 1) * per_key, :] = x[:per_key]
        beta_ref[m * per_key : (m + 1) * per_key, :] = x[per_key:gates]
        for part, start in enumerate(places(G, per_key)):
            to = slice(start(m), start(m) + DK)
            ref, lane = (o_ref, 0) if part == 0 else (dx_ref, (part - 1) * DK)
            rows_ref[:early, to] = ref[m, :early, lane : lane + DK]
            rim = x[gates + taps + 3 * part : gates + taps + 3 * part + 3] * last_ref[0]
            rim = jnp.concatenate([jnp.zeros((RIM - 3, DK), f32), rim], 0)
            rows_ref[early:, to] = (ref[m, early:length, lane : lane + DK].astype(f32) + rim).astype(bf16)
            dw_ref[:, to] = x[gates + 4 * part : gates + 4 * part + 4]


def three(x):
    hi = lax.reduce_precision(x, 8, 7)
    mid = lax.reduce_precision(x - hi, 8, 7)
    return jnp.stack([hi, mid, x - hi - mid], -2).astype(bf16)


def local(mixed, conv_weight, log_decay, beta, doc_ids, out_grad):
    n_seq, n_dp = lax.axis_size("seq"), lax.axis_size("dp")
    rows, docs, og = mixed[0], doc_ids[0], out_grad[0]
    length, channels = rows.shape
    heads = log_decay.shape[1]
    key_heads = (channels - heads * DK) // (2 * DK)
    per_key = heads // key_heads
    G = key_heads
    assert n_seq % G == 0 and G * length >= DOC_MOST
    member = lax.axis_index("seq") % G
    team = [list(range(s, s + G)) for s in range(0, n_seq, G)]
    own = DK + per_key * DK

    def shifted(x, by):
        return lax.ppermute(x, "seq", [(s, s + by) for s in range(n_seq) if 0 <= s + by < n_seq])

    def by_member(x):
        return jnp.moveaxis(x.reshape(x.shape[:-1] + (G, -1)), -2, 0)

    def of_members(x):
        return jnp.moveaxis(x, 0, -2).reshape(x.shape[1:-1] + (-1,))

    def keys_values(x):
        return jnp.concatenate([by_member(x[..., G * DK : 2 * G * DK]), by_member(x[..., 2 * G * DK :])], -1)

    def swap(x):
        return lax.all_to_all(x, "seq", 0, 0, axis_index_groups=team)

    doc_row = jnp.pad((docs[-3:] + 1).astype(bf16), (0, channels - 3))
    rim = shifted(jnp.concatenate([rows[-3:], doc_row[None]], 0), 1)
    held = rim[3, :3] == (docs[0] + 1).astype(bf16)
    rim_rows = jnp.where(held[:, None], rim[:3], 0)
    code = (docs + 1 + CODE * jnp.sum(held.astype(jnp.int32))).astype(bf16)
    numbers = jnp.concatenate(
        [
            jnp.broadcast_to(code, (G, 1, length)),
            three(log_decay[0].reshape(G, per_key, length)).reshape(G, -1, length),
            three(beta[0].reshape(G, per_key, length)).reshape(G, -1, length),
        ],
        1,
    )
    numbers = jnp.pad(numbers, ((0, 0), (0, 0), (0, own - DK)))
    x = swap(jnp.concatenate([keys_values(rows), keys_values(rim_rows), numbers], 1))
    queries = jnp.concatenate([by_member(rows[:, : G * DK]), by_member(rim_rows[:, : G * DK])], 1)
    queries = jnp.pad(queries, ((0, 0), (0, RIM - 3), (0, 0)))
    asked = jnp.pad(by_member(og), ((0, 0), (0, RIM), (0, 0)))
    y = jnp.concatenate([queries, asked], 2)
    y, x = lax.optimization_barrier((y, x))
    y = swap(y)
    taps = conv_weight.astype(f32)
    w_q, w_k, w_v = [
        lax.dynamic_index_in_dim(by_member(part), member, 0, keepdims=False)
        for part in (taps[:, : G * DK], taps[:, G * DK : 2 * G * DK], taps[:, 2 * G * DK :])
    ]
    w_kv = jnp.concatenate([w_k, w_v], 1)

    pair = (per_key, DK, DK)
    block = (length, DK)

    def call(kernel, count, name, back, fulls, ins, out_shapes, out_fulls, scratch, flops, behind=0):
        steps = G // count
        out_fulls = [s if isinstance(s[0], tuple) else (s, f32) for s in out_fulls]
        order = (lambda s: steps - 1 - s) if back else (lambda s: s)

        def spec(shape):
            return pl.BlockSpec((count,) + shape, lambda s: (order(s),) + (0,) * len(shape))

        def full(shape):
            return pl.BlockSpec(shape, lambda s: (0,) * len(shape))

        in_specs = [full(a.shape) if m in fulls else spec(a.shape[1:]) for m, a in enumerate(ins)]
        return pl.pallas_call(
            functools.partial(kernel, per_key, count),
            grid=(steps,),
            in_specs=in_specs,
            out_specs=[spec(s) for s, _ in out_shapes] + [full(s) for s, _ in out_fulls],
            out_shape=[
                jax.ShapeDtypeStruct((G, s[0] + (0 if m else behind)) + s[1:], t) for m, (s, t) in enumerate(out_shapes)
            ]
            + [jax.ShapeDtypeStruct(s, t) for s, t in out_fulls],
            scratch_shapes=scratch(count),
            compiler_params=pltpu.CompilerParams(vmem_limit_bytes=VMEM),
            cost_estimate=pl.CostEstimate(flops=flops, bytes_accessed=8 << 20, transcendentals=0),
            name=name,
        )(*ins)

    def conv_scratch(width):
        return lambda count: [
            pltpu.VMEM((count, 8 + length, width), f32),
            pltpu.VMEM((16 + length, width), f32),
            pltpu.VMEM((8, DK), f32),
        ]

    def chain_scratch(width):
        return lambda count: [pltpu.VMEM((per_key, DK, 2 * DK), f32), pltpu.VMEM((count, 8 + length, width), f32)]

    k, t, w_out, u, a, m_fwd, s_local, end = call(
        key_kernel, COUNTS[0], "keys", False, (1,), (x, w_kv), [(block, f32)] + [(pair, f32)] * 6, [pair],
        chain_scratch(own), 15 * 10**9,
    )
    state_in = shifted(end, G)
    e, m_bwd, g_local, start = call(
        query_kernel, COUNTS[1], "queries", True, (2,), (x, y, w_q, k, t, a), [(pair, f32)] * 3, [pair],
        chain_scratch(DK), 8 * 10**9,
    )
    back_in = shifted(start, -G)
    o, d, s, dk, dc, rim_q, dw_q = call(
        read_kernel, COUNTS[2], "reads", True, (0, 3), (state_in, x, y, w_q, k, w_out, u, m_fwd, s_local),
        [((length, own), bf16), (pair, f32), (pair, f32), (block, f32), ((per_key, length), f32)],
        [(3, DK), (4, DK)], conv_scratch(DK), 8 * 10**9,
    )
    o = swap(o)
    behind = 2 * per_key + 7 * (2 + per_key)
    assert behind == 2 * RIM
    dx, gates, small = call(
        write_kernel, COUNTS[3], "writes", True, (0, 2, 12, 13),
        (back_in, x, w_kv, k, t, e, m_bwd, g_local, d, s, dk, dc, dw_q, rim_q),
        [((length, own), bf16), ((2 * per_key, length), f32)], [(8, DK + own)],
        lambda count: conv_scratch(own)(count) + [pltpu.VMEM((4, own), f32), pltpu.VMEM((3, own), f32)],
        15 * 10**9, behind,
    )
    me = lax.axis_index("seq")
    terms, nexts = [], []
    for p in range(n_dp):
        for q in range(0, n_seq, G):
            perm = [(i * n_seq + j, (i ^ p) * n_seq + (j ^ q)) for i in range(n_dp) for j in range(n_seq)]
            terms.append(lax.ppermute(small, ("dp", "seq"), perm) if p or q else small)
            if p == 0:
                nexts.append((me ^ q) == me + G)
    tail = pl.BlockSpec((G, behind, own), lambda s: (0, length // behind, 0))
    dx = pl.pallas_call(
        functools.partial(tail_kernel, n_seq // G),
        grid=(1,),
        in_specs=[pl.BlockSpec(memory_space=pltpu.SMEM), pl.BlockSpec(gates.shape, lambda s: (0, 0, 0)), tail]
        + [pl.BlockSpec(small.shape, lambda s: (0, 0))] * len(terms),
        out_specs=tail,
        out_shape=jax.ShapeDtypeStruct(dx.shape, bf16),
        input_output_aliases={2: 0},
        name="tails",
    )(jnp.stack(nexts).astype(f32), gates, dx, *terms)
    dx, o = lax.optimization_barrier((dx, o))
    dx = swap(dx)
    output = pl.pallas_call(
        functools.partial(reads_kernel, G, per_key * DK),
        out_shape=jax.ShapeDtypeStruct((length, heads * DK), bf16),
        cost_estimate=pl.CostEstimate(flops=0, bytes_accessed=3 << 20, transcendentals=0),
        name="outputs",
    )(o)
    dx, output = lax.optimization_barrier((dx, output))
    d_rows, d_weight, d_decay, d_beta = pl.pallas_call(
        functools.partial(unpack_kernel, G, per_key),
        in_specs=[pl.BlockSpec(memory_space=pltpu.SMEM)] + [pl.BlockSpec(memory_space=pltpu.VMEM)] * 2,
        out_shape=[
            jax.ShapeDtypeStruct((length, channels), bf16),
            jax.ShapeDtypeStruct((4, channels), f32),
            jax.ShapeDtypeStruct((heads, length), f32),
            jax.ShapeDtypeStruct((heads, length), f32),
        ],
        compiler_params=pltpu.CompilerParams(vmem_limit_bytes=VMEM),
        name="unpack",
    )((member == G - 1).astype(f32)[None], o, dx)
    return (output[None], d_rows[None], d_weight, d_decay[None], d_beta[None])


def solution(mesh):
    in_specs = (
        P("dp", "seq", None),
        P(),
        P("dp", None, "seq"),
        P("dp", None, "seq"),
        P("dp", "seq"),
        P("dp", "seq", None),
    )
    out_specs = (
        P("dp", "seq", None),
        P("dp", "seq", None),
        P(),
        P("dp", None, "seq"),
        P("dp", None, "seq"),
    )
    return jax.shard_map(
        local, mesh=mesh, in_specs=in_specs, out_specs=out_specs, check_vma=False
    )
```

```python
import functools

import jax
import jax.numpy as jnp
from jax import lax
from jax.experimental import pallas as pl
from jax.experimental.pallas import tpu as pltpu
from jax.sharding import PartitionSpec as P

DK = 128
DOC_MOST = 1024
EPS = 1e-6
CODE = 16
COUNTS = (4, 4, 4, 4)
VMEM = 64 << 20
RIM = 16
f32 = jnp.float32
bf16 = jnp.bfloat16


def dg(a, b, ca, cb):
    return lax.dot_general(a, b, (((ca,), (cb,)), ((), ())), preferred_element_type=f32)


def split(x):
    hi = x.astype(bf16)
    return (hi, (x - hi.astype(f32)).astype(bf16))


def cat(parts, axis):
    return tuple(jnp.concatenate(leaves, axis) for leaves in zip(*parts))


def mm(a, b, ca, cb):
    out = dg(a[0], b[0], ca, cb)
    if len(b) > 1:
        out = out + dg(a[0], b[1], ca, cb)
    if len(a) > 1:
        out = out + dg(a[1], b[0], ca, cb)
    return out


def iota2(shape, dim):
    return lax.broadcasted_iota(jnp.int32, shape, dim)


def conv_inputs(x_ref, n, width, shift_ref, docs, rim=None):
    length, lane = docs.shape[0], 0
    to = slice(0, width)
    if rim is None:
        rim = x_ref[n, length : length + RIM, :width].astype(f32)[:3]
    shift_ref[5:8, to] = rim
    rows = x_ref[n, :length, lane : lane + width].astype(f32)
    shift_ref[8 : 8 + length, to] = rows
    at = iota2((length, DK), 0)
    first = docs[0:1, :]
    taps = [rows]
    for off in (1, 2, 3):
        earlier = jnp.where(at >= off, pltpu.roll(docs, off, 0), first)
        ok = earlier == docs
        moved = shift_ref[8 - off : 8 - off + length, to]
        taps.append(jnp.where(wide(ok, width), moved, 0.0))
    return taps


def query_rim(x_ref, n, length):
    return x_ref[n, length : length + RIM, DK : 2 * DK].astype(f32)[3:6]


def wide(x, width):
    return jnp.concatenate([x] * (width // DK), 1)


def conv_out(taps, w):
    return sum(w[3 - off : 4 - off, :] * taps[off] for off in range(4))


def conv_back(dz, taps, w, code, plain, dz_ref, doc_next, dw_ref, rim_ref):
    length, width = dz.shape
    dz_ref[8 + length :, :] = dz_ref[8:16, :]
    dz_ref[8 : 8 + length, :] = dz
    docs_after = doc_next[...]
    at = iota2((length, DK), 0)
    dx = w[3:4, :] * dz
    for off in (1, 2, 3):
        ahead = pltpu.roll(plain, length - off, 0)
        for r in range(off):
            ahead = jnp.where(at == length - off + r, docs_after[r : r + 1, :], ahead)
        moved = dz_ref[8 + off : 8 + off + length, :]
        dx = dx + w[3 - off : 4 - off, :] * jnp.where(wide(ahead == plain, width), moved, 0.0)
    doc_next[...] = plain[0:8, :]
    for off in range(4):
        dw_ref[3 - off : 4 - off, :] += jnp.sum(dz * taps[off], 0, keepdims=True)
    head = jnp.where(wide(code[0:8, :] == code[0:1, :], width), dz[0:8, :], 0.0)
    held = wide(code[0:1, :], width)
    for r in range(3):
        total = 0.0
        for off in range(3 - r, 4):
            total = total + w[3 - off : 4 - off, :] * head[r + off - 3 : r + off - 2, :]
        rim_ref[r : r + 1, :] = jnp.where(held >= CODE * (3 - r), total, 0.0)
    return dx


def unit(x):
    inv = lax.rsqrt(jnp.sum(x * x, -1, keepdims=True) + EPS)
    return x * inv, inv


def unit_back(grad, hat, inv):
    return inv * (grad - hat * jnp.sum(grad * hat, -1, keepdims=True))


def sigmoid(z):
    return 1.0 / (1.0 + jnp.exp(-z))


class Meta:
    def __init__(self, numbers, per_key):
        length = numbers.shape[1]
        rows = numbers.astype(f32)
        row_at = iota2((RIM, DK), 0)
        i, j = iota2((length, length), 0), iota2((length, length), 1)
        self.lower, self.strict = i >= j, i > j

        def column(first, count):
            pick = ((row_at >= first) & (row_at < first + count)).astype(f32).astype(bf16)
            return dg(numbers, pick, 0, 0)

        self.code = column(3, 1)
        self.plain = self.code - CODE * jnp.floor(self.code * (1.0 / CODE))
        code_row = rows[3:4]
        self.same = (self.code == code_row) & self.lower
        carry = (self.code >= CODE) & (self.code == code_row[:, 0:1])
        ending = self.code == code_row[:, length - 1 : length]
        until = (i <= j).astype(f32).astype(bf16)
        row_sums = dg(numbers, until, 1, 0)
        ones = jnp.ones((length, DK), bf16)
        self.c_row, self.c_col, self.beta, self.beta_row = [], [], [], []
        self.entry, self.tail, self.keep, self.both = [], [], [], []
        for h in range(per_key):
            at = 4 + 3 * h
            self.c_row.append(row_sums[at : at + 1] + row_sums[at + 1 : at + 2] + row_sums[at + 2 : at + 3])
            c_col = 0.0
            for part in (2, 1, 0):
                c_col = c_col + dg(jnp.where(self.lower, rows[at + part : at + part + 1], 0.0).astype(bf16), ones, 1, 0)
            self.c_col.append(c_col)
            at = 4 + 3 * per_key + 3 * h
            self.beta.append(column(at, 3))
            self.beta_row.append(rows[at : at + 1] + rows[at + 1 : at + 2] + rows[at + 2 : at + 3])
            self.entry.append(jnp.where(carry, jnp.exp(c_col), 0.0))
            last = self.c_row[h][:, length - 1 : length]
            self.tail.append(jnp.where(ending, jnp.exp(jnp.minimum(last - c_col, 0.0)), 0.0))
            self.keep.append(self.entry[h][length - 1 : length, :])
            self.both.append(self.beta[h] * self.entry[h])

    def fading(self, h):
        gap = jnp.minimum(self.c_col[h] - self.c_row[h], 0.0)
        return jnp.where(self.same, jnp.exp(gap), 0.0)


def inverse(mats):
    length = mats[0].shape[0]
    i, j = iota2((length, length), 0), iota2((length, length), 1)
    eye = (i == j).astype(f32)
    inner = [jnp.where((i // 8) == (j // 8), n, 0.0) for n in mats]
    s1 = [split(n) for n in inner]
    s2 = [split(mm(a, a, 1, 0)) for a in s1]
    low = [eye - n + (a[0].astype(f32) + a[1].astype(f32)) - mm(b, a, 1, 0) for n, a, b in zip(inner, s2, s1)]
    s4 = [split(mm(a, a, 1, 0)) for a in s2]
    inv = [t + mm(split(t), a, 1, 0) for t, a in zip(low, s4)]
    width = 8
    while width < length:
        cross = ((i // (2 * width)) == (j // (2 * width))) & ((i // width) > (j // width))
        st = [split(t) for t in inv]
        half = [mm(split(jnp.where(cross, n, 0.0)), t, 1, 0) for n, t in zip(mats, st)]
        inv = [t - mm(s, split(x), 1, 0) for t, s, x in zip(inv, st, half)]
        width *= 2
    return inv


def rows_from(xs):
    wide_x = split(jnp.concatenate(xs, 1))
    shape = (len(xs) * DK, DK)
    pick = ((iota2(shape, 0) // DK) == iota2(shape, 1)).astype(f32).astype(bf16)
    return mm(wide_x, (pick,), 1, 0).T


def key_kernel(per_key, count, x_ref, w_ref, k_ref, t_ref, w_out, u_ref, a_ref, m_ref, s_ref, end_ref, chain, shift_ref):
    step = pl.program_id(0)
    length = k_ref.shape[1]
    own = w_ref.shape[1]
    eye = (iota2((DK, DK), 0) == iota2((DK, DK), 1)).astype(f32)

    @pl.when(step == 0)
    def _():
        for h in range(per_key):
            chain[h] = jnp.concatenate([eye, jnp.zeros((DK, DK), f32)], 1)

    w = w_ref[...]
    pairs = [(n, h) for n in range(count) for h in range(per_key)]
    metas, ks, vs = [], [], []
    for n in range(count):
        meta = Meta(x_ref[n, length:, :DK], per_key)
        z = conv_out(conv_inputs(x_ref, n, own, shift_ref.at[n], meta.code), w)
        act = z * sigmoid(z)
        k, _ = unit(act[:, :DK])
        k_ref[n] = k
        metas.append(meta)
        ks.append(k)
        vs.append(act[:, DK:])
    sk = [split(k) for k in ks]
    kk = [mm(s, s, 1, 1) for s in sk]
    ns = [
        jnp.where(metas[n].strict, metas[n].beta[h] * kk[n] * metas[n].fading(h), 0.0) for n, h in pairs
    ]
    ts = inverse(ns)
    rhs = [
        jnp.concatenate([metas[n].both[h] * ks[n], metas[n].beta[h] * vs[n][:, h * DK : (h + 1) * DK]], 1)
        for n, h in pairs
    ]
    wu = [mm(split(t), split(r), 1, 0) for t, r in zip(ts, rhs)]
    kwu = [mm(split(metas[n].tail[h] * ks[n]), split(x), 0, 0) for (n, h), x in zip(pairs, wu)]
    for m, (n, h) in enumerate(pairs):
        t_ref[n, h], w_out[n, h], u_ref[n, h] = ts[m], wu[m][:, :DK], wu[m][:, DK:]
        a = metas[n].keep[h] * eye - kwu[m][:, :DK]
        a_ref[n, h] = a
        now = chain[h]
        m_ref[n, h], s_ref[n, h] = now[:, :DK], now[:, DK:]
        later = mm(split(a), split(now), 1, 0)
        chain[h] = jnp.concatenate([later[:, :DK], later[:, DK:] + kwu[m][:, DK:]], 1)
    for h in range(per_key):
        end_ref[h] = chain[h, :, DK:]


def query_kernel(per_key, count, x_ref, y_ref, w_ref, k_ref, t_ref, a_ref, e_ref, m_ref, g_ref, start_ref, chain, shift_ref):
    step = pl.program_id(0)
    length = k_ref.shape[1]
    eye = (iota2((DK, DK), 0) == iota2((DK, DK), 1)).astype(f32)

    @pl.when(step == 0)
    def _():
        for h in range(per_key):
            chain[h] = jnp.concatenate([eye, jnp.zeros((DK, DK), f32)], 1)

    w = w_ref[...]
    pairs = [(n, h) for n in reversed(range(count)) for h in range(per_key)]
    metas, sq, sk, qk = {}, {}, {}, {}
    for n in range(count):
        metas[n] = Meta(x_ref[n, length:, :DK], per_key)
        z = conv_out(conv_inputs(y_ref, n, DK, shift_ref.at[n], metas[n].code, query_rim(x_ref, n, length)), w)
        q, _ = unit(z * sigmoid(z))
        sq[n], sk[n] = split(q * DK**-0.5), split(k_ref[n])
        qk[n] = mm(sq[n], sk[n], 1, 1)
    dos = [(y_ref[n, :length, (h + 1) * DK : (h + 2) * DK],) for n, h in pairs]
    rs = [mm(split(qk[n] * metas[n].fading(h)), d, 0, 0) for (n, h), d in zip(pairs, dos)]
    es = [mm(split(t_ref[n, h]), split(r), 0, 0) for (n, h), r in zip(pairs, rs)]
    gs = []
    for at in range(0, len(pairs), per_key):
        n = pairs[at][0]
        asked = jnp.concatenate([metas[n].entry[h] * dos[at + h][0].astype(f32) for h in range(per_key)], 1)
        undone = jnp.concatenate([-metas[n].both[h] * es[at + h] for h in range(per_key)], 1)
        b = mm(cat([sq[n], sk[n]], 0), cat([split(asked), split(undone)], 0), 0, 0)
        gs += [b[:, h * DK : (h + 1) * DK] for h in range(per_key)]
    for m, (n, h) in enumerate(pairs):
        e_ref[n, h] = es[m]
        now = chain[h]
        m_ref[n, h], g_ref[n, h] = now[:, :DK], now[:, DK:]
        later = mm(split(a_ref[n, h]), split(now), 0, 0)
        chain[h] = jnp.concatenate([later[:, :DK], later[:, DK:] + gs[m]], 1)
    for h in range(per_key):
        start_ref[h] = chain[h, :, DK:]


def read_kernel(per_key, count, in_ref, x_ref, y_ref, w_ref, k_ref, w_in, u_ref, m_ref, sl_ref, out_ref, d_ref, s_ref,
                dk_ref, dc_ref, rim_ref, dw_ref, shift_ref, dz_ref, doc_next):
    length = k_ref.shape[1]

    @pl.when(pl.program_id(0) == 0)
    def _():
        dw_ref[...] = jnp.zeros_like(dw_ref)
        dz_ref[...] = jnp.zeros_like(dz_ref)
        doc_next[...] = jnp.zeros_like(doc_next)

    w = w_ref[...]
    s_in = [split(in_ref[h]) for h in range(per_key)]
    pairs = [(n, h) for n in reversed(range(count)) for h in range(per_key)]
    metas, taps, sig, zs, hats, inv, qs, sq, sk, qk = {}, {}, {}, {}, {}, {}, {}, {}, {}, {}
    for n in range(count):
        metas[n] = Meta(x_ref[n, length:, :DK], per_key)
        taps[n] = conv_inputs(y_ref, n, DK, shift_ref.at[n], metas[n].code, query_rim(x_ref, n, length))
        zs[n] = conv_out(taps[n], w)
        sig[n] = sigmoid(zs[n])
        hats[n], inv[n] = unit(zs[n] * sig[n])
        qs[n] = hats[n] * DK**-0.5
        sq[n], sk[n] = split(qs[n]), split(k_ref[n])
        qk[n] = mm(sq[n], sk[n], 1, 1)
    states = [sl_ref[n, h] + mm(split(m_ref[n, h]), s_in[h], 1, 0) for n, h in pairs]
    ss = [split(s) for s in states]
    fs = [metas[n].fading(h) for n, h in pairs]
    ds = [u_ref[n, h] - mm(split(w_in[n, h]), s, 1, 0) for (n, h), s in zip(pairs, ss)]
    sd = [split(d) for d in ds]
    qss = {n: mm(sq[n], cat([ss[m] for m in range(len(pairs)) if pairs[m][0] == n], 1), 1, 0) for n in range(count)}
    outs = [
        metas[n].entry[h] * qss[n][:, h * DK : (h + 1) * DK] + mm(split(qk[n] * f), d, 1, 0)
        for (n, h), f, d in zip(pairs, fs, sd)
    ]
    dos = [(y_ref[n, :length, (h + 1) * DK : (h + 2) * DK],) for n, h in pairs]
    back = [mm(do, cat([d, s], 0), 1, 1) for do, d, s in zip(dos, sd, ss)]
    dps = [x[:, :length] * f for x, f in zip(back, fs)]
    enters = [metas[n].entry[h] * x[:, length:] for (n, h), x in zip(pairs, back)]
    dq, dk = {}, {}
    for n in range(count):
        mine = [m for m in range(len(pairs)) if pairs[m][0] == n]
        s_dp = split(sum(dps[m] for m in mine))
        dq[n] = mm(s_dp, sk[n], 1, 0) + sum(enters[m] for m in mine)
        dk[n] = mm(s_dp, sq[n], 0, 0)
        gaps = [dps[m] * qk[n] for m in mine]
        sums = rows_from([g + enters[m] * qs[n] for g, m in zip(gaps, mine)])
        for h, m in enumerate(mine):
            s_ref[n, h], d_ref[n, h] = states[m], ds[m]
            out_ref[n, :, (h + 1) * DK : (h + 2) * DK] = outs[m].astype(bf16)
            dc_ref[n, h : h + 1, :] = sums[h : h + 1] - jnp.sum(gaps[h], 0, keepdims=True)
    for n in reversed(range(count)):
        dk_ref[n] = dk[n]
        grad = unit_back(DK**-0.5 * dq[n], hats[n], inv[n])
        dz = grad * (sig[n] + zs[n] * sig[n] * (1.0 - sig[n]))
        dx = conv_back(dz, taps[n], w, metas[n].code, metas[n].plain, dz_ref, doc_next, dw_ref, rim_ref)
        out_ref[n, :, :DK] = dx.astype(bf16)


def write_kernel(per_key, count, in_ref, x_ref, w_ref, k_ref, t_ref, e_ref, m_ref, gl_ref, d_ref, s_ref, dk_ref, dc_ref,
                 dwq_ref, rimq_ref, dx_ref, gates_ref, small_ref, shift_ref, dz_ref, doc_next, dw_ref, rim_ref):
    step, steps = pl.program_id(0), pl.num_programs(0)
    length = k_ref.shape[1]
    own = w_ref.shape[1]

    @pl.when(step == 0)
    def _():
        dw_ref[...] = jnp.zeros_like(dw_ref)
        dz_ref[...] = jnp.zeros_like(dz_ref)
        doc_next[...] = jnp.zeros_like(doc_next)

    w = w_ref[...]
    i, j = iota2((length, length), 0), iota2((length, length), 1)
    from_here = (i >= j).astype(f32).astype(bf16)
    g_in = [split(in_ref[h]) for h in range(per_key)]
    pairs = [(n, h) for n in reversed(range(count)) for h in range(per_key)]
    metas, taps, sig, zs, hats, inv, vs, sk, kk = {}, {}, {}, {}, {}, {}, {}, {}, {}
    for n in range(count):
        metas[n] = Meta(x_ref[n, length:, :DK], per_key)
        taps[n] = conv_inputs(x_ref, n, own, shift_ref.at[n], metas[n].code)
        zs[n] = conv_out(taps[n], w)
        sig[n] = sigmoid(zs[n])
        act = zs[n] * sig[n]
        hats[n], inv[n] = unit(act[:, :DK])
        vs[n] = act[:, DK:]
        sk[n] = split(k_ref[n])
        kk[n] = mm(sk[n], sk[n], 1, 1)
    later = [gl_ref[n, h] + mm(split(m_ref[n, h]), g_in[h], 1, 0) for n, h in pairs]
    s_later = [split(x) for x in later]
    s_d = [split(d_ref[n, h]) for n, h in pairs]
    s_s = [split(s_ref[n, h]) for n, h in pairs]
    kg = {n: mm(sk[n], cat([s_later[m] for m in range(len(pairs)) if pairs[m][0] == n], 1), 1, 0) for n in range(count)}
    x1 = [metas[n].tail[h] * kg[n][:, h * DK : (h + 1) * DK] for n, h in pairs]
    es = [e_ref[n, h] + mm(split(t_ref[n, h]), split(x), 0, 0) for (n, h), x in zip(pairs, x1)]
    se = [split(e) for e in es]
    ends = [metas[n].tail[h] * mm(d, s, 1, 1) for (n, h), d, s in zip(pairs, s_d, s_later)]
    back = [mm(e, cat([d, s], 0), 1, 1) for e, d, s in zip(se, s_d, s_s)]
    ess = [x[:, length:] for x in back]
    dkk = [
        jnp.where(metas[n].strict, x[:, :length] * (-metas[n].beta[h] * metas[n].fading(h)), 0.0)
        for (n, h), x in zip(pairs, back)
    ]
    dk, dv, rows = {}, {}, {}
    for n in range(count):
        mine = [m for m in range(len(pairs)) if pairs[m][0] == n]
        meta, k = metas[n], k_ref[n]
        s_dkk = split(sum(dkk[m] for m in mine))
        bes = [meta.both[h] * ess[m] for h, m in enumerate(mine)]
        dk[n] = dk_ref[n] + mm(s_dkk, sk[n], 1, 0) + mm(s_dkk, sk[n], 0, 0) + sum(ends[m] - b for b, m in zip(bes, mine))
        nn = [dkk[m] * kk[n] for m in mine]
        ek = [ends[m] * k for m in mine]
        mats = [x - b * k - y for x, b, y in zip(nn, bes, ek)] + nn
        mats += [
            es[m] * vs[n][:, h * DK : (h + 1) * DK] - meta.entry[h] * ess[m] * k for h, m in enumerate(mine)
        ]
        sums = rows_from(mats)
        dc = [
            dc_ref[n, h : h + 1, :] + sums[h : h + 1] - jnp.sum(nn[h], 0, keepdims=True) for h in range(per_key)
        ]
        dc = jnp.concatenate(dc + [jnp.zeros((8 - per_key, length), f32)], 0)
        decays = mm(split(dc), (from_here,), 1, 0)
        for h, m in enumerate(mine):
            dv[n, h] = meta.beta[h] * es[m]
            last = jnp.sum(ek[h] + later[m] * s_ref[n, h] * meta.keep[h], 0, keepdims=True)
            rows[n, h] = decays[h : h + 1] + jnp.sum(last, 1, keepdims=True)
            rows[n, per_key + h] = (
                sums[2 * per_key + h : 2 * per_key + h + 1] + sums[per_key + h : per_key + h + 1] / meta.beta_row[h]
            )
    for n in reversed(range(count)):
        dk_act = unit_back(dk[n], hats[n], inv[n])
        d_act = jnp.concatenate([dk_act] + [dv[n, h] for h in range(per_key)], 1)
        dz = d_act * (sig[n] + zs[n] * sig[n] * (1.0 - sig[n]))
        dx = conv_back(dz, taps[n], w, metas[n].code, metas[n].plain, dz_ref, doc_next, dw_ref, rim_ref)
        dx_ref[n] = dx.astype(bf16)
        gates_ref[n] = jnp.concatenate([rows[n, m] for m in range(2 * per_key)], 0)

    @pl.when(step == steps - 1)
    def _():
        small_ref[0:4, :DK], small_ref[0:4, DK:] = dwq_ref[...], dw_ref[...]
        small_ref[4:7, :DK], small_ref[4:7, DK:] = rimq_ref[...], rim_ref[...]
        small_ref[7:8, :] = jnp.zeros((1, small_ref.shape[1]), f32)


def places(G, per_key):
    starts = [lambda m: m * DK, lambda m: (G + m) * DK]
    starts += [lambda m, h=h: (2 * G + m * per_key + h) * DK for h in range(per_key)]
    return starts


def tail_kernel(groups, next_ref, gates_ref, *refs):
    refs, out_ref = refs[:-1], refs[-1]
    taps = [ref[0:4, :] for ref in refs]
    while len(taps) > 1:
        taps = [i + j for i, j in zip(taps[::2], taps[1::2])]
    rims = sum(next_ref[q] * refs[q][4:7, :] for q in range(groups))
    parts = range(refs[0].shape[1] // DK)
    shared = [taps[0][:, m * DK : (m + 1) * DK] for m in parts] + [rims[:, m * DK : (m + 1) * DK] for m in parts]
    for m in range(out_ref.shape[0]):
        x = jnp.concatenate([gates_ref[m]] + shared, 0)
        hi = x.astype(bf16)
        mid = (x - hi.astype(f32)).astype(bf16)
        low = (x - hi.astype(f32) - mid.astype(f32)).astype(bf16)
        out_ref[m] = jnp.concatenate([hi, mid, low], 1)


def reads_kernel(G, width, o_ref, out_ref):
    for m in range(G):
        out_ref[:, m * width : (m + 1) * width] = o_ref[m, :, DK:]


def unpack_kernel(G, per_key, o_ref, dx_ref, rows_ref):
    for m in range(G):
        for part, start in enumerate(places(G, per_key)):
            ref, lane = (o_ref, 0) if part == 0 else (dx_ref, (part - 1) * DK)
            rows_ref[:, start(m) : start(m) + DK] = ref[m, :, lane : lane + DK]


def final_kernel(G, per_key, last_ref, tail_ref, rows_in, rows_ref, dw_ref, decay_ref, beta_ref):
    gates, taps = 2 * per_key, 4 * (2 + per_key)
    for m in range(G):
        x = tail_ref[m].astype(f32)
        x = x[:, :DK] + (x[:, DK : 2 * DK] + x[:, 2 * DK : 3 * DK])
        decay_ref[m * per_key : (m + 1) * per_key, :] = x[:per_key]
        beta_ref[m * per_key : (m + 1) * per_key, :] = x[per_key:gates]
        for part, start in enumerate(places(G, per_key)):
            to = slice(start(m), start(m) + DK)
            rim = x[gates + taps + 3 * part : gates + taps + 3 * part + 3] * last_ref[0]
            rim = jnp.concatenate([jnp.zeros((RIM - 3, DK), f32), rim], 0)
            rows_ref[:, to] = (rows_in[:, to].astype(f32) + rim).astype(bf16)
            dw_ref[:, to] = x[gates + 4 * part : gates + 4 * part + 4]


def three(x):
    hi = lax.reduce_precision(x, 8, 7)
    mid = lax.reduce_precision(x - hi, 8, 7)
    return jnp.stack([hi, mid, x - hi - mid], -2).astype(bf16)


def local(mixed, conv_weight, log_decay, beta, doc_ids, out_grad):
    n_seq, n_dp = lax.axis_size("seq"), lax.axis_size("dp")
    rows, docs, og = mixed[0], doc_ids[0], out_grad[0]
    length, channels = rows.shape
    heads = log_decay.shape[1]
    key_heads = (channels - heads * DK) // (2 * DK)
    per_key = heads // key_heads
    G = key_heads
    assert n_seq % G == 0 and G * length >= DOC_MOST
    member = lax.axis_index("seq") % G
    team = [list(range(s, s + G)) for s in range(0, n_seq, G)]
    own = DK + per_key * DK

    def shifted(x, by):
        return lax.ppermute(x, "seq", [(s, s + by) for s in range(n_seq) if 0 <= s + by < n_seq])

    def by_member(x):
        return jnp.moveaxis(x.reshape(x.shape[:-1] + (G, -1)), -2, 0)

    def of_members(x):
        return jnp.moveaxis(x, 0, -2).reshape(x.shape[1:-1] + (-1,))

    def keys_values(x):
        return jnp.concatenate([by_member(x[..., G * DK : 2 * G * DK]), by_member(x[..., 2 * G * DK :])], -1)

    def swap(x):
        return lax.all_to_all(x, "seq", 0, 0, axis_index_groups=team)

    marks = jnp.broadcast_to((docs[-3:] + 1).astype(bf16)[:, None], (3, DK)).reshape(-1)
    marks = jnp.pad(marks, (0, channels - 3 * DK))
    first = jnp.broadcast_to((docs[:1] + 1).astype(bf16), (DK,))
    rim = shifted(jnp.concatenate([rows[-3:], marks[None]], 0), 1)
    held = rim[3, : 3 * DK].reshape(3, DK) == first
    rim_rows = jnp.where(held[:, None], rim[:3].reshape(3, -1, DK), 0).reshape(3, channels)
    code = (docs + 1).reshape(-1, DK) + CODE * (held[0].astype(jnp.int32) + held[1] + held[2])
    code = code.reshape(length).astype(bf16)
    numbers = jnp.concatenate(
        [
            jnp.broadcast_to(code, (G, 1, length)),
            three(log_decay[0].reshape(G, per_key, length)).reshape(G, -1, length),
            three(beta[0].reshape(G, per_key, length)).reshape(G, -1, length),
        ],
        1,
    )
    rim_q = jnp.pad(by_member(rim_rows[:, : G * DK]), ((0, 0), (0, RIM - 6), (0, own - 2 * DK)))
    x = swap(
        jnp.concatenate(
            [keys_values(rows), keys_values(rim_rows), jnp.concatenate([numbers, rim_q], 2)], 1
        )
    )
    y = jnp.concatenate([by_member(rows[:, : G * DK]), by_member(og)], 2)
    taps = conv_weight.astype(f32)
    w_q, w_k, w_v = [
        lax.dynamic_index_in_dim(by_member(part), member, 0, keepdims=False)
        for part in (taps[:, : G * DK], taps[:, G * DK : 2 * G * DK], taps[:, 2 * G * DK :])
    ]
    w_kv = jnp.concatenate([w_k, w_v], 1)
    me = lax.axis_index("seq")
    nexts = jnp.stack([(me ^ q) == me + G for q in range(0, n_seq, G)]).astype(f32)
    last = (member == G - 1).astype(f32)[None]
    y, x, w_q, w_kv, nexts, last = lax.optimization_barrier((y, x, w_q, w_kv, nexts, last))
    y = swap(y)

    pair = (per_key, DK, DK)
    block = (length, DK)

    def call(kernel, count, name, back, fulls, ins, out_shapes, out_fulls, scratch, flops, behind=0):
        steps = G // count
        out_fulls = [s if isinstance(s[0], tuple) else (s, f32) for s in out_fulls]
        order = (lambda s: steps - 1 - s) if back else (lambda s: s)

        def spec(shape):
            return pl.BlockSpec((count,) + shape, lambda s: (order(s),) + (0,) * len(shape))

        def full(shape):
            return pl.BlockSpec(shape, lambda s: (0,) * len(shape))

        in_specs = [full(a.shape) if m in fulls else spec(a.shape[1:]) for m, a in enumerate(ins)]
        return pl.pallas_call(
            functools.partial(kernel, per_key, count),
            grid=(steps,),
            in_specs=in_specs,
            out_specs=[spec(s) for s, _ in out_shapes] + [full(s) for s, _ in out_fulls],
            out_shape=[
                jax.ShapeDtypeStruct((G, s[0] + (0 if m else behind)) + s[1:], t) for m, (s, t) in enumerate(out_shapes)
            ]
            + [jax.ShapeDtypeStruct(s, t) for s, t in out_fulls],
            scratch_shapes=scratch(count),
            compiler_params=pltpu.CompilerParams(vmem_limit_bytes=VMEM),
            cost_estimate=pl.CostEstimate(flops=flops, bytes_accessed=8 << 20, transcendentals=0),
            name=name,
        )(*ins)

    def conv_scratch(width):
        return lambda count: [
            pltpu.VMEM((count, 8 + length, width), f32),
            pltpu.VMEM((16 + length, width), f32),
            pltpu.VMEM((8, DK), f32),
        ]

    def chain_scratch(width):
        return lambda count: [pltpu.VMEM((per_key, DK, 2 * DK), f32), pltpu.VMEM((count, 8 + length, width), f32)]

    k, t, w_out, u, a, m_fwd, s_local, end = call(
        key_kernel, COUNTS[0], "keys", False, (1,), (x, w_kv), [(block, f32)] + [(pair, f32)] * 6, [pair],
        chain_scratch(own), 15 * 10**9,
    )
    state_in = shifted(end, G)
    e, m_bwd, g_local, start = call(
        query_kernel, COUNTS[1], "queries", True, (2,), (x, y, w_q, k, t, a), [(pair, f32)] * 3, [pair],
        chain_scratch(DK), 8 * 10**9,
    )
    back_in = shifted(start, -G)
    o, d, s, dk, dc, rim_q, dw_q = call(
        read_kernel, COUNTS[2], "reads", True, (0, 3), (state_in, x, y, w_q, k, w_out, u, m_fwd, s_local),
        [((length, own), bf16), (pair, f32), (pair, f32), (block, f32), ((per_key, length), f32)],
        [(3, DK), (4, DK)], conv_scratch(DK), 8 * 10**9,
    )
    o = swap(o)
    behind = 2 * per_key + 7 * (2 + per_key)
    assert behind == 2 * RIM
    dx, gates, small = call(
        write_kernel, COUNTS[3], "writes", True, (0, 2, 12, 13),
        (back_in, x, w_kv, k, t, e, m_bwd, g_local, d, s, dk, dc, dw_q, rim_q),
        [((length, own), bf16), ((2 * per_key, length), f32)], [(8, DK + own)],
        lambda count: conv_scratch(own)(count) + [pltpu.VMEM((4, own), f32), pltpu.VMEM((3, own), f32)],
        15 * 10**9,
    )
    terms = []
    for p in range(n_dp):
        for q in range(0, n_seq, G):
            perm = [(i * n_seq + j, (i ^ p) * n_seq + (j ^ q)) for i in range(n_dp) for j in range(n_seq)]
            terms.append(lax.ppermute(small, ("dp", "seq"), perm) if p or q else small)
    tails = pl.pallas_call(
        functools.partial(tail_kernel, n_seq // G),
        in_specs=[pl.BlockSpec(memory_space=pltpu.SMEM)] + [pl.BlockSpec(memory_space=pltpu.VMEM)] * (1 + len(terms)),
        out_shape=jax.ShapeDtypeStruct((G, behind, own), bf16),
        name="tails",
    )(nexts, gates, *terms)
    dx, o = lax.optimization_barrier((dx, o))
    dx = swap(dx)
    output = pl.pallas_call(
        functools.partial(reads_kernel, G, per_key * DK),
        out_shape=jax.ShapeDtypeStruct((length, heads * DK), bf16),
        cost_estimate=pl.CostEstimate(flops=0, bytes_accessed=3 << 20, transcendentals=0),
        name="outputs",
    )(o)
    dx, tails = lax.optimization_barrier((dx, tails))
    tails = swap(tails)
    d_rows = pl.pallas_call(
        functools.partial(unpack_kernel, G, per_key),
        out_shape=jax.ShapeDtypeStruct((length, channels), bf16),
        compiler_params=pltpu.CompilerParams(vmem_limit_bytes=VMEM),
        name="unpack",
    )(o, dx)
    d_rows, tails, output = lax.optimization_barrier((d_rows, tails, output))
    last_rows = pl.BlockSpec((RIM, channels), lambda s: (length // RIM - 1, 0))
    d_rows, d_weight, d_decay, d_beta = pl.pallas_call(
        functools.partial(final_kernel, G, per_key),
        grid=(1,),
        in_specs=[
            pl.BlockSpec(memory_space=pltpu.SMEM),
            pl.BlockSpec(tails.shape, lambda s: (0, 0, 0)),
            last_rows,
        ],
        out_specs=[last_rows]
        + [pl.BlockSpec(shape, lambda s: (0, 0)) for shape in ((4, channels), (heads, length), (heads, length))],
        out_shape=[
            jax.ShapeDtypeStruct((length, channels), bf16),
            jax.ShapeDtypeStruct((4, channels), f32),
            jax.ShapeDtypeStruct((heads, length), f32),
            jax.ShapeDtypeStruct((heads, length), f32),
        ],
        input_output_aliases={2: 0},
        name="totals",
    )(last, tails, d_rows)
    return (output[None], d_rows[None], d_weight, d_decay[None], d_beta[None])


def solution(mesh):
    in_specs = (
        P("dp", "seq", None),
        P(),
        P("dp", None, "seq"),
        P("dp", None, "seq"),
        P("dp", "seq"),
        P("dp", "seq", None),
    )
    out_specs = (
        P("dp", "seq", None),
        P("dp", "seq", None),
        P(),
        P("dp", None, "seq"),
        P("dp", None, "seq"),
    )
    return jax.shard_map(
        local, mesh=mesh, in_specs=in_specs, out_specs=out_specs, check_vma=False
    )
```

```python
import functools

import jax
import jax.numpy as jnp
from jax import lax
from jax.experimental import pallas as pl
from jax.experimental.pallas import tpu as pltpu
from jax.sharding import PartitionSpec as P

DK = 128
DOC_MOST = 1024
EPS = 1e-6
CODE = 16
COUNTS = (4, 4, 4, 4)
VMEM = 64 << 20
RIM = 16
f32 = jnp.float32
bf16 = jnp.bfloat16


def dg(a, b, ca, cb):
    return lax.dot_general(a, b, (((ca,), (cb,)), ((), ())), preferred_element_type=f32)


def split(x):
    hi = x.astype(bf16)
    return (hi, (x - hi.astype(f32)).astype(bf16))


def cat(parts, axis):
    return tuple(jnp.concatenate(leaves, axis) for leaves in zip(*parts))


def mm(a, b, ca, cb):
    out = dg(a[0], b[0], ca, cb)
    if len(b) > 1:
        out = out + dg(a[0], b[1], ca, cb)
    if len(a) > 1:
        out = out + dg(a[1], b[0], ca, cb)
    return out


def joined(a, b, ca, cb):
    if len(a) > 1 and len(b) > 1:
        left, right = (a[0], a[0], a[1]), (b[0], b[1], b[0])
    elif len(a) > 1:
        left, right = a, b * 2
    else:
        left, right = a * len(b), b
    return dg(jnp.concatenate(left, ca), jnp.concatenate(right, cb), ca, cb)


def iota2(shape, dim):
    return lax.broadcasted_iota(jnp.int32, shape, dim)


def conv_inputs(x_ref, n, width, shift_ref, docs, rim=None):
    length, lane = docs.shape[0], 0
    to = slice(0, width)
    if rim is None:
        rim = x_ref[n, length : length + RIM, :width].astype(f32)[:3]
    shift_ref[5:8, to] = rim
    rows = x_ref[n, :length, lane : lane + width].astype(f32)
    shift_ref[8 : 8 + length, to] = rows
    at = iota2((length, DK), 0)
    first = docs[0:1, :]
    taps = [rows]
    for off in (1, 2, 3):
        earlier = jnp.where(at >= off, pltpu.roll(docs, off, 0), first)
        ok = earlier == docs
        moved = shift_ref[8 - off : 8 - off + length, to]
        taps.append(jnp.where(wide(ok, width), moved, 0.0))
    return taps


def query_rim(x_ref, n, length):
    return x_ref[n, length : length + RIM, DK : 2 * DK].astype(f32)[3:6]


def wide(x, width):
    return jnp.concatenate([x] * (width // DK), 1)


def conv_out(taps, w):
    return sum(w[3 - off : 4 - off, :] * taps[off] for off in range(4))


def conv_back(dz, taps, w, code, plain, dz_ref, doc_next, dw_ref, rim_ref):
    length, width = dz.shape
    dz_ref[8 + length :, :] = dz_ref[8:16, :]
    dz_ref[8 : 8 + length, :] = dz
    docs_after = doc_next[...]
    at = iota2((length, DK), 0)
    dx = w[3:4, :] * dz
    for off in (1, 2, 3):
        ahead = pltpu.roll(plain, length - off, 0)
        for r in range(off):
            ahead = jnp.where(at == length - off + r, docs_after[r : r + 1, :], ahead)
        moved = dz_ref[8 + off : 8 + off + length, :]
        dx = dx + w[3 - off : 4 - off, :] * jnp.where(wide(ahead == plain, width), moved, 0.0)
    doc_next[...] = plain[0:8, :]
    for off in range(4):
        dw_ref[3 - off : 4 - off, :] += jnp.sum(dz * taps[off], 0, keepdims=True)
    head = jnp.where(wide(code[0:8, :] == code[0:1, :], width), dz[0:8, :], 0.0)
    held = wide(code[0:1, :], width)
    for r in range(3):
        total = 0.0
        for off in range(3 - r, 4):
            total = total + w[3 - off : 4 - off, :] * head[r + off - 3 : r + off - 2, :]
        rim_ref[r : r + 1, :] = jnp.where(held >= CODE * (3 - r), total, 0.0)
    return dx


def unit(x):
    inv = lax.rsqrt(jnp.sum(x * x, -1, keepdims=True) + EPS)
    return x * inv, inv


def unit_back(grad, hat, inv):
    return inv * (grad - hat * jnp.sum(grad * hat, -1, keepdims=True))


def sigmoid(z):
    return 1.0 / (1.0 + jnp.exp(-z))


class Meta:
    def __init__(self, numbers, per_key):
        length = numbers.shape[1]
        rows = numbers.astype(f32)
        row_at = iota2((RIM, DK), 0)
        i, j = iota2((length, length), 0), iota2((length, length), 1)
        self.lower, self.strict = i >= j, i > j

        def column(first, count):
            pick = ((row_at >= first) & (row_at < first + count)).astype(f32).astype(bf16)
            return dg(numbers, pick, 0, 0)

        self.code = column(3, 1)
        self.plain = self.code - CODE * jnp.floor(self.code * (1.0 / CODE))
        code_row = rows[3:4]
        self.same = (self.code == code_row) & self.lower
        carry = (self.code >= CODE) & (self.code == code_row[:, 0:1])
        ending = self.code == code_row[:, length - 1 : length]
        until = (i <= j).astype(f32).astype(bf16)
        row_sums = dg(numbers, until, 1, 0)
        ones = jnp.ones((length, DK), bf16)
        self.c_row, self.c_col, self.beta, self.beta_row = [], [], [], []
        self.entry, self.tail, self.keep, self.both = [], [], [], []
        for h in range(per_key):
            at = 4 + 3 * h
            self.c_row.append(row_sums[at : at + 1] + row_sums[at + 1 : at + 2] + row_sums[at + 2 : at + 3])
            c_col = 0.0
            for part in (2, 1, 0):
                c_col = c_col + dg(jnp.where(self.lower, rows[at + part : at + part + 1], 0.0).astype(bf16), ones, 1, 0)
            self.c_col.append(c_col)
            at = 4 + 3 * per_key + 3 * h
            self.beta.append(column(at, 3))
            self.beta_row.append(rows[at : at + 1] + rows[at + 1 : at + 2] + rows[at + 2 : at + 3])
            self.entry.append(jnp.where(carry, jnp.exp(c_col), 0.0))
            last = self.c_row[h][:, length - 1 : length]
            self.tail.append(jnp.where(ending, jnp.exp(jnp.minimum(last - c_col, 0.0)), 0.0))
            self.keep.append(self.entry[h][length - 1 : length, :])
            self.both.append(self.beta[h] * self.entry[h])

    def fading(self, h):
        gap = jnp.minimum(self.c_col[h] - self.c_row[h], 0.0)
        return jnp.where(self.same, jnp.exp(gap), 0.0)


def inverse(mats):
    length = mats[0].shape[0]
    i, j = iota2((length, length), 0), iota2((length, length), 1)
    eye = (i == j).astype(f32)
    inner = [jnp.where((i // 8) == (j // 8), n, 0.0) for n in mats]
    s1 = [split(n) for n in inner]
    s2 = [split(joined(a, a, 1, 0)) for a in s1]
    low = [eye - n + (a[0].astype(f32) + a[1].astype(f32)) - joined(b, a, 1, 0) for n, a, b in zip(inner, s2, s1)]
    s4 = [split(joined(a, a, 1, 0)) for a in s2]
    inv = [t + joined(split(t), a, 1, 0) for t, a in zip(low, s4)]
    width = 8
    while width < length:
        cross = ((i // (2 * width)) == (j // (2 * width))) & ((i // width) > (j // width))
        st = [split(t) for t in inv]
        half = [joined(split(jnp.where(cross, n, 0.0)), t, 1, 0) for n, t in zip(mats, st)]
        inv = [t - joined(s, split(x), 1, 0) for t, s, x in zip(inv, st, half)]
        width *= 2
    return inv


def rows_from(xs):
    wide_x = split(jnp.concatenate(xs, 1))
    shape = (len(xs) * DK, DK)
    pick = ((iota2(shape, 0) // DK) == iota2(shape, 1)).astype(f32).astype(bf16)
    return mm(wide_x, (pick,), 1, 0).T


def key_kernel(per_key, count, x_ref, w_ref, k_ref, t_ref, w_out, u_ref, a_ref, m_ref, s_ref, end_ref, chain, shift_ref):
    step = pl.program_id(0)
    length = k_ref.shape[1]
    own = w_ref.shape[1]
    eye = (iota2((DK, DK), 0) == iota2((DK, DK), 1)).astype(f32)

    @pl.when(step == 0)
    def _():
        for h in range(per_key):
            chain[h] = jnp.concatenate([eye, jnp.zeros((DK, DK), f32)], 1)

    w = w_ref[...]
    pairs = [(n, h) for n in range(count) for h in range(per_key)]
    metas, ks, vs = [], [], []
    for n in range(count):
        meta = Meta(x_ref[n, length:, :DK], per_key)
        z = conv_out(conv_inputs(x_ref, n, own, shift_ref.at[n], meta.code), w)
        act = z * sigmoid(z)
        k, _ = unit(act[:, :DK])
        k_ref[n] = k
        metas.append(meta)
        ks.append(k)
        vs.append(act[:, DK:])
    sk = [split(k) for k in ks]
    kk = [joined(s, s, 1, 1) for s in sk]
    ns = [
        jnp.where(metas[n].strict, metas[n].beta[h] * kk[n] * metas[n].fading(h), 0.0) for n, h in pairs
    ]
    ts = inverse(ns)
    rhs = [
        jnp.concatenate([metas[n].both[h] * ks[n], metas[n].beta[h] * vs[n][:, h * DK : (h + 1) * DK]], 1)
        for n, h in pairs
    ]
    wu = [joined(split(t), split(r), 1, 0) for t, r in zip(ts, rhs)]
    kwu = [joined(split(metas[n].tail[h] * ks[n]), split(x), 0, 0) for (n, h), x in zip(pairs, wu)]
    for m, (n, h) in enumerate(pairs):
        t_ref[n, h], w_out[n, h], u_ref[n, h] = ts[m], wu[m][:, :DK], wu[m][:, DK:]
        a = metas[n].keep[h] * eye - kwu[m][:, :DK]
        a_ref[n, h] = a
        now = chain[h]
        m_ref[n, h], s_ref[n, h] = now[:, :DK], now[:, DK:]
        later = joined(split(a), split(now), 1, 0)
        chain[h] = jnp.concatenate([later[:, :DK], later[:, DK:] + kwu[m][:, DK:]], 1)
    for h in range(per_key):
        end_ref[h] = chain[h, :, DK:]


def query_kernel(per_key, count, x_ref, y_ref, w_ref, k_ref, t_ref, a_ref, e_ref, m_ref, g_ref, start_ref, chain, shift_ref):
    step = pl.program_id(0)
    length = k_ref.shape[1]
    eye = (iota2((DK, DK), 0) == iota2((DK, DK), 1)).astype(f32)

    @pl.when(step == 0)
    def _():
        for h in range(per_key):
            chain[h] = jnp.concatenate([eye, jnp.zeros((DK, DK), f32)], 1)

    w = w_ref[...]
    pairs = [(n, h) for n in reversed(range(count)) for h in range(per_key)]
    metas, sq, sk, qk = {}, {}, {}, {}
    for n in range(count):
        metas[n] = Meta(x_ref[n, length:, :DK], per_key)
        z = conv_out(conv_inputs(y_ref, n, DK, shift_ref.at[n], metas[n].code, query_rim(x_ref, n, length)), w)
        q, _ = unit(z * sigmoid(z))
        sq[n], sk[n] = split(q * DK**-0.5), split(k_ref[n])
        qk[n] = mm(sq[n], sk[n], 1, 1)
    dos = [(y_ref[n, :length, (h + 1) * DK : (h + 2) * DK],) for n, h in pairs]
    rs = [mm(split(qk[n] * metas[n].fading(h)), d, 0, 0) for (n, h), d in zip(pairs, dos)]
    es = [mm(split(t_ref[n, h]), split(r), 0, 0) for (n, h), r in zip(pairs, rs)]
    gs = []
    for at in range(0, len(pairs), per_key):
        n = pairs[at][0]
        asked = jnp.concatenate([metas[n].entry[h] * dos[at + h][0].astype(f32) for h in range(per_key)], 1)
        undone = jnp.concatenate([-metas[n].both[h] * es[at + h] for h in range(per_key)], 1)
        b = mm(cat([sq[n], sk[n]], 0), cat([split(asked), split(undone)], 0), 0, 0)
        gs += [b[:, h * DK : (h + 1) * DK] for h in range(per_key)]
    for m, (n, h) in enumerate(pairs):
        e_ref[n, h] = es[m]
        now = chain[h]
        m_ref[n, h], g_ref[n, h] = now[:, :DK], now[:, DK:]
        later = mm(split(a_ref[n, h]), split(now), 0, 0)
        chain[h] = jnp.concatenate([later[:, :DK], later[:, DK:] + gs[m]], 1)
    for h in range(per_key):
        start_ref[h] = chain[h, :, DK:]


def read_kernel(per_key, count, in_ref, x_ref, y_ref, w_ref, k_ref, w_in, u_ref, m_ref, sl_ref, out_ref, d_ref, s_ref,
                dk_ref, dc_ref, rim_ref, dw_ref, shift_ref, dz_ref, doc_next):
    length = k_ref.shape[1]

    @pl.when(pl.program_id(0) == 0)
    def _():
        dw_ref[...] = jnp.zeros_like(dw_ref)
        dz_ref[...] = jnp.zeros_like(dz_ref)
        doc_next[...] = jnp.zeros_like(doc_next)

    w = w_ref[...]
    s_in = [split(in_ref[h]) for h in range(per_key)]
    pairs = [(n, h) for n in reversed(range(count)) for h in range(per_key)]
    metas, taps, sig, zs, hats, inv, qs, sq, sk, qk = {}, {}, {}, {}, {}, {}, {}, {}, {}, {}
    for n in range(count):
        metas[n] = Meta(x_ref[n, length:, :DK], per_key)
        taps[n] = conv_inputs(y_ref, n, DK, shift_ref.at[n], metas[n].code, query_rim(x_ref, n, length))
        zs[n] = conv_out(taps[n], w)
        sig[n] = sigmoid(zs[n])
        hats[n], inv[n] = unit(zs[n] * sig[n])
        qs[n] = hats[n] * DK**-0.5
        sq[n], sk[n] = split(qs[n]), split(k_ref[n])
        qk[n] = mm(sq[n], sk[n], 1, 1)
    states = [sl_ref[n, h] + mm(split(m_ref[n, h]), s_in[h], 1, 0) for n, h in pairs]
    ss = [split(s) for s in states]
    fs = [metas[n].fading(h) for n, h in pairs]
    ds = [u_ref[n, h] - mm(split(w_in[n, h]), s, 1, 0) for (n, h), s in zip(pairs, ss)]
    sd = [split(d) for d in ds]
    qss = {n: mm(sq[n], cat([ss[m] for m in range(len(pairs)) if pairs[m][0] == n], 1), 1, 0) for n in range(count)}
    outs = [
        metas[n].entry[h] * qss[n][:, h * DK : (h + 1) * DK] + mm(split(qk[n] * f), d, 1, 0)
        for (n, h), f, d in zip(pairs, fs, sd)
    ]
    dos = [(y_ref[n, :length, (h + 1) * DK : (h + 2) * DK],) for n, h in pairs]
    back = [mm(do, cat([d, s], 0), 1, 1) for do, d, s in zip(dos, sd, ss)]
    dps = [x[:, :length] * f for x, f in zip(back, fs)]
    enters = [metas[n].entry[h] * x[:, length:] for (n, h), x in zip(pairs, back)]
    dq, dk = {}, {}
    for n in range(count):
        mine = [m for m in range(len(pairs)) if pairs[m][0] == n]
        s_dp = split(sum(dps[m] for m in mine))
        dq[n] = mm(s_dp, sk[n], 1, 0) + sum(enters[m] for m in mine)
        dk[n] = mm(s_dp, sq[n], 0, 0)
        gaps = [dps[m] * qk[n] for m in mine]
        sums = rows_from([g + enters[m] * qs[n] for g, m in zip(gaps, mine)])
        for h, m in enumerate(mine):
            s_ref[n, h], d_ref[n, h] = states[m], ds[m]
            out_ref[n, :, (h + 1) * DK : (h + 2) * DK] = outs[m].astype(bf16)
            dc_ref[n, h : h + 1, :] = sums[h : h + 1] - jnp.sum(gaps[h], 0, keepdims=True)
    for n in reversed(range(count)):
        dk_ref[n] = dk[n]
        grad = unit_back(DK**-0.5 * dq[n], hats[n], inv[n])
        dz = grad * (sig[n] + zs[n] * sig[n] * (1.0 - sig[n]))
        dx = conv_back(dz, taps[n], w, metas[n].code, metas[n].plain, dz_ref, doc_next, dw_ref, rim_ref)
        out_ref[n, :, :DK] = dx.astype(bf16)


def write_kernel(per_key, count, in_ref, x_ref, w_ref, k_ref, t_ref, e_ref, m_ref, gl_ref, d_ref, s_ref, dk_ref, dc_ref,
                 dwq_ref, rimq_ref, dx_ref, gates_ref, small_ref, shift_ref, dz_ref, doc_next, dw_ref, rim_ref):
    step, steps = pl.program_id(0), pl.num_programs(0)
    length = k_ref.shape[1]
    own = w_ref.shape[1]

    @pl.when(step == 0)
    def _():
        dw_ref[...] = jnp.zeros_like(dw_ref)
        dz_ref[...] = jnp.zeros_like(dz_ref)
        doc_next[...] = jnp.zeros_like(doc_next)

    w = w_ref[...]
    i, j = iota2((length, length), 0), iota2((length, length), 1)
    from_here = (i >= j).astype(f32).astype(bf16)
    g_in = [split(in_ref[h]) for h in range(per_key)]
    pairs = [(n, h) for n in reversed(range(count)) for h in range(per_key)]
    metas, taps, sig, zs, hats, inv, vs, sk, kk = {}, {}, {}, {}, {}, {}, {}, {}, {}
    for n in range(count):
        metas[n] = Meta(x_ref[n, length:, :DK], per_key)
        taps[n] = conv_inputs(x_ref, n, own, shift_ref.at[n], metas[n].code)
        zs[n] = conv_out(taps[n], w)
        sig[n] = sigmoid(zs[n])
        act = zs[n] * sig[n]
        hats[n], inv[n] = unit(act[:, :DK])
        vs[n] = act[:, DK:]
        sk[n] = split(k_ref[n])
        kk[n] = joined(sk[n], sk[n], 1, 1)
    later = [gl_ref[n, h] + joined(split(m_ref[n, h]), g_in[h], 1, 0) for n, h in pairs]
    s_later = [split(x) for x in later]
    s_d = [split(d_ref[n, h]) for n, h in pairs]
    s_s = [split(s_ref[n, h]) for n, h in pairs]
    kg = {n: joined(sk[n], cat([s_later[m] for m in range(len(pairs)) if pairs[m][0] == n], 1), 1, 0) for n in range(count)}
    x1 = [metas[n].tail[h] * kg[n][:, h * DK : (h + 1) * DK] for n, h in pairs]
    es = [e_ref[n, h] + joined(split(t_ref[n, h]), split(x), 0, 0) for (n, h), x in zip(pairs, x1)]
    se = [split(e) for e in es]
    ends = [metas[n].tail[h] * joined(d, s, 1, 1) for (n, h), d, s in zip(pairs, s_d, s_later)]
    back = [joined(e, cat([d, s], 0), 1, 1) for e, d, s in zip(se, s_d, s_s)]
    ess = [x[:, length:] for x in back]
    dkk = [
        jnp.where(metas[n].strict, x[:, :length] * (-metas[n].beta[h] * metas[n].fading(h)), 0.0)
        for (n, h), x in zip(pairs, back)
    ]
    dk, dv, rows = {}, {}, {}
    for n in range(count):
        mine = [m for m in range(len(pairs)) if pairs[m][0] == n]
        meta, k = metas[n], k_ref[n]
        s_dkk = split(sum(dkk[m] for m in mine))
        bes = [meta.both[h] * ess[m] for h, m in enumerate(mine)]
        dk[n] = dk_ref[n] + joined(s_dkk, sk[n], 1, 0) + joined(s_dkk, sk[n], 0, 0) + sum(ends[m] - b for b, m in zip(bes, mine))
        nn = [dkk[m] * kk[n] for m in mine]
        ek = [ends[m] * k for m in mine]
        mats = [x - b * k - y for x, b, y in zip(nn, bes, ek)] + nn
        mats += [
            es[m] * vs[n][:, h * DK : (h + 1) * DK] - meta.entry[h] * ess[m] * k for h, m in enumerate(mine)
        ]
        sums = rows_from(mats)
        dc = [
            dc_ref[n, h : h + 1, :] + sums[h : h + 1] - jnp.sum(nn[h], 0, keepdims=True) for h in range(per_key)
        ]
        dc = jnp.concatenate(dc + [jnp.zeros((8 - per_key, length), f32)], 0)
        decays = joined(split(dc), (from_here,), 1, 0)
        for h, m in enumerate(mine):
            dv[n, h] = meta.beta[h] * es[m]
            last = jnp.sum(ek[h] + later[m] * s_ref[n, h] * meta.keep[h], 0, keepdims=True)
            rows[n, h] = decays[h : h + 1] + jnp.sum(last, 1, keepdims=True)
            rows[n, per_key + h] = (
                sums[2 * per_key + h : 2 * per_key + h + 1] + sums[per_key + h : per_key + h + 1] / meta.beta_row[h]
            )
    for n in reversed(range(count)):
        dk_act = unit_back(dk[n], hats[n], inv[n])
        d_act = jnp.concatenate([dk_act] + [dv[n, h] for h in range(per_key)], 1)
        dz = d_act * (sig[n] + zs[n] * sig[n] * (1.0 - sig[n]))
        dx = conv_back(dz, taps[n], w, metas[n].code, metas[n].plain, dz_ref, doc_next, dw_ref, rim_ref)
        dx_ref[n] = dx.astype(bf16)
        gates_ref[n] = jnp.concatenate([rows[n, m] for m in range(2 * per_key)], 0)

    @pl.when(step == steps - 1)
    def _():
        small_ref[0:4, :DK], small_ref[0:4, DK:] = dwq_ref[...], dw_ref[...]
        small_ref[4:7, :DK], small_ref[4:7, DK:] = rimq_ref[...], rim_ref[...]
        small_ref[7:8, :] = jnp.zeros((1, small_ref.shape[1]), f32)


def places(G, per_key):
    starts = [lambda m: m * DK, lambda m: (G + m) * DK]
    starts += [lambda m, h=h: (2 * G + m * per_key + h) * DK for h in range(per_key)]
    return starts


def tail_kernel(groups, next_ref, gates_ref, *refs):
    refs, out_ref = refs[:-1], refs[-1]
    taps = [ref[0:4, :] for ref in refs]
    while len(taps) > 1:
        taps = [i + j for i, j in zip(taps[::2], taps[1::2])]
    rims = sum(next_ref[q] * refs[q][4:7, :] for q in range(groups))
    parts = range(refs[0].shape[1] // DK)
    shared = [taps[0][:, m * DK : (m + 1) * DK] for m in parts] + [rims[:, m * DK : (m + 1) * DK] for m in parts]
    for m in range(out_ref.shape[0]):
        x = jnp.concatenate([gates_ref[m]] + shared, 0)
        hi = x.astype(bf16)
        mid = (x - hi.astype(f32)).astype(bf16)
        low = (x - hi.astype(f32) - mid.astype(f32)).astype(bf16)
        out_ref[m] = jnp.concatenate([hi, mid, low], 1)


def reads_kernel(G, width, o_ref, out_ref):
    for m in range(G):
        out_ref[:, m * width : (m + 1) * width] = o_ref[m, :, DK:]


def unpack_kernel(G, per_key, o_ref, dx_ref, rows_ref):
    for m in range(G):
        for part, start in enumerate(places(G, per_key)):
            ref, lane = (o_ref, 0) if part == 0 else (dx_ref, (part - 1) * DK)
            rows_ref[:, start(m) : start(m) + DK] = ref[m, :, lane : lane + DK]


def final_kernel(G, per_key, last_ref, tail_ref, rows_in, rows_ref, dw_ref, decay_ref, beta_ref):
    gates, taps = 2 * per_key, 4 * (2 + per_key)
    for m in range(G):
        x = tail_ref[m].astype(f32)
        x = x[:, :DK] + (x[:, DK : 2 * DK] + x[:, 2 * DK : 3 * DK])
        decay_ref[m * per_key : (m + 1) * per_key, :] = x[:per_key]
        beta_ref[m * per_key : (m + 1) * per_key, :] = x[per_key:gates]
        for part, start in enumerate(places(G, per_key)):
            to = slice(start(m), start(m) + DK)
            rim = x[gates + taps + 3 * part : gates + taps + 3 * part + 3] * last_ref[0]
            rim = jnp.concatenate([jnp.zeros((RIM - 3, DK), f32), rim], 0)
            rows_ref[:, to] = (rows_in[:, to].astype(f32) + rim).astype(bf16)
            dw_ref[:, to] = x[gates + 4 * part : gates + 4 * part + 4]


def three(x):
    hi = lax.reduce_precision(x, 8, 7)
    mid = lax.reduce_precision(x - hi, 8, 7)
    return jnp.stack([hi, mid, x - hi - mid], -2).astype(bf16)


def local(mixed, conv_weight, log_decay, beta, doc_ids, out_grad):
    n_seq, n_dp = lax.axis_size("seq"), lax.axis_size("dp")
    rows, docs, og = mixed[0], doc_ids[0], out_grad[0]
    length, channels = rows.shape
    heads = log_decay.shape[1]
    key_heads = (channels - heads * DK) // (2 * DK)
    per_key = heads // key_heads
    G = key_heads
    assert n_seq % G == 0 and G * length >= DOC_MOST
    member = lax.axis_index("seq") % G
    team = [list(range(s, s + G)) for s in range(0, n_seq, G)]
    own = DK + per_key * DK

    def shifted(x, by):
        return lax.ppermute(x, "seq", [(s, s + by) for s in range(n_seq) if 0 <= s + by < n_seq])

    def by_member(x):
        return jnp.moveaxis(x.reshape(x.shape[:-1] + (G, -1)), -2, 0)

    def of_members(x):
        return jnp.moveaxis(x, 0, -2).reshape(x.shape[1:-1] + (-1,))

    def keys_values(x):
        return jnp.concatenate([by_member(x[..., G * DK : 2 * G * DK]), by_member(x[..., 2 * G * DK :])], -1)

    def swap(x):
        return lax.all_to_all(x, "seq", 0, 0, axis_index_groups=team)

    marks = jnp.broadcast_to((docs[-3:] + 1).astype(bf16)[:, None], (3, DK)).reshape(-1)
    marks = jnp.pad(marks, (0, channels - 3 * DK))
    first = jnp.broadcast_to((docs[:1] + 1).astype(bf16), (DK,))
    rim = shifted(jnp.concatenate([rows[-3:], marks[None]], 0), 1)
    held = rim[3, : 3 * DK].reshape(3, DK) == first
    rim_rows = jnp.where(held[:, None], rim[:3].reshape(3, -1, DK), 0).reshape(3, channels)
    code = (docs + 1).reshape(-1, DK) + CODE * (held[0].astype(jnp.int32) + held[1] + held[2])
    code = code.reshape(length).astype(bf16)
    numbers = jnp.concatenate(
        [
            jnp.broadcast_to(code, (G, 1, length)),
            three(log_decay[0].reshape(G, per_key, length)).reshape(G, -1, length),
            three(beta[0].reshape(G, per_key, length)).reshape(G, -1, length),
        ],
        1,
    )
    rim_q = jnp.pad(by_member(rim_rows[:, : G * DK]), ((0, 0), (0, RIM - 6), (0, own - 2 * DK)))
    x = swap(
        jnp.concatenate(
            [keys_values(rows), keys_values(rim_rows), jnp.concatenate([numbers, rim_q], 2)], 1
        )
    )
    y = jnp.concatenate([by_member(rows[:, : G * DK]), by_member(og)], 2)
    taps = conv_weight.astype(f32)
    w_q, w_k, w_v = [
        lax.dynamic_index_in_dim(by_member(part), member, 0, keepdims=False)
        for part in (taps[:, : G * DK], taps[:, G * DK : 2 * G * DK], taps[:, 2 * G * DK :])
    ]
    w_kv = jnp.concatenate([w_k, w_v], 1)
    me = lax.axis_index("seq")
    nexts = jnp.stack([(me ^ q) == me + G for q in range(0, n_seq, G)]).astype(f32)
    last = (member == G - 1).astype(f32)[None]
    y, x, w_q, w_kv, nexts, last = lax.optimization_barrier((y, x, w_q, w_kv, nexts, last))
    y = swap(y)

    pair = (per_key, DK, DK)
    block = (length, DK)

    def call(kernel, count, name, back, fulls, ins, out_shapes, out_fulls, scratch, flops, behind=0):
        steps = G // count
        out_fulls = [s if isinstance(s[0], tuple) else (s, f32) for s in out_fulls]
        order = (lambda s: steps - 1 - s) if back else (lambda s: s)

        def spec(shape):
            return pl.BlockSpec((count,) + shape, lambda s: (order(s),) + (0,) * len(shape))

        def full(shape):
            return pl.BlockSpec(shape, lambda s: (0,) * len(shape))

        in_specs = [full(a.shape) if m in fulls else spec(a.shape[1:]) for m, a in enumerate(ins)]
        return pl.pallas_call(
            functools.partial(kernel, per_key, count),
            grid=(steps,),
            in_specs=in_specs,
            out_specs=[spec(s) for s, _ in out_shapes] + [full(s) for s, _ in out_fulls],
            out_shape=[
                jax.ShapeDtypeStruct((G, s[0] + (0 if m else behind)) + s[1:], t) for m, (s, t) in enumerate(out_shapes)
            ]
            + [jax.ShapeDtypeStruct(s, t) for s, t in out_fulls],
            scratch_shapes=scratch(count),
            compiler_params=pltpu.CompilerParams(vmem_limit_bytes=VMEM),
            cost_estimate=pl.CostEstimate(flops=flops, bytes_accessed=8 << 20, transcendentals=0),
            name=name,
        )(*ins)

    def conv_scratch(width):
        return lambda count: [
            pltpu.VMEM((count, 8 + length, width), f32),
            pltpu.VMEM((16 + length, width), f32),
            pltpu.VMEM((8, DK), f32),
        ]

    def chain_scratch(width):
        return lambda count: [pltpu.VMEM((per_key, DK, 2 * DK), f32), pltpu.VMEM((count, 8 + length, width), f32)]

    k, t, w_out, u, a, m_fwd, s_local, end = call(
        key_kernel, COUNTS[0], "keys", False, (1,), (x, w_kv), [(block, f32)] + [(pair, f32)] * 6, [pair],
        chain_scratch(own), 15 * 10**9,
    )
    state_in = shifted(end, G)
    e, m_bwd, g_local, start = call(
        query_kernel, COUNTS[1], "queries", True, (2,), (x, y, w_q, k, t, a), [(pair, f32)] * 3, [pair],
        chain_scratch(DK), 8 * 10**9,
    )
    back_in = shifted(start, -G)
    o, d, s, dk, dc, rim_q, dw_q = call(
        read_kernel, COUNTS[2], "reads", True, (0, 3), (state_in, x, y, w_q, k, w_out, u, m_fwd, s_local),
        [((length, own), bf16), (pair, f32), (pair, f32), (block, f32), ((per_key, length), f32)],
        [(3, DK), (4, DK)], conv_scratch(DK), 8 * 10**9,
    )
    o = swap(o)
    behind = 2 * per_key + 7 * (2 + per_key)
    assert behind == 2 * RIM
    dx, gates, small = call(
        write_kernel, COUNTS[3], "writes", True, (0, 2, 12, 13),
        (back_in, x, w_kv, k, t, e, m_bwd, g_local, d, s, dk, dc, dw_q, rim_q),
        [((length, own), bf16), ((2 * per_key, length), f32)], [(8, DK + own)],
        lambda count: conv_scratch(own)(count) + [pltpu.VMEM((4, own), f32), pltpu.VMEM((3, own), f32)],
        15 * 10**9,
    )
    terms = []
    for p in range(n_dp):
        for q in range(0, n_seq, G):
            perm = [(i * n_seq + j, (i ^ p) * n_seq + (j ^ q)) for i in range(n_dp) for j in range(n_seq)]
            terms.append(lax.ppermute(small, ("dp", "seq"), perm) if p or q else small)
    tails = pl.pallas_call(
        functools.partial(tail_kernel, n_seq // G),
        in_specs=[pl.BlockSpec(memory_space=pltpu.SMEM)] + [pl.BlockSpec(memory_space=pltpu.VMEM)] * (1 + len(terms)),
        out_shape=jax.ShapeDtypeStruct((G, behind, own), bf16),
        name="tails",
    )(nexts, gates, *terms)
    dx, o = lax.optimization_barrier((dx, o))
    dx = swap(dx)
    output = pl.pallas_call(
        functools.partial(reads_kernel, G, per_key * DK),
        out_shape=jax.ShapeDtypeStruct((length, heads * DK), bf16),
        cost_estimate=pl.CostEstimate(flops=0, bytes_accessed=3 << 20, transcendentals=0),
        name="outputs",
    )(o)
    dx, tails = lax.optimization_barrier((dx, tails))
    tails = swap(tails)
    d_rows = pl.pallas_call(
        functools.partial(unpack_kernel, G, per_key),
        out_shape=jax.ShapeDtypeStruct((length, channels), bf16),
        compiler_params=pltpu.CompilerParams(vmem_limit_bytes=VMEM),
        name="unpack",
    )(o, dx)
    d_rows, tails, output = lax.optimization_barrier((d_rows, tails, output))
    last_rows = pl.BlockSpec((RIM, channels), lambda s: (length // RIM - 1, 0))
    d_rows, d_weight, d_decay, d_beta = pl.pallas_call(
        functools.partial(final_kernel, G, per_key),
        grid=(1,),
        in_specs=[
            pl.BlockSpec(memory_space=pltpu.SMEM),
            pl.BlockSpec(tails.shape, lambda s: (0, 0, 0)),
            last_rows,
        ],
        out_specs=[last_rows]
        + [pl.BlockSpec(shape, lambda s: (0, 0)) for shape in ((4, channels), (heads, length), (heads, length))],
        out_shape=[
            jax.ShapeDtypeStruct((length, channels), bf16),
            jax.ShapeDtypeStruct((4, channels), f32),
            jax.ShapeDtypeStruct((heads, length), f32),
            jax.ShapeDtypeStruct((heads, length), f32),
        ],
        input_output_aliases={2: 0},
        name="totals",
    )(last, tails, d_rows)
    return (output[None], d_rows[None], d_weight, d_decay[None], d_beta[None])


def solution(mesh):
    in_specs = (
        P("dp", "seq", None),
        P(),
        P("dp", None, "seq"),
        P("dp", None, "seq"),
        P("dp", "seq"),
        P("dp", "seq", None),
    )
    out_specs = (
        P("dp", "seq", None),
        P("dp", "seq", None),
        P(),
        P("dp", None, "seq"),
        P("dp", None, "seq"),
    )
    return jax.shard_map(
        local, mesh=mesh, in_specs=in_specs, out_specs=out_specs, check_vma=False
    )
```

```python
import functools

import jax
import jax.numpy as jnp
from jax import lax
from jax.experimental import pallas as pl
from jax.experimental.pallas import tpu as pltpu
from jax.sharding import PartitionSpec as P

DK = 128
DOC_MOST = 1024
EPS = 1e-6
CODE = 16
COUNTS = (4, 4, 4, 4)
VMEM = 64 << 20
RIM = 16
f32 = jnp.float32
bf16 = jnp.bfloat16


def dg(a, b, ca, cb):
    return lax.dot_general(a, b, (((ca,), (cb,)), ((), ())), preferred_element_type=f32)


def split(x):
    hi = x.astype(bf16)
    return (hi, (x - hi.astype(f32)).astype(bf16))


def cat(parts, axis):
    return tuple(jnp.concatenate(leaves, axis) for leaves in zip(*parts))


def mm(a, b, ca, cb):
    out = dg(a[0], b[0], ca, cb)
    if len(b) > 1:
        out = out + dg(a[0], b[1], ca, cb)
    if len(a) > 1:
        out = out + dg(a[1], b[0], ca, cb)
    return out


def joined(a, b, ca, cb):
    if len(a) > 1 and len(b) > 1:
        left, right = (a[0], a[0], a[1]), (b[0], b[1], b[0])
    elif len(a) > 1:
        left, right = a, b * 2
    else:
        left, right = a * len(b), b
    return dg(jnp.concatenate(left, ca), jnp.concatenate(right, cb), ca, cb)


def iota2(shape, dim):
    return lax.broadcasted_iota(jnp.int32, shape, dim)


def conv_inputs(x_ref, n, width, shift_ref, docs, rim=None):
    length, lane = docs.shape[0], 0
    to = slice(0, width)
    if rim is None:
        rim = x_ref[n, length : length + RIM, :width].astype(f32)[:3]
    shift_ref[5:8, to] = rim
    rows = x_ref[n, :length, lane : lane + width].astype(f32)
    shift_ref[8 : 8 + length, to] = rows
    at = iota2((length, DK), 0)
    first = docs[0:1, :]
    taps = [rows]
    for off in (1, 2, 3):
        earlier = jnp.where(at >= off, pltpu.roll(docs, off, 0), first)
        ok = earlier == docs
        moved = shift_ref[8 - off : 8 - off + length, to]
        taps.append(jnp.where(wide(ok, width), moved, 0.0))
    return taps


def query_rim(x_ref, n, length):
    return x_ref[n, length : length + RIM, DK : 2 * DK].astype(f32)[3:6]


def wide(x, width):
    return jnp.concatenate([x] * (width // DK), 1)


def conv_out(taps, w):
    return sum(w[3 - off : 4 - off, :] * taps[off] for off in range(4))


def conv_back(dz, taps, w, code, plain, dz_ref, doc_next, dw_ref, rim_ref):
    length, width = dz.shape
    dz_ref[8 + length :, :] = dz_ref[8:16, :]
    dz_ref[8 : 8 + length, :] = dz
    docs_after = doc_next[...]
    at = iota2((length, DK), 0)
    dx = w[3:4, :] * dz
    for off in (1, 2, 3):
        ahead = pltpu.roll(plain, length - off, 0)
        for r in range(off):
            ahead = jnp.where(at == length - off + r, docs_after[r : r + 1, :], ahead)
        moved = dz_ref[8 + off : 8 + off + length, :]
        dx = dx + w[3 - off : 4 - off, :] * jnp.where(wide(ahead == plain, width), moved, 0.0)
    doc_next[...] = plain[0:8, :]
    for off in range(4):
        dw_ref[3 - off : 4 - off, :] += jnp.sum(dz * taps[off], 0, keepdims=True)
    head = jnp.where(wide(code[0:8, :] == code[0:1, :], width), dz[0:8, :], 0.0)
    held = wide(code[0:1, :], width)
    for r in range(3):
        total = 0.0
        for off in range(3 - r, 4):
            total = total + w[3 - off : 4 - off, :] * head[r + off - 3 : r + off - 2, :]
        rim_ref[r : r + 1, :] = jnp.where(held >= CODE * (3 - r), total, 0.0)
    return dx


def unit(x):
    inv = lax.rsqrt(jnp.sum(x * x, -1, keepdims=True) + EPS)
    return x * inv, inv


def unit_back(grad, hat, inv):
    return inv * (grad - hat * jnp.sum(grad * hat, -1, keepdims=True))


def sigmoid(z):
    return 1.0 / (1.0 + jnp.exp(-z))


class Meta:
    def __init__(self, numbers, per_key):
        length = numbers.shape[1]
        rows = numbers.astype(f32)
        row_at = iota2((RIM, DK), 0)
        i, j = iota2((length, length), 0), iota2((length, length), 1)
        self.lower, self.strict = i >= j, i > j

        def column(first, count):
            pick = ((row_at >= first) & (row_at < first + count)).astype(f32).astype(bf16)
            return dg(numbers, pick, 0, 0)

        self.code = column(3, 1)
        self.plain = self.code - CODE * jnp.floor(self.code * (1.0 / CODE))
        code_row = rows[3:4]
        self.same = (self.code == code_row) & self.lower
        carry = (self.code >= CODE) & (self.code == code_row[:, 0:1])
        ending = self.code == code_row[:, length - 1 : length]
        until = (i <= j).astype(f32).astype(bf16)
        row_sums = dg(numbers, until, 1, 0)
        ones = jnp.ones((length, DK), bf16)
        self.c_row, self.c_col, self.beta, self.beta_row = [], [], [], []
        self.entry, self.tail, self.keep, self.both = [], [], [], []
        for h in range(per_key):
            at = 4 + 3 * h
            self.c_row.append(row_sums[at : at + 1] + row_sums[at + 1 : at + 2] + row_sums[at + 2 : at + 3])
            c_col = 0.0
            for part in (2, 1, 0):
                c_col = c_col + dg(jnp.where(self.lower, rows[at + part : at + part + 1], 0.0).astype(bf16), ones, 1, 0)
            self.c_col.append(c_col)
            at = 4 + 3 * per_key + 3 * h
            self.beta.append(column(at, 3))
            self.beta_row.append(rows[at : at + 1] + rows[at + 1 : at + 2] + rows[at + 2 : at + 3])
            self.entry.append(jnp.where(carry, jnp.exp(c_col), 0.0))
            last = self.c_row[h][:, length - 1 : length]
            self.tail.append(jnp.where(ending, jnp.exp(jnp.minimum(last - c_col, 0.0)), 0.0))
            self.keep.append(self.entry[h][length - 1 : length, :])
            self.both.append(self.beta[h] * self.entry[h])

    def fading(self, h):
        gap = jnp.minimum(self.c_col[h] - self.c_row[h], 0.0)
        return jnp.where(self.same, jnp.exp(gap), 0.0)


def inverse(mats):
    length = mats[0].shape[0]
    i, j = iota2((length, length), 0), iota2((length, length), 1)
    eye = (i == j).astype(f32)
    inner = [jnp.where((i // 8) == (j // 8), n, 0.0) for n in mats]
    s1 = [split(n) for n in inner]
    s2 = [split(joined(a, a, 1, 0)) for a in s1]
    low = [eye - n + (a[0].astype(f32) + a[1].astype(f32)) - joined(b, a, 1, 0) for n, a, b in zip(inner, s2, s1)]
    s4 = [split(joined(a, a, 1, 0)) for a in s2]
    inv = [t + joined(split(t), a, 1, 0) for t, a in zip(low, s4)]
    width = 8
    while width < min(16, length):
        cross = ((i // (2 * width)) == (j // (2 * width))) & ((i // width) > (j // width))
        st = [split(t) for t in inv]
        half = [joined(split(jnp.where(cross, n, 0.0)), t, 1, 0) for n, t in zip(mats, st)]
        inv = [t - joined(s, split(x), 1, 0) for t, s, x in zip(inv, st, half)]
        width *= 2
    while width < length:
        starts = range(width, length, 2 * width)

        def seconds(x):
            return jnp.concatenate([x[at : at + width] for at in starts], 0)

        def back(x):
            gap = jnp.zeros((width, length), x.dtype)
            return jnp.concatenate([y for m in range(len(starts)) for y in (gap, x[m * width : (m + 1) * width])], 0)

        shape = (length // 2, length)
        cross = (iota2(shape, 1) // width) == 2 * (iota2(shape, 0) // width)
        st = [split(t) for t in inv]
        half = [joined(split(jnp.where(cross, seconds(n), 0.0)), t, 1, 0) for n, t in zip(mats, st)]
        half = [tuple(back(leaf) for leaf in split(x)) for x in half]
        inv = [t - back(joined(tuple(seconds(leaf) for leaf in s), x, 1, 0)) for t, s, x in zip(inv, st, half)]
        width *= 2
    return inv


def rows_from(xs):
    wide_x = split(jnp.concatenate(xs, 1))
    shape = (len(xs) * DK, DK)
    pick = ((iota2(shape, 0) // DK) == iota2(shape, 1)).astype(f32).astype(bf16)
    return mm(wide_x, (pick,), 1, 0).T


def key_kernel(per_key, count, x_ref, w_ref, k_ref, t_ref, w_out, u_ref, a_ref, m_ref, s_ref, end_ref, chain, shift_ref):
    step = pl.program_id(0)
    length = k_ref.shape[1]
    own = w_ref.shape[1]
    eye = (iota2((DK, DK), 0) == iota2((DK, DK), 1)).astype(f32)

    @pl.when(step == 0)
    def _():
        for h in range(per_key):
            chain[h] = jnp.concatenate([eye, jnp.zeros((DK, DK), f32)], 1)

    w = w_ref[...]
    pairs = [(n, h) for n in range(count) for h in range(per_key)]
    metas, ks, vs = [], [], []
    for n in range(count):
        meta = Meta(x_ref[n, length:, :DK], per_key)
        z = conv_out(conv_inputs(x_ref, n, own, shift_ref.at[n], meta.code), w)
        act = z * sigmoid(z)
        k, _ = unit(act[:, :DK])
        k_ref[n] = k
        metas.append(meta)
        ks.append(k)
        vs.append(act[:, DK:])
    sk = [split(k) for k in ks]
    kk = [joined(s, s, 1, 1) for s in sk]
    ns = [
        jnp.where(metas[n].strict, metas[n].beta[h] * kk[n] * metas[n].fading(h), 0.0) for n, h in pairs
    ]
    ts = inverse(ns)
    rhs = [
        jnp.concatenate([metas[n].both[h] * ks[n], metas[n].beta[h] * vs[n][:, h * DK : (h + 1) * DK]], 1)
        for n, h in pairs
    ]
    wu = [joined(split(t), split(r), 1, 0) for t, r in zip(ts, rhs)]
    kwu = [joined(split(metas[n].tail[h] * ks[n]), split(x), 0, 0) for (n, h), x in zip(pairs, wu)]
    for m, (n, h) in enumerate(pairs):
        t_ref[n, h], w_out[n, h], u_ref[n, h] = ts[m], wu[m][:, :DK], wu[m][:, DK:]
        a = metas[n].keep[h] * eye - kwu[m][:, :DK]
        a_ref[n, h] = a
        now = chain[h]
        m_ref[n, h], s_ref[n, h] = now[:, :DK], now[:, DK:]
        later = joined(split(a), split(now), 1, 0)
        chain[h] = jnp.concatenate([later[:, :DK], later[:, DK:] + kwu[m][:, DK:]], 1)
    for h in range(per_key):
        end_ref[h] = chain[h, :, DK:]


def query_kernel(per_key, count, x_ref, y_ref, w_ref, k_ref, t_ref, a_ref, e_ref, m_ref, g_ref, start_ref, chain, shift_ref):
    step = pl.program_id(0)
    length = k_ref.shape[1]
    eye = (iota2((DK, DK), 0) == iota2((DK, DK), 1)).astype(f32)

    @pl.when(step == 0)
    def _():
        for h in range(per_key):
            chain[h] = jnp.concatenate([eye, jnp.zeros((DK, DK), f32)], 1)

    w = w_ref[...]
    pairs = [(n, h) for n in reversed(range(count)) for h in range(per_key)]
    metas, sq, sk, qk = {}, {}, {}, {}
    for n in range(count):
        metas[n] = Meta(x_ref[n, length:, :DK], per_key)
        z = conv_out(conv_inputs(y_ref, n, DK, shift_ref.at[n], metas[n].code, query_rim(x_ref, n, length)), w)
        q, _ = unit(z * sigmoid(z))
        sq[n], sk[n] = split(q * DK**-0.5), split(k_ref[n])
        qk[n] = mm(sq[n], sk[n], 1, 1)
    dos = [(y_ref[n, :length, (h + 1) * DK : (h + 2) * DK],) for n, h in pairs]
    rs = [mm(split(qk[n] * metas[n].fading(h)), d, 0, 0) for (n, h), d in zip(pairs, dos)]
    es = [mm(split(t_ref[n, h]), split(r), 0, 0) for (n, h), r in zip(pairs, rs)]
    gs = []
    for at in range(0, len(pairs), per_key):
        n = pairs[at][0]
        asked = jnp.concatenate([metas[n].entry[h] * dos[at + h][0].astype(f32) for h in range(per_key)], 1)
        undone = jnp.concatenate([-metas[n].both[h] * es[at + h] for h in range(per_key)], 1)
        b = mm(cat([sq[n], sk[n]], 0), cat([split(asked), split(undone)], 0), 0, 0)
        gs += [b[:, h * DK : (h + 1) * DK] for h in range(per_key)]
    for m, (n, h) in enumerate(pairs):
        e_ref[n, h] = es[m]
        now = chain[h]
        m_ref[n, h], g_ref[n, h] = now[:, :DK], now[:, DK:]
        later = mm(split(a_ref[n, h]), split(now), 0, 0)
        chain[h] = jnp.concatenate([later[:, :DK], later[:, DK:] + gs[m]], 1)
    for h in range(per_key):
        start_ref[h] = chain[h, :, DK:]


def read_kernel(per_key, count, in_ref, x_ref, y_ref, w_ref, k_ref, w_in, u_ref, m_ref, sl_ref, out_ref, d_ref, s_ref,
                dk_ref, dc_ref, rim_ref, dw_ref, shift_ref, dz_ref, doc_next):
    length = k_ref.shape[1]

    @pl.when(pl.program_id(0) == 0)
    def _():
        dw_ref[...] = jnp.zeros_like(dw_ref)
        dz_ref[...] = jnp.zeros_like(dz_ref)
        doc_next[...] = jnp.zeros_like(doc_next)

    w = w_ref[...]
    s_in = [split(in_ref[h]) for h in range(per_key)]
    pairs = [(n, h) for n in reversed(range(count)) for h in range(per_key)]
    metas, taps, sig, zs, hats, inv, qs, sq, sk, qk = {}, {}, {}, {}, {}, {}, {}, {}, {}, {}
    for n in range(count):
        metas[n] = Meta(x_ref[n, length:, :DK], per_key)
        taps[n] = conv_inputs(y_ref, n, DK, shift_ref.at[n], metas[n].code, query_rim(x_ref, n, length))
        zs[n] = conv_out(taps[n], w)
        sig[n] = sigmoid(zs[n])
        hats[n], inv[n] = unit(zs[n] * sig[n])
        qs[n] = hats[n] * DK**-0.5
        sq[n], sk[n] = split(qs[n]), split(k_ref[n])
        qk[n] = mm(sq[n], sk[n], 1, 1)
    states = [sl_ref[n, h] + mm(split(m_ref[n, h]), s_in[h], 1, 0) for n, h in pairs]
    ss = [split(s) for s in states]
    fs = [metas[n].fading(h) for n, h in pairs]
    ds = [u_ref[n, h] - mm(split(w_in[n, h]), s, 1, 0) for (n, h), s in zip(pairs, ss)]
    sd = [split(d) for d in ds]
    qss = {n: mm(sq[n], cat([ss[m] for m in range(len(pairs)) if pairs[m][0] == n], 1), 1, 0) for n in range(count)}
    outs = [
        metas[n].entry[h] * qss[n][:, h * DK : (h + 1) * DK] + mm(split(qk[n] * f), d, 1, 0)
        for (n, h), f, d in zip(pairs, fs, sd)
    ]
    dos = [(y_ref[n, :length, (h + 1) * DK : (h + 2) * DK],) for n, h in pairs]
    back = [mm(do, cat([d, s], 0), 1, 1) for do, d, s in zip(dos, sd, ss)]
    dps = [x[:, :length] * f for x, f in zip(back, fs)]
    enters = [metas[n].entry[h] * x[:, length:] for (n, h), x in zip(pairs, back)]
    dq, dk = {}, {}
    for n in range(count):
        mine = [m for m in range(len(pairs)) if pairs[m][0] == n]
        s_dp = split(sum(dps[m] for m in mine))
        dq[n] = mm(s_dp, sk[n], 1, 0) + sum(enters[m] for m in mine)
        dk[n] = mm(s_dp, sq[n], 0, 0)
        gaps = [dps[m] * qk[n] for m in mine]
        sums = rows_from([g + enters[m] * qs[n] for g, m in zip(gaps, mine)])
        for h, m in enumerate(mine):
            s_ref[n, h], d_ref[n, h] = states[m], ds[m]
            out_ref[n, :, (h + 1) * DK : (h + 2) * DK] = outs[m].astype(bf16)
            dc_ref[n, h : h + 1, :] = sums[h : h + 1] - jnp.sum(gaps[h], 0, keepdims=True)
    for n in reversed(range(count)):
        dk_ref[n] = dk[n]
        grad = unit_back(DK**-0.5 * dq[n], hats[n], inv[n])
        dz = grad * (sig[n] + zs[n] * sig[n] * (1.0 - sig[n]))
        dx = conv_back(dz, taps[n], w, metas[n].code, metas[n].plain, dz_ref, doc_next, dw_ref, rim_ref)
        out_ref[n, :, :DK] = dx.astype(bf16)


def write_kernel(per_key, count, in_ref, x_ref, w_ref, k_ref, t_ref, e_ref, m_ref, gl_ref, d_ref, s_ref, dk_ref, dc_ref,
                 dwq_ref, rimq_ref, dx_ref, gates_ref, small_ref, shift_ref, dz_ref, doc_next, dw_ref, rim_ref):
    step, steps = pl.program_id(0), pl.num_programs(0)
    length = k_ref.shape[1]
    own = w_ref.shape[1]

    @pl.when(step == 0)
    def _():
        dw_ref[...] = jnp.zeros_like(dw_ref)
        dz_ref[...] = jnp.zeros_like(dz_ref)
        doc_next[...] = jnp.zeros_like(doc_next)

    w = w_ref[...]
    i, j = iota2((length, length), 0), iota2((length, length), 1)
    from_here = (i >= j).astype(f32).astype(bf16)
    g_in = [split(in_ref[h]) for h in range(per_key)]
    pairs = [(n, h) for n in reversed(range(count)) for h in range(per_key)]
    metas, taps, sig, zs, hats, inv, vs, sk, kk = {}, {}, {}, {}, {}, {}, {}, {}, {}
    for n in range(count):
        metas[n] = Meta(x_ref[n, length:, :DK], per_key)
        taps[n] = conv_inputs(x_ref, n, own, shift_ref.at[n], metas[n].code)
        zs[n] = conv_out(taps[n], w)
        sig[n] = sigmoid(zs[n])
        act = zs[n] * sig[n]
        hats[n], inv[n] = unit(act[:, :DK])
        vs[n] = act[:, DK:]
        sk[n] = split(k_ref[n])
        kk[n] = joined(sk[n], sk[n], 1, 1)
    later = [gl_ref[n, h] + joined(split(m_ref[n, h]), g_in[h], 1, 0) for n, h in pairs]
    s_later = [split(x) for x in later]
    s_d = [split(d_ref[n, h]) for n, h in pairs]
    s_s = [split(s_ref[n, h]) for n, h in pairs]
    kg = {n: joined(sk[n], cat([s_later[m] for m in range(len(pairs)) if pairs[m][0] == n], 1), 1, 0) for n in range(count)}
    x1 = [metas[n].tail[h] * kg[n][:, h * DK : (h + 1) * DK] for n, h in pairs]
    es = [e_ref[n, h] + joined(split(t_ref[n, h]), split(x), 0, 0) for (n, h), x in zip(pairs, x1)]
    se = [split(e) for e in es]
    ends = [metas[n].tail[h] * joined(d, s, 1, 1) for (n, h), d, s in zip(pairs, s_d, s_later)]
    back = [joined(e, cat([d, s], 0), 1, 1) for e, d, s in zip(se, s_d, s_s)]
    ess = [x[:, length:] for x in back]
    dkk = [
        jnp.where(metas[n].strict, x[:, :length] * (-metas[n].beta[h] * metas[n].fading(h)), 0.0)
        for (n, h), x in zip(pairs, back)
    ]
    dk, dv, rows = {}, {}, {}
    for n in range(count):
        mine = [m for m in range(len(pairs)) if pairs[m][0] == n]
        meta, k = metas[n], k_ref[n]
        s_dkk = split(sum(dkk[m] for m in mine))
        bes = [meta.both[h] * ess[m] for h, m in enumerate(mine)]
        dk[n] = dk_ref[n] + joined(s_dkk, sk[n], 1, 0) + joined(s_dkk, sk[n], 0, 0) + sum(ends[m] - b for b, m in zip(bes, mine))
        nn = [dkk[m] * kk[n] for m in mine]
        ek = [ends[m] * k for m in mine]
        mats = [x - b * k - y for x, b, y in zip(nn, bes, ek)] + nn
        mats += [
            es[m] * vs[n][:, h * DK : (h + 1) * DK] - meta.entry[h] * ess[m] * k for h, m in enumerate(mine)
        ]
        sums = rows_from(mats)
        dc = [
            dc_ref[n, h : h + 1, :] + sums[h : h + 1] - jnp.sum(nn[h], 0, keepdims=True) for h in range(per_key)
        ]
        dc = jnp.concatenate(dc + [jnp.zeros((8 - per_key, length), f32)], 0)
        decays = joined(split(dc), (from_here,), 1, 0)
        for h, m in enumerate(mine):
            dv[n, h] = meta.beta[h] * es[m]
            last = jnp.sum(ek[h] + later[m] * s_ref[n, h] * meta.keep[h], 0, keepdims=True)
            rows[n, h] = decays[h : h + 1] + jnp.sum(last, 1, keepdims=True)
            rows[n, per_key + h] = (
                sums[2 * per_key + h : 2 * per_key + h + 1] + sums[per_key + h : per_key + h + 1] / meta.beta_row[h]
            )
    for n in reversed(range(count)):
        dk_act = unit_back(dk[n], hats[n], inv[n])
        d_act = jnp.concatenate([dk_act] + [dv[n, h] for h in range(per_key)], 1)
        dz = d_act * (sig[n] + zs[n] * sig[n] * (1.0 - sig[n]))
        dx = conv_back(dz, taps[n], w, metas[n].code, metas[n].plain, dz_ref, doc_next, dw_ref, rim_ref)
        dx_ref[n] = dx.astype(bf16)
        gates_ref[n] = jnp.concatenate([rows[n, m] for m in range(2 * per_key)], 0)

    @pl.when(step == steps - 1)
    def _():
        small_ref[0:4, :DK], small_ref[0:4, DK:] = dwq_ref[...], dw_ref[...]
        small_ref[4:7, :DK], small_ref[4:7, DK:] = rimq_ref[...], rim_ref[...]
        small_ref[7:8, :] = jnp.zeros((1, small_ref.shape[1]), f32)


def places(G, per_key):
    starts = [lambda m: m * DK, lambda m: (G + m) * DK]
    starts += [lambda m, h=h: (2 * G + m * per_key + h) * DK for h in range(per_key)]
    return starts


def tail_kernel(groups, next_ref, gates_ref, *refs):
    refs, out_ref = refs[:-1], refs[-1]
    taps = [ref[0:4, :] for ref in refs]
    while len(taps) > 1:
        taps = [i + j for i, j in zip(taps[::2], taps[1::2])]
    rims = sum(next_ref[q] * refs[q][4:7, :] for q in range(groups))
    parts = range(refs[0].shape[1] // DK)
    shared = [taps[0][:, m * DK : (m + 1) * DK] for m in parts] + [rims[:, m * DK : (m + 1) * DK] for m in parts]
    for m in range(out_ref.shape[0]):
        x = jnp.concatenate([gates_ref[m]] + shared, 0)
        hi = x.astype(bf16)
        mid = (x - hi.astype(f32)).astype(bf16)
        low = (x - hi.astype(f32) - mid.astype(f32)).astype(bf16)
        out_ref[m] = jnp.concatenate([hi, mid, low], 1)


def reads_kernel(G, width, o_ref, out_ref):
    for m in range(G):
        out_ref[:, m * width : (m + 1) * width] = o_ref[m, :, DK:]


def unpack_kernel(G, per_key, o_ref, dx_ref, rows_ref):
    for m in range(G):
        for part, start in enumerate(places(G, per_key)):
            ref, lane = (o_ref, 0) if part == 0 else (dx_ref, (part - 1) * DK)
            rows_ref[:, start(m) : start(m) + DK] = ref[m, :, lane : lane + DK]


def final_kernel(G, per_key, last_ref, tail_ref, rows_in, rows_ref, dw_ref, decay_ref, beta_ref):
    gates, taps = 2 * per_key, 4 * (2 + per_key)
    for m in range(G):
        x = tail_ref[m].astype(f32)
        x = x[:, :DK] + (x[:, DK : 2 * DK] + x[:, 2 * DK : 3 * DK])
        decay_ref[m * per_key : (m + 1) * per_key, :] = x[:per_key]
        beta_ref[m * per_key : (m + 1) * per_key, :] = x[per_key:gates]
        for part, start in enumerate(places(G, per_key)):
            to = slice(start(m), start(m) + DK)
            rim = x[gates + taps + 3 * part : gates + taps + 3 * part + 3] * last_ref[0]
            rim = jnp.concatenate([jnp.zeros((RIM - 3, DK), f32), rim], 0)
            rows_ref[:, to] = (rows_in[:, to].astype(f32) + rim).astype(bf16)
            dw_ref[:, to] = x[gates + 4 * part : gates + 4 * part + 4]


def three(x):
    hi = lax.reduce_precision(x, 8, 7)
    mid = lax.reduce_precision(x - hi, 8, 7)
    return jnp.stack([hi, mid, x - hi - mid], -2).astype(bf16)


def local(mixed, conv_weight, log_decay, beta, doc_ids, out_grad):
    n_seq, n_dp = lax.axis_size("seq"), lax.axis_size("dp")
    rows, docs, og = mixed[0], doc_ids[0], out_grad[0]
    length, channels = rows.shape
    heads = log_decay.shape[1]
    key_heads = (channels - heads * DK) // (2 * DK)
    per_key = heads // key_heads
    G = key_heads
    assert n_seq % G == 0 and G * length >= DOC_MOST
    member = lax.axis_index("seq") % G
    team = [list(range(s, s + G)) for s in range(0, n_seq, G)]
    own = DK + per_key * DK

    def shifted(x, by):
        return lax.ppermute(x, "seq", [(s, s + by) for s in range(n_seq) if 0 <= s + by < n_seq])

    def by_member(x):
        return jnp.moveaxis(x.reshape(x.shape[:-1] + (G, -1)), -2, 0)

    def of_members(x):
        return jnp.moveaxis(x, 0, -2).reshape(x.shape[1:-1] + (-1,))

    def keys_values(x):
        return jnp.concatenate([by_member(x[..., G * DK : 2 * G * DK]), by_member(x[..., 2 * G * DK :])], -1)

    def swap(x):
        return lax.all_to_all(x, "seq", 0, 0, axis_index_groups=team)

    marks = jnp.broadcast_to((docs[-3:] + 1).astype(bf16)[:, None], (3, DK)).reshape(-1)
    marks = jnp.pad(marks, (0, channels - 3 * DK))
    first = jnp.broadcast_to((docs[:1] + 1).astype(bf16), (DK,))
    rim = shifted(jnp.concatenate([rows[-3:], marks[None]], 0), 1)
    held = rim[3, : 3 * DK].reshape(3, DK) == first
    rim_rows = jnp.where(held[:, None], rim[:3].reshape(3, -1, DK), 0).reshape(3, channels)
    code = (docs + 1).reshape(-1, DK) + CODE * (held[0].astype(jnp.int32) + held[1] + held[2])
    code = code.reshape(length).astype(bf16)
    numbers = jnp.concatenate(
        [
            jnp.broadcast_to(code, (G, 1, length)),
            three(log_decay[0].reshape(G, per_key, length)).reshape(G, -1, length),
            three(beta[0].reshape(G, per_key, length)).reshape(G, -1, length),
        ],
        1,
    )
    rim_q = jnp.pad(by_member(rim_rows[:, : G * DK]), ((0, 0), (0, RIM - 6), (0, own - 2 * DK)))
    x = swap(
        jnp.concatenate(
            [keys_values(rows), keys_values(rim_rows), jnp.concatenate([numbers, rim_q], 2)], 1
        )
    )
    y = jnp.concatenate([by_member(rows[:, : G * DK]), by_member(og)], 2)
    taps = conv_weight.astype(f32)
    w_q, w_k, w_v = [
        lax.dynamic_index_in_dim(by_member(part), member, 0, keepdims=False)
        for part in (taps[:, : G * DK], taps[:, G * DK : 2 * G * DK], taps[:, 2 * G * DK :])
    ]
    w_kv = jnp.concatenate([w_k, w_v], 1)
    me = lax.axis_index("seq")
    nexts = jnp.stack([(me ^ q) == me + G for q in range(0, n_seq, G)]).astype(f32)
    last = (member == G - 1).astype(f32)[None]
    y, x, w_q, w_kv, nexts, last = lax.optimization_barrier((y, x, w_q, w_kv, nexts, last))
    y = swap(y)

    pair = (per_key, DK, DK)
    block = (length, DK)

    def call(kernel, count, name, back, fulls, ins, out_shapes, out_fulls, scratch, flops, behind=0):
        steps = G // count
        out_fulls = [s if isinstance(s[0], tuple) else (s, f32) for s in out_fulls]
        order = (lambda s: steps - 1 - s) if back else (lambda s: s)

        def spec(shape):
            return pl.BlockSpec((count,) + shape, lambda s: (order(s),) + (0,) * len(shape))

        def full(shape):
            return pl.BlockSpec(shape, lambda s: (0,) * len(shape))

        in_specs = [full(a.shape) if m in fulls else spec(a.shape[1:]) for m, a in enumerate(ins)]
        return pl.pallas_call(
            functools.partial(kernel, per_key, count),
            grid=(steps,),
            in_specs=in_specs,
            out_specs=[spec(s) for s, _ in out_shapes] + [full(s) for s, _ in out_fulls],
            out_shape=[
                jax.ShapeDtypeStruct((G, s[0] + (0 if m else behind)) + s[1:], t) for m, (s, t) in enumerate(out_shapes)
            ]
            + [jax.ShapeDtypeStruct(s, t) for s, t in out_fulls],
            scratch_shapes=scratch(count),
            compiler_params=pltpu.CompilerParams(vmem_limit_bytes=VMEM),
            cost_estimate=pl.CostEstimate(flops=flops, bytes_accessed=8 << 20, transcendentals=0),
            name=name,
        )(*ins)

    def conv_scratch(width):
        return lambda count: [
            pltpu.VMEM((count, 8 + length, width), f32),
            pltpu.VMEM((16 + length, width), f32),
            pltpu.VMEM((8, DK), f32),
        ]

    def chain_scratch(width):
        return lambda count: [pltpu.VMEM((per_key, DK, 2 * DK), f32), pltpu.VMEM((count, 8 + length, width), f32)]

    k, t, w_out, u, a, m_fwd, s_local, end = call(
        key_kernel, COUNTS[0], "keys", False, (1,), (x, w_kv), [(block, f32)] + [(pair, f32)] * 6, [pair],
        chain_scratch(own), 15 * 10**9,
    )
    state_in = shifted(end, G)
    e, m_bwd, g_local, start = call(
        query_kernel, COUNTS[1], "queries", True, (2,), (x, y, w_q, k, t, a), [(pair, f32)] * 3, [pair],
        chain_scratch(DK), 8 * 10**9,
    )
    back_in = shifted(start, -G)
    o, d, s, dk, dc, rim_q, dw_q = call(
        read_kernel, COUNTS[2], "reads", True, (0, 3), (state_in, x, y, w_q, k, w_out, u, m_fwd, s_local),
        [((length, own), bf16), (pair, f32), (pair, f32), (block, f32), ((per_key, length), f32)],
        [(3, DK), (4, DK)], conv_scratch(DK), 8 * 10**9,
    )
    o = swap(o)
    behind = 2 * per_key + 7 * (2 + per_key)
    assert behind == 2 * RIM
    dx, gates, small = call(
        write_kernel, COUNTS[3], "writes", True, (0, 2, 12, 13),
        (back_in, x, w_kv, k, t, e, m_bwd, g_local, d, s, dk, dc, dw_q, rim_q),
        [((length, own), bf16), ((2 * per_key, length), f32)], [(8, DK + own)],
        lambda count: conv_scratch(own)(count) + [pltpu.VMEM((4, own), f32), pltpu.VMEM((3, own), f32)],
        15 * 10**9,
    )
    terms = []
    for p in range(n_dp):
        for q in range(0, n_seq, G):
            perm = [(i * n_seq + j, (i ^ p) * n_seq + (j ^ q)) for i in range(n_dp) for j in range(n_seq)]
            terms.append(lax.ppermute(small, ("dp", "seq"), perm) if p or q else small)
    tails = pl.pallas_call(
        functools.partial(tail_kernel, n_seq // G),
        in_specs=[pl.BlockSpec(memory_space=pltpu.SMEM)] + [pl.BlockSpec(memory_space=pltpu.VMEM)] * (1 + len(terms)),
        out_shape=jax.ShapeDtypeStruct((G, behind, own), bf16),
        name="tails",
    )(nexts, gates, *terms)
    dx, o = lax.optimization_barrier((dx, o))
    dx = swap(dx)
    output = pl.pallas_call(
        functools.partial(reads_kernel, G, per_key * DK),
        out_shape=jax.ShapeDtypeStruct((length, heads * DK), bf16),
        cost_estimate=pl.CostEstimate(flops=0, bytes_accessed=3 << 20, transcendentals=0),
        name="outputs",
    )(o)
    dx, tails = lax.optimization_barrier((dx, tails))
    tails = swap(tails)
    d_rows = pl.pallas_call(
        functools.partial(unpack_kernel, G, per_key),
        out_shape=jax.ShapeDtypeStruct((length, channels), bf16),
        compiler_params=pltpu.CompilerParams(vmem_limit_bytes=VMEM),
        name="unpack",
    )(o, dx)
    d_rows, tails, output = lax.optimization_barrier((d_rows, tails, output))
    last_rows = pl.BlockSpec((RIM, channels), lambda s: (length // RIM - 1, 0))
    d_rows, d_weight, d_decay, d_beta = pl.pallas_call(
        functools.partial(final_kernel, G, per_key),
        grid=(1,),
        in_specs=[
            pl.BlockSpec(memory_space=pltpu.SMEM),
            pl.BlockSpec(tails.shape, lambda s: (0, 0, 0)),
            last_rows,
        ],
        out_specs=[last_rows]
        + [pl.BlockSpec(shape, lambda s: (0, 0)) for shape in ((4, channels), (heads, length), (heads, length))],
        out_shape=[
            jax.ShapeDtypeStruct((length, channels), bf16),
            jax.ShapeDtypeStruct((4, channels), f32),
            jax.ShapeDtypeStruct((heads, length), f32),
            jax.ShapeDtypeStruct((heads, length), f32),
        ],
        input_output_aliases={2: 0},
        name="totals",
    )(last, tails, d_rows)
    return (output[None], d_rows[None], d_weight, d_decay[None], d_beta[None])


def solution(mesh):
    in_specs = (
        P("dp", "seq", None),
        P(),
        P("dp", None, "seq"),
        P("dp", None, "seq"),
        P("dp", "seq"),
        P("dp", "seq", None),
    )
    out_specs = (
        P("dp", "seq", None),
        P("dp", "seq", None),
        P(),
        P("dp", None, "seq"),
        P("dp", None, "seq"),
    )
    return jax.shard_map(
        local, mesh=mesh, in_specs=in_specs, out_specs=out_specs, check_vma=False
    )
```
